32 devices in a mesh: dev: 32 (over z, y, x, core).
Axes of the slice: x: 2, y: 2, z: 4, core: 2. Of those that a mesh axis runs over, the one named last changes fastest.
Arguments:
- row_ids: int32 [4096, 16, 4], P('dev'), may hold values from 0 to 32767, as said below
- lengths: int32 [4096, 16], P('dev'), may hold values from 1 to 4
- counts: int32 [32], P('dev'), may hold values from 1 to 128, as said below
- mask: int32 [4096], P('dev'), may hold values 0 or 1
- labels: float32 [4096, 5], P('dev'), may hold values from 0 to 1
- row_home: int32 [16, 256], replicated, may hold values from 0 to 255, as said below
- mat_home: int32 [13], replicated, may hold values from 0 to 31, as said below
- table: float32 [524288, 64], P('dev'), may hold values from -3.5 to 3.5
- table_m: float32 [524288, 64], P('dev'), may hold values from -1.66893e-06 to 1.66893e-06
- table_v: float32 [524288], P('dev'), may hold values from 5.9604645e-15 to 2.3841858e-14
- experts_w: float32 [2, 1024, 512], replicated, may hold values from -0.1875 to 0.1875
- gates_w: float32 [5, 1024, 2], replicated, may hold values from -0.1875 to 0.1875
- towers_w: float32 [5, 512, 64], replicated, may hold values from -0.25 to 0.25
- small_params: float32 [1669], replicated, may hold values from -0.875 to 0.875
- experts_m: float32 [32, 2, 1024, 512], P('dev'), may hold values from -6.1035156e-05 to 6.1035156e-05
- experts_v: float32 [32, 2, 1024, 512], P('dev'), may hold values from 8.789062e-12 to 3.515625e-11
- gates_m: float32 [32, 5, 1024, 2], P('dev'), may hold values from -0.00030517578 to 0.00030517578
- gates_v: float32 [32, 5, 1024, 2], P('dev'), may hold values from 2.1972656e-10 to 8.789062e-10
- towers_m: float32 [32, 5, 512, 64], P('dev'), may hold values from -0.00015258789 to 0.00015258789
- towers_v: float32 [32, 5, 512, 64], P('dev'), may hold values from 5.493164e-11 to 2.1972656e-10
- small_m: float32 [32, 1669], P('dev'), may hold values from -0.00030517578 to 0.00030517578
- small_v: float32 [32, 1669], P('dev'), may hold values from 2.1972656e-10 to 8.789062e-10
Outputs:
- loss_sum: float32 [], replicated
- weight_sum: float32 [], replicated
- table_new: float32 [524288, 64], P('dev')
- table_m_new: float32 [524288, 64], P('dev')
- table_v_new: float32 [524288], P('dev')
- experts_new: float32 [2, 1024, 512], replicated
- gates_new: float32 [5, 1024, 2], replicated
- towers_new: float32 [5, 512, 64], replicated
- small_new: float32 [1669], replicated
- experts_m_new: float32 [32, 2, 1024, 512], P('dev')
- experts_v_new: float32 [32, 2, 1024, 512], P('dev')
- gates_m_new: float32 [32, 5, 1024, 2], P('dev')
- gates_v_new: float32 [32, 5, 1024, 2], P('dev')
- towers_m_new: float32 [32, 5, 512, 64], P('dev')
- towers_v_new: float32 [32, 5, 512, 64], P('dev')
- small_m_new: float32 [32, 1669], P('dev')
- small_v_new: float32 [32, 1669], P('dev')
- experts_low: bfloat16 [32, 2, 1024, 512], P('dev')
- gates_low: bfloat16 [32, 5, 1024, 2], P('dev')
- towers_low: bfloat16 [32, 5, 512, 64], P('dev')
- small_low: bfloat16 [32, 1669], P('dev')
The draws below stay inside these ranges and needn't reach their ends.
Inputs may be any that keep to these rules, and one draw needn't show every extreme that they name: `row_ids`: A row number of table t for every slot of bag t, used or not. Of the 8192 ids of one device's sample slots, at most 384 are stored on any one device, and every device reaches 384 for some storing device. `row_home`: each table's row is a permutation: home h means device h // 8. Device i holds its first counts[i] sample slots; the last device holds all 128. `mat_home`: owners may repeat.
All inputs are finite; a program needn't handle non-finite values. No bound on the sum of `mask` on one device may be relied on, other than what follows from the above.
Results may differ from the reference program's by a relative error of at most 0.001.
Values sent between devices are 32-bit elements; how exact they have to be, the bound alone decides.
A program may use at most 192 MiB of HBM per device.

```python
import math
import jax
import jax.numpy as jnp
from jax import lax

S_DEV = 128
NT = 16
EMB = 64
LBAG = 4
BLOCK = 128
ROWS_DEV = 16384
HID = 512
EXPERTS = 2
TASKS = 5
TOWER = 64
STEP = 5
IN = 1024
SAMPLES = 4096
BPT = 8
BLOCKS_T = 256
SMALL = 1669
ITEMS = 13
N_DEV = 32
DEVICES = 32


def home_table(key):
    table_keys = jax.random.split(key, NT)
    return jax.vmap(lambda single: jax.random.permutation(single, BLOCKS_T))(table_keys).astype(jnp.int32)


def draw_row_home(key, part):
    homes = home_table(key)
    return homes


def draw_row_ids(key, part):
    homes = home_table(key)
    key = jax.random.fold_in(key, 2)
    inverse = jnp.argsort(homes, axis=1).astype(jnp.int32)
    slots = S_DEV * NT * LBAG
    average = slots // DEVICES

    def one_device(device_key):
        key_pairs, key_delta, key_shuffle, key_pick, key_offset = jax.random.split(device_key, 5)
        pairs = jax.random.permutation(key_pairs, DEVICES)
        delta = jax.random.randint(key_delta, (DEVICES // 2,), 0, average // 2 + 1)
        delta = delta.at[0].set(average // 2)
        loads = jnp.zeros(DEVICES, jnp.int32)
        loads = loads.at[pairs[0::2]].set(average + delta).at[pairs[1::2]].set(average - delta)
        bounds = jnp.cumsum(loads)
        dest_sorted = jnp.searchsorted(bounds, jnp.arange(slots), side='right').astype(jnp.int32)
        targets = dest_sorted[jax.random.permutation(key_shuffle, slots)]
        table_of = jnp.arange(slots) // LBAG % NT
        picks = jax.random.randint(key_pick, (slots,), 0, BPT)
        block_ids = inverse[table_of, targets * BPT + picks]
        offsets = jax.random.randint(key_offset, (slots,), 0, BLOCK)
        return block_ids * BLOCK + offsets
    identities = jax.vmap(one_device)(jax.random.split(key, DEVICES))
    return identities.reshape(SAMPLES, NT, LBAG).astype(jnp.int32)


def draw_counts(key, part):
    key = jax.random.fold_in(key, 3)
    lowest = S_DEV // 3
    rising = lowest + (S_DEV - lowest) * jnp.arange(DEVICES) // (DEVICES - 1)
    jitter = jax.random.randint(key, (DEVICES,), 0, S_DEV // 8 + 1)
    jitter = jitter.at[DEVICES - 1].set(0)
    return jnp.maximum(rising - jitter, 1).astype(jnp.int32)


def draw_mat_home(key, part):
    key = jax.random.fold_in(key, 5)
    key_owner, key_pick = jax.random.split(key)
    owners = jax.random.randint(key_owner, (ITEMS,), 0, DEVICES)
    picks = jax.random.permutation(key_pick, ITEMS)
    owners = owners.at[picks[0]].set(DEVICES // 2).at[picks[1]].set(0)
    return owners.astype(jnp.int32)


def set_ends(drawn, stream_key, low, largest):
    dims = drawn.shape
    spot = [jax.random.randint(jax.random.fold_in(stream_key, axis), (), 0, dims[axis]) for axis in range(len(dims))]
    drawn = drawn.at[tuple(spot)].set(low)
    longest = dims.index(max(dims))
    spot[longest] = (spot[longest] + 1) % dims[longest]
    return drawn.at[tuple(spot)].set(largest)


def block_scale(stream_key, extent, cuts, low, top_value):
    loudness = 1.0
    for dim, blocks in cuts:
        draws = jax.random.uniform(jax.random.fold_in(jax.random.fold_in(stream_key, 6), dim), (blocks,), jnp.float32, low / len(cuts), top_value / len(cuts))
        loudness = loudness * jnp.repeat(jnp.exp(draws), extent[dim] // blocks).reshape((-1,) + (1,) * (len(extent) - 1 - dim))
    return loudness


def bell_draw(rng, dims, scale, reach, cuts=(), held_as=jnp.bfloat16):
    factor_of = block_scale(rng, dims, cuts, -0.22, 0.18) if cuts else 1.0
    values = jax.random.normal(rng, dims, jnp.float32) * scale * factor_of
    return jnp.minimum(jnp.maximum(values, -reach), reach).astype(held_as)


def setup_inputs(seed: int = 0) -> dict:
    streams_of = jax.random.split(jax.random.key(seed), 23)
    row_ids = draw_row_ids(jax.random.fold_in(streams_of[22], 71), 0)
    lengths = set_ends(jax.random.randint(streams_of[1], (SAMPLES, NT), 1, LBAG + 1), jax.random.fold_in(streams_of[1], 1), 1, LBAG).astype(jnp.int32)
    counts = draw_counts(jax.random.fold_in(streams_of[22], 71), 0)
    mask = set_ends((jax.random.randint(streams_of[3], (SAMPLES,), 0, 4) < 3).astype(jnp.int32), jax.random.fold_in(streams_of[3], 1), 0, 1)
    labels = jnp.clip(1.0 * jax.random.uniform(streams_of[4], (SAMPLES, TASKS), jnp.float32) ** block_scale(streams_of[4], (SAMPLES, TASKS), ((0, 32),), -0.2, 0.2), 0.0, 1.0)
    row_home = draw_row_home(jax.random.fold_in(streams_of[22], 71), 0)
    mat_home = draw_mat_home(jax.random.fold_in(streams_of[22], 71), 0)
    table = bell_draw(streams_of[7], (N_DEV * ROWS_DEV, EMB), 0.6, 3.5, ((0, 32),), jnp.float32)
    table_m = bell_draw(streams_of[8], (N_DEV * ROWS_DEV, EMB), (0.0011 / SAMPLES), 1.6689300537109375e-06, ((0, 32),), jnp.float32)
    table_v = jnp.clip(jnp.exp(math.log(2.3841858188774524e-14) - 1.3862944 * jax.random.uniform(streams_of[9], (N_DEV * ROWS_DEV,), jnp.float32) ** block_scale(streams_of[9], (N_DEV * ROWS_DEV,), ((0, 32),), -0.2, 0.2)), 5.960464547193631e-15, 2.3841858188774524e-14)
    experts_w = bell_draw(streams_of[10], (EXPERTS, IN, HID), IN ** -0.5, 0.1875, (), jnp.float32)
    gates_w = bell_draw(streams_of[11], (TASKS, IN, EXPERTS), IN ** -0.5, 0.1875, (), jnp.float32)
    towers_w = bell_draw(streams_of[12], (TASKS, HID, TOWER), HID ** -0.5, 0.25, (), jnp.float32)
    small_params = bell_draw(streams_of[13], (SMALL,), 0.15, 0.875, (), jnp.float32)
    experts_m = bell_draw(streams_of[14], (N_DEV, EXPERTS, IN, HID), (0.0007 / SAMPLES ** 0.5), 6.103515625e-05, ((0, 32),), jnp.float32)
    experts_v = jnp.clip(jnp.exp(math.log(3.5156249439394216e-11) - 1.3862944 * jax.random.uniform(streams_of[15], (N_DEV, EXPERTS, IN, HID), jnp.float32) ** block_scale(streams_of[15], (N_DEV, EXPERTS, IN, HID), ((0, 32),), -0.2, 0.2)), 8.789062359848554e-12, 3.5156249439394216e-11)
    gates_m = bell_draw(streams_of[16], (N_DEV, TASKS, IN, EXPERTS), (0.0033 / SAMPLES ** 0.5), 0.00030517578, ((0, 32),), jnp.float32)
    gates_v = jnp.clip(jnp.exp(math.log(8.789062255765145e-10) - 1.3862944 * jax.random.uniform(streams_of[17], (N_DEV, TASKS, IN, EXPERTS), jnp.float32) ** block_scale(streams_of[17], (N_DEV, TASKS, IN, EXPERTS), ((0, 32),), -0.2, 0.2)), 2.1972655639412864e-10, 8.789062255765145e-10)
    towers_m = bell_draw(streams_of[18], (N_DEV, TASKS, HID, TOWER), (0.0017 / SAMPLES ** 0.5), 0.00015258789, ((0, 32),), jnp.float32)
    towers_v = jnp.clip(jnp.exp(math.log(2.1972655639412864e-10) - 1.3862944 * jax.random.uniform(streams_of[19], (N_DEV, TASKS, HID, TOWER), jnp.float32) ** block_scale(streams_of[19], (N_DEV, TASKS, HID, TOWER), ((0, 32),), -0.2, 0.2)), 5.493163909853216e-11, 2.1972655639412864e-10)
    small_m = bell_draw(streams_of[20], (N_DEV, SMALL), (0.0033 / SAMPLES ** 0.5), 0.00030517578, ((0, 32),), jnp.float32)
    small_v = jnp.clip(jnp.exp(math.log(8.789062255765145e-10) - 1.3862944 * jax.random.uniform(streams_of[21], (N_DEV, SMALL), jnp.float32) ** block_scale(streams_of[21], (N_DEV, SMALL), ((0, 32),), -0.2, 0.2)), 2.1972655639412864e-10, 8.789062255765145e-10)
    return dict(row_ids=row_ids, lengths=lengths, counts=counts, mask=mask, labels=labels, row_home=row_home, mat_home=mat_home, table=table, table_m=table_m, table_v=table_v, experts_w=experts_w, gates_w=gates_w, towers_w=towers_w, small_params=small_params, experts_m=experts_m, experts_v=experts_v, gates_m=gates_m, gates_v=gates_v, towers_m=towers_m, towers_v=towers_v, small_m=small_m, small_v=small_v)


HIGHEST = lax.Precision.HIGHEST
BETA_ONE = 0.9
BETA_TWO = 0.999
EPSILON = 1e-08
DECAY = 0.01
RATE_DENSE = 0.02
RATE_ROWS = 0.3

def dense_forward(params, pooled, labels, weights):
    experts_w, gates_w, towers_w, small = params
    n_experts, _, hidden = experts_w.shape
    tasks, _, tower = towers_w.shape
    start = n_experts * hidden
    expert_bias = small[:start].reshape(n_experts, hidden)
    tower_bias = small[start:start + tasks * tower].reshape(tasks, tower)
    start = start + tasks * tower
    out_weight = small[start:start + tasks * tower].reshape(tasks, tower)
    task_bias = small[start + tasks * tower:]
    hidden_act = jax.nn.silu(jnp.einsum('si,eih->seh', pooled, experts_w, precision=HIGHEST) + expert_bias)
    gate = jax.nn.softmax(jnp.einsum('si,kie->ske', pooled, gates_w, precision=HIGHEST), axis=-1)
    mixed = jnp.einsum('ske,seh->skh', gate, hidden_act, precision=HIGHEST)
    zed = jax.nn.silu(jnp.einsum('skh,khc->skc', mixed, towers_w, precision=HIGHEST) + tower_bias)
    logit = lax.optimization_barrier(jnp.sum(zed * out_weight, axis=-1)) + task_bias
    losses = jax.nn.softplus(logit) - labels * logit
    return jnp.sum(weights[:, None] * losses)

def adam_step(weight, first, second, grad, rate):
    first_new = BETA_ONE * first + (1.0 - BETA_ONE) * grad
    second_new = BETA_TWO * second + (1.0 - BETA_TWO) * grad * grad
    first_hat = first_new / (1.0 - BETA_ONE ** STEP)
    second_hat = second_new / (1.0 - BETA_TWO ** STEP)
    weight_new = weight - rate * (first_hat / (jnp.sqrt(second_hat) + EPSILON) + DECAY * weight)
    return (weight_new, first_new, second_new)

def copies(value):
    low_value = value.astype(jnp.bfloat16)
    return jnp.broadcast_to(low_value[None], (N_DEV,) + low_value.shape)

def reference(row_ids, lengths, counts, mask, labels, row_home, mat_home, table, table_m, table_v, experts_w, gates_w, towers_w, small_params, experts_m, experts_v, gates_m, gates_v, towers_m, towers_v, small_m, small_v):
    places = jnp.arange(SAMPLES)
    device_of = places // S_DEV
    present = places % S_DEV < counts[device_of]
    weights = jnp.where(present & (mask == 1), 1.0, 0.0).astype(table.dtype)
    live = present[:, None, None] & (jnp.arange(LBAG)[None, None, :] < lengths[:, :, None])
    table_of = jnp.arange(NT)[None, :, None]
    homes = row_home[table_of, row_ids // BLOCK]
    stored = homes // BPT * ROWS_DEV + (table_of * BPT + homes % BPT) * BLOCK + row_ids % BLOCK
    live_float = live.astype(table.dtype)

    def full(rows_table, params):
        rows = rows_table[stored] * live_float[..., None]
        pooled = lax.optimization_barrier(jnp.sum(rows, axis=2)).reshape(SAMPLES, IN)
        return dense_forward(params, pooled, labels, weights)
    params = (experts_w, gates_w, towers_w, small_params)
    loss_sum, pull = jax.vjp(full, table, params)
    weight_sum = jnp.sum(weights)
    grad_table, grads = pull(1.0 / weight_sum)
    grad_experts, grad_gates, grad_towers, grad_small = grads
    table_m_new = BETA_ONE * table_m + (1.0 - BETA_ONE) * grad_table
    table_v_new = BETA_TWO * table_v + (1.0 - BETA_TWO) * lax.optimization_barrier(jnp.mean(grad_table * grad_table, axis=1))
    first_hat = table_m_new / (1.0 - BETA_ONE ** STEP)
    second_hat = table_v_new / (1.0 - BETA_TWO ** STEP)
    table_new = table - RATE_ROWS * (first_hat / (jnp.sqrt(second_hat)[:, None] + EPSILON) + DECAY * table)
    kinds = ((experts_w, experts_m, experts_v, grad_experts), (gates_w, gates_m, gates_v, grad_gates), (towers_w, towers_m, towers_v, grad_towers), (small_params[None], small_m[:, None], small_v[:, None], grad_small[None]))
    results = []
    base = 0
    for stack, firsts, seconds, grad in kinds:
        new_stack = stack
        new_firsts = jnp.zeros_like(firsts)
        new_seconds = jnp.zeros_like(seconds)
        for position in range(stack.shape[0]):
            owner_id = mat_home[base + position]
            weight_new, first_new, second_new = adam_step(stack[position], firsts[owner_id, position], seconds[owner_id, position], grad[position], RATE_DENSE)
            new_stack = new_stack.at[position].set(weight_new)
            new_firsts = new_firsts.at[owner_id, position].set(first_new)
            new_seconds = new_seconds.at[owner_id, position].set(second_new)
        base = base + stack.shape[0]
        results.append((new_stack, new_firsts, new_seconds))
    (experts_new, experts_m_new, experts_v_new), (gates_new, gates_m_new, gates_v_new), (towers_new, towers_m_new, towers_v_new), (small_stack, small_firsts, small_seconds) = results
    small_new = small_stack[0]
    return (loss_sum, weight_sum, table_new, table_m_new, table_v_new, experts_new, gates_new, towers_new, small_new, experts_m_new, experts_v_new, gates_m_new, gates_v_new, towers_m_new, towers_v_new, small_firsts[:, 0], small_seconds[:, 0], copies(experts_new), copies(gates_new), copies(towers_new), copies(small_new))
```

```python
import functools
import jax
import jax.numpy as jnp
from jax import lax
from jax.experimental import pallas as pl
from jax.experimental.pallas import tpu as pltpu
from jax.sharding import PartitionSpec as P

MESH = pl.DeviceIdType.MESH
F32, BF16, I32 = jnp.float32, jnp.bfloat16, jnp.int32
NN, NT, TN = (((1,), (0,)), ((), ())), (((1,), (1,)), ((), ())), (((0,), (0,)), ((), ()))
LANES = 128


def iota(shape, dim):
    return lax.broadcasted_iota(I32, shape, dim)


def dot(a, b, dims=NN):
    return lax.dot_general(a, b, dims, preferred_element_type=F32)


def split3(x):
    high = x.astype(BF16)
    rest = x - high.astype(F32)
    middle = rest.astype(BF16)
    low = (rest - middle.astype(F32)).astype(BF16)
    return high, middle, low


def greet_all(n, me):
    barrier = pltpu.get_barrier_semaphore()

    def signal(k, carry):
        pl.semaphore_signal(barrier, inc=1, device_id=(me ^ k,), device_id_type=MESH)
        return carry

    lax.fori_loop(1, n, signal, 0)
    pl.semaphore_wait(barrier, n - 1)


def exchange(n, me, source, target, sends, receives, k):
    peer = me ^ k
    return pltpu.make_async_remote_copy(
        src_ref=source.at[peer],
        dst_ref=target.at[me],
        send_sem=sends.at[k],
        recv_sem=receives.at[k],
        device_id=(peer,),
        device_id_type=MESH,
    )


def for_range(low, high, body):
    def step(k, carry):
        body(k)
        return carry

    lax.fori_loop(low, high, step, 0)


def route_kernel(
    sizes,
    ids_ref, lengths_ref, counts_ref, mask_ref, labels_ref, homes_ref,
    fields_ref, pos_ref, owner_ref, rank_ref, local_ref, mine_ref, theirs_ref, stat_ref,
    outbox, inbox, message, replies, lists, field_scratch,
    send_a, recv_a, send_b, recv_b, local_sem,
):
    n, cap, tables, bag, tasks, per_table, block_rows, rows_dev = sizes
    rows = tables * bag
    me = lax.axis_index("dev")
    shift = lax.rem(me * 13, n)
    per_pair = LANES // n
    table_of = lax.div(iota((rows, LANES), 0), bag)
    slot_of = lax.rem(iota((rows, LANES), 0), bag)
    expand = jnp.where(lax.div(iota((rows, tables), 0), bag) == iota((rows, tables), 1), 1.0, 0.0).astype(BF16)
    used = dot(expand, lengths_ref[...].astype(F32).astype(BF16)).astype(I32)
    present = iota((1, LANES), 1) < counts_ref[0]
    live = present & (slot_of < used)
    field_scratch[0:rows, :] = jnp.where(live, ids_ref[...], -1).astype(F32)
    field_scratch[rows : rows + tasks, :] = labels_ref[...]
    field_scratch[rows + tasks : rows + tasks + 1, :] = jnp.where(present & (mask_ref[...] == 1), 1.0, 0.0)
    field_scratch[rows + tasks + 1 :, :] = jnp.zeros((LANES - rows - tasks - 1, LANES), F32)
    row = iota((n * 8, LANES), 0)
    peer_of, piece = lax.div(row, 8), lax.rem(row, 8)
    column = iota((n * 8, LANES), 1)
    pick = jnp.where((piece < per_pair) & (column == piece * n + lax.rem(peer_of - shift + n, n)), 1.0, 0.0).astype(BF16)
    high, middle, low = split3(field_scratch[...])
    spread = dot(pick, high, NT) + dot(pick, middle, NT) + dot(pick, low, NT)
    outbox[...] = spread.reshape(n, 8, LANES)
    greet_all(n, me)
    own_copy = pltpu.make_async_copy(outbox.at[me], inbox.at[me], local_sem)
    own_copy.start()
    for_range(1, n, lambda k: exchange(n, me, outbox, inbox, send_a, recv_a, k).start())
    homes = homes_ref[...]
    blocks = homes.shape[1]
    homes_rows = (
        dot(expand, (homes >> 5).astype(F32).astype(BF16)) * 32.0 + dot(expand, (homes & 31).astype(F32).astype(BF16))
    ).astype(I32)
    gather_back = jnp.where((piece < per_pair) & (column == peer_of * per_pair + piece), 1.0, 0.0).astype(BF16)
    before = jnp.where(iota((LANES, LANES), 0) < iota((LANES, LANES), 1), 1.0, 0.0).astype(BF16)
    ones = jnp.ones((LANES, LANES), BF16)
    r_out, r_in = iota((rows + 8, rows), 0), iota((rows + 8, rows), 1)
    parity_in = lax.rem(lax.div(r_in, bag), 2)
    earlier = (r_out < rows) & (r_in < r_out) & (parity_in == lax.rem(lax.div(r_out, bag), 2))
    totals = (r_out == rows + 2 + parity_in)
    above = jnp.where(earlier | totals, 1.0, 0.0).astype(BF16)
    for_range(1, n, lambda k: exchange(n, me, outbox, inbox, send_a, recv_a, k).wait())
    own_copy.wait()
    arrived = inbox[...].reshape(n * 8, LANES).T
    high, middle, low = split3(arrived)
    fields = dot(high, gather_back) + dot(middle, gather_back) + dot(low, gather_back)
    fields_ref[...] = fields[rows : rows + 8]
    ids = fields[0:rows].astype(I32)
    weight_count = jnp.sum(fields[rows + tasks : rows + tasks + 1], axis=1, keepdims=True).astype(I32)
    live = ids >= 0
    ids = jnp.maximum(ids, 0)
    block = lax.div(ids, block_rows)
    lane = block & (LANES - 1)
    home = jnp.zeros((rows, LANES), I32)
    for part in range(blocks // LANES):
        found = jnp.take_along_axis(homes_rows[:, part * LANES : (part + 1) * LANES], lane, axis=1, mode="promise_in_bounds")
        home = jnp.where(lax.div(block, LANES) == part, found, home)
    owner = jnp.where(live, lax.div(home, per_table), n)
    local = (table_of * per_table + lax.rem(home, per_table)) * block_rows + lax.rem(ids, block_rows)
    owner_ref[...] = owner
    local_ref[...] = local

    def rank_step(o, carry):
        rank, most = carry
        is_mine = owner == o
        flags = jnp.where(is_mine, 1.0, 0.0).astype(BF16)
        row_totals = dot(flags, ones).astype(BF16)
        bases = dot(above, row_totals)
        count = bases[rows : rows + 8].astype(I32)
        message[o] = count
        rank = jnp.where(is_mine, (dot(flags, before) + bases[0:rows]).astype(I32), rank)
        return rank, jnp.maximum(most, count)

    rank, most = lax.fori_loop(
        0, n, rank_step, (jnp.zeros((rows, LANES), I32), jnp.zeros((8, LANES), I32)), unroll=4
    )
    rank_ref[...] = rank
    most = jnp.max(most, axis=0, keepdims=True)
    pos_ref[...] = jnp.where(live, jnp.where(rank < cap, owner * cap + rank, n * cap + 1), n * cap)
    lists[...] = jnp.zeros_like(lists)
    device_row = iota((n, LANES), 0)
    rank_row = iota((LANES, LANES), 0)
    lane_value = (iota((n, LANES), 1)).astype(F32)

    def list_step(q, carry):
        for parity in range(2):
            picks, places = [], []
            for j in range(bag):
                r = (2 * q + parity) * bag + j
                owner_row = owner_ref[pl.ds(r, 1), :]
                local_row = local_ref[pl.ds(r, 1), :]
                hit = device_row == owner_row
                picks.append(
                    jnp.concatenate(
                        [
                            jnp.where(hit, ((local_row >> 7) + 1).astype(F32), 0.0),
                            jnp.where(hit, (local_row & 127).astype(F32), 0.0),
                            jnp.where(hit, (q + 1).astype(F32), 0.0),
                            jnp.where(hit, lane_value, 0.0),
                        ],
                        axis=0,
                    ).astype(BF16)
                )
                places.append(jnp.where(rank_row == rank_ref[pl.ds(r, 1), :], 1.0, 0.0).astype(BF16))
            lists[parity] += dot(jnp.concatenate(picks, axis=1), jnp.concatenate(places, axis=1), NT)
        return carry

    lax.fori_loop(0, tables // 2, list_step, 0)
    sub = iota((8, LANES), 0)
    is_last = iota((1, LANES), 1) == LANES - 1

    def post(k):
        o = me ^ k
        tile = message[o]
        rows_out = []
        for parity in range(2):
            count = tile[2 + parity : 3 + parity]
            got = [lists[parity, pl.ds(part * n + o, 1), :].astype(I32) for part in range(4)]
            asked = jnp.where(got[0] > 0, (got[0] - 1) * LANES + got[1], rows_dev)
            slot = jnp.where(got[0] > 0, (got[2] - 1) * LANES + got[3], tables // 2 * LANES)
            rows_out.append(jnp.where(is_last, count, asked))
            mine_ref[o, parity : parity + 1, :] = jnp.where(is_last, count, slot)
        tile = jnp.where(sub == 0, rows_out[0], jnp.where(sub == 1, rows_out[1], tile))
        message[o] = jnp.where(sub == 4, most, jnp.where(sub == 5, weight_count, tile))

    def post_and_send(k):
        post(k)
        exchange(n, me, message, replies, send_b, recv_b, k).start()

    for_range(1, n, post_and_send)
    post(0)
    own_copy = pltpu.make_async_copy(message.at[me], replies.at[me], local_sem)
    own_copy.start()
    for_range(1, n, lambda k: exchange(n, me, message, replies, send_b, recv_b, k).wait())
    own_copy.wait()

    def take(s, carry):
        most, total = carry
        tile = replies[s]
        theirs_ref[s] = tile[0:2]
        return jnp.maximum(most, tile), total + tile

    most, total = lax.fori_loop(0, n, take, (jnp.zeros((8, LANES), I32), jnp.zeros((8, LANES), I32)))
    stat_ref[...] = jnp.where(sub == 4, most, total)


def route(n, cap, row_ids, lengths, counts, mask, labels, row_home, rows_dev):
    samples, tables, bag = row_ids.shape
    tasks = labels.shape[1]
    per_table = row_home.shape[1] // n
    block_rows = rows_dev // (tables * per_table)
    sizes = (n, cap, tables, bag, tasks, per_table, block_rows, rows_dev)
    ids = row_ids.transpose(1, 2, 0).reshape(tables * bag, samples)
    vmem = pl.BlockSpec(memory_space=pltpu.VMEM)
    smem = pl.BlockSpec(memory_space=pltpu.SMEM)
    slots = jax.ShapeDtypeStruct((tables * bag, LANES), I32)
    lists = jax.ShapeDtypeStruct((n, 2, LANES), I32)
    return pl.pallas_call(
        functools.partial(route_kernel, sizes),
        out_shape=(
            jax.ShapeDtypeStruct((8, LANES), F32), slots, slots, slots, slots, lists, lists,
            jax.ShapeDtypeStruct((8, LANES), I32),
        ),
        in_specs=[vmem, vmem, smem, vmem, vmem, vmem],
        out_specs=(vmem,) * 8,
        scratch_shapes=[
            pltpu.VMEM((n, 8, LANES), F32), pltpu.VMEM((n, 8, LANES), F32),
            pltpu.VMEM((n, 8, LANES), I32), pltpu.VMEM((n, 8, LANES), I32),
            pltpu.VMEM((2, 4 * n, LANES), F32), pltpu.VMEM((LANES, LANES), F32),
            pltpu.SemaphoreType.DMA((n,)), pltpu.SemaphoreType.DMA((n,)),
            pltpu.SemaphoreType.DMA((n,)), pltpu.SemaphoreType.DMA((n,)),
            pltpu.SemaphoreType.DMA,
        ],
        compiler_params=pltpu.CompilerParams(collective_id=0, has_side_effects=True, vmem_limit_bytes=32 * 2**20),
        name="route",
    )(ids, lengths.T, counts, mask.reshape(1, samples), labels.T, row_home)

STEP = 5
BETA_ONE = 0.9
BETA_TWO = 0.999
EPSILON = 1e-08
DECAY = 0.01
RATE_DENSE = 0.02
RATE_ROWS = 0.3

def rows_exchange_kernel(n, cap, spare, from_table, lists_ref, source_ref, lines_ref, *scratch):
    if from_table:
        rows_ref, outbox, sends, receives = scratch
    else:
        outbox, sends, receives = scratch
        rows_ref = source_ref
    me = lax.axis_index("dev")
    greet_all(n, me)
    lines_ref[n] = jnp.zeros((cap, LANES), F32)
    if from_table:
        width, rows_dev = source_ref.shape
        rows_ref[rows_dev : rows_dev + spare, :] = jnp.zeros((spare, LANES), F32)

        def turn(b):
            at = pl.ds(pl.multiple_of(b * LANES, LANES), LANES)
            piece = source_ref[:, at]
            rows_ref[at, :] = jnp.concatenate([piece] * (LANES // width), axis=0).T

        for_range(0, rows_dev // LANES, turn)
    left = iota((1, LANES), 1) < LANES // 2

    def collect(peer, target, slot):
        def lines(g, carry):
            for i in range(8):
                r = g * 8 + i
                even = rows_ref[pl.ds(lists_ref[peer, 0, r], 1), :]
                odd = rows_ref[pl.ds(lists_ref[peer, 1, r], 1), :]
                target[slot, pl.ds(r, 1), :] = jnp.where(left, even, odd)
            return carry

        lax.fori_loop(0, cap // 8, lines, 0)

    def collect_and_send(i):
        k = n - i
        collect(me ^ k, outbox, me ^ k)
        exchange(n, me, outbox, lines_ref, sends, receives, k).start()

    for_range(1, n, collect_and_send)
    collect(me, lines_ref, me)
    for_range(1, n, lambda k: exchange(n, me, outbox, lines_ref, sends, receives, k).wait())


def rows_exchange(n, cap, lists, source, from_table, collective_id, name):
    spare = 8
    scratch = [pltpu.VMEM((n, cap, LANES), F32), pltpu.SemaphoreType.DMA((n,)), pltpu.SemaphoreType.DMA((n,))]
    if from_table:
        scratch = [pltpu.VMEM((source.shape[1] + spare, LANES), F32)] + scratch
    return pl.pallas_call(
        functools.partial(rows_exchange_kernel, n, cap, spare, from_table),
        out_shape=jax.ShapeDtypeStruct((n + 1, cap, LANES), F32),
        in_specs=[pl.BlockSpec(memory_space=pltpu.SMEM), pl.BlockSpec(memory_space=pltpu.VMEM)],
        out_specs=pl.BlockSpec(memory_space=pltpu.VMEM),
        scratch_shapes=scratch,
        compiler_params=pltpu.CompilerParams(
            collective_id=collective_id, has_side_effects=True, vmem_limit_bytes=40 * 2**20
        ),
        name=name,
    )(lists, source)


def pool_kernel(nothing, tables, bag, pos_ref, lines_ref, pooled_ref):
    samples = pos_ref.shape[1]
    pooled_ref[...] = jnp.zeros_like(pooled_ref)
    left = iota((1, LANES), 1) < LANES // 2

    def sample(s):
        @pl.when(pos_ref[0, s] != nothing)
        def _():
            for q in range(tables // 2):
                sums = []
                for parity in range(2):
                    base = (2 * q + parity) * bag
                    total = lines_ref[pl.ds(pos_ref[base, s], 1), :]
                    for j in range(1, bag):
                        total = total + lines_ref[pl.ds(pos_ref[base + j, s], 1), :]
                    sums.append(total)
                pooled_ref[pl.ds(q * samples + s, 1), :] = jnp.where(left, sums[0], sums[1])

    for_range(0, samples, sample)


def pool(n, cap, tables, bag, pos, lines):
    samples = pos.shape[1]
    return pl.pallas_call(
        functools.partial(pool_kernel, n * cap, tables, bag),
        out_shape=jax.ShapeDtypeStruct((tables // 2 * samples, LANES), F32),
        in_specs=[pl.BlockSpec(memory_space=pltpu.SMEM), pl.BlockSpec(memory_space=pltpu.VMEM)],
        out_specs=pl.BlockSpec(memory_space=pltpu.VMEM),
        compiler_params=pltpu.CompilerParams(vmem_limit_bytes=24 * 2**20),
        name="pool",
    )(pos, lines.reshape((n + 1) * cap, LANES))


def split2(x):
    high = x.astype(BF16)
    return high, (x - high.astype(F32)).astype(BF16)


def dot3(a, b, dims=NN):
    return dot(a[0], b[0], dims) + dot(a[0], b[1], dims) + dot(a[1], b[0], dims)


def sigmoid(x):
    return 1.0 / (1.0 + jnp.exp(-x))


def dense_kernel(
    sizes, stat_ref, fields_ref, pooled_ref, experts_ref, gates_ref, towers_ref, small_ref,
    grad_a_ref, grad_b_ref, rows_ref, side,
):
    experts, hidden, tasks, tower, half_tail = sizes
    samples = fields_ref.shape[1]
    features = pooled_ref.shape[0] // samples * LANES
    halves = (grad_a_ref, grad_b_ref)
    for ref in halves:
        ref[features:, :] = jnp.zeros((half_tail, hidden), F32)

    def put_tail(row, value):
        count = value.shape[0]
        for low, high, ref in ((0, half_tail, grad_a_ref), (half_tail, 2 * half_tail, grad_b_ref)):
            first, last = max(low, row), min(high, row + count)
            if first < last:
                ref[features + first - low : features + last - low, :] = value[first - row : last - row]

    start = experts * hidden
    tower_at = start
    weight_at = start + tasks * tower
    bias_at = weight_at + tasks * tower
    side[0:8, :] = fields_ref[...]
    side[8:, :] = jnp.zeros((samples - 8, samples), F32)
    by_sample = side[...].T
    weight = by_sample[:, tasks : tasks + 1]
    scale = weight / stat_ref[0].astype(F32)
    x = jnp.concatenate([pooled_ref[q * samples : (q + 1) * samples] for q in range(features // LANES)], axis=1)
    x2 = split2(x)
    gate_w = gates_ref[...]
    gate_w2 = split2(gate_w)
    gate_logits = dot3(x2, gate_w2, NT)
    pres, sigs, hids = [], [], []
    for e in range(experts):
        pre = dot3(x2, split2(experts_ref[e])) + small_ref[0:1, e * hidden : (e + 1) * hidden]
        sig = sigmoid(pre)
        pres.append(pre)
        sigs.append(sig)
        hids.append(pre * sig)
    dhids = [jnp.zeros((samples, hidden), F32) for _ in range(experts)]
    dgate_logits = []
    loss = jnp.zeros((samples, 1), F32)
    small_rows = []
    tower_bias_grads, out_weight_grads, task_bias_grads = [], [], []
    for k in range(tasks):
        logits = [gate_logits[:, k * experts + e : k * experts + e + 1] for e in range(experts)]
        top = functools.reduce(jnp.maximum, logits)
        powers = [jnp.exp(v - top) for v in logits]
        whole = functools.reduce(jnp.add, powers)
        gates = [v / whole for v in powers]
        mix = functools.reduce(jnp.add, [gates[e] * hids[e] for e in range(experts)])
        mix2 = split2(mix)
        tower2 = split2(towers_ref[k])
        at = tower_at + k * tower
        pre = dot3(mix2, tower2, NT) + small_ref[0:1, at : at + tower]
        sig = sigmoid(pre)
        zed = pre * sig
        at = weight_at + k * tower
        out_weight = small_ref[0:1, at : at + tower]
        logit = jnp.sum(zed * out_weight, axis=1, keepdims=True) + small_ref[0:1, bias_at + k : bias_at + k + 1]
        label = by_sample[:, k : k + 1]
        softplus = jnp.maximum(logit, 0.0) + jnp.log1p(jnp.exp(-jnp.abs(logit)))
        loss = loss + weight * (softplus - label * logit)
        dlogit = scale * (sigmoid(logit) - label)
        task_bias_grads.append(jnp.sum(dlogit, axis=0, keepdims=True))
        out_weight_grads.append(jnp.sum(dlogit * zed, axis=0, keepdims=True))
        dpre = dlogit * out_weight * (sig * (1.0 + pre * (1.0 - sig)))
        tower_bias_grads.append(jnp.sum(dpre, axis=0, keepdims=True))
        dpre2 = split2(dpre)
        put_tail(k * tower, dot3(split2(dpre.T), mix2))
        dmix = dot3(dpre2, tower2)
        dgates = [jnp.sum(dmix * hids[e], axis=1, keepdims=True) for e in range(experts)]
        mean = functools.reduce(jnp.add, [gates[e] * dgates[e] for e in range(experts)])
        for e in range(experts):
            dgate_logits.append(gates[e] * (dgates[e] - mean))
            dhids[e] = dhids[e] + gates[e] * dmix
    lane = iota((samples, LANES), 1)
    dgl = jnp.zeros((samples, LANES), F32)
    for i, v in enumerate(dgate_logits):
        dgl = jnp.where(lane == i, v, dgl)
    count = tasks * experts
    dgl_t2 = split2(dgl.T[0:16])
    dgates_w = dot3(dgl_t2, x2)
    tail_at = tasks * tower
    put_tail(tail_at, dgates_w[:, :hidden])
    put_tail(tail_at + 16, dgates_w[:, hidden:])
    x_t2 = split2(x.T)
    dx = dot3(split2(dgl[:, :count]), gate_w2)
    expert_bias_grads = []
    for e in range(experts):
        dpre = dhids[e] * (sigs[e] * (1.0 + pres[e] * (1.0 - sigs[e])))
        expert_bias_grads.append(jnp.sum(dpre, axis=0, keepdims=True))
        dpre2 = split2(dpre)
        halves[e][0:features, :] = dot3(x_t2, dpre2)
        dx = dx + dot3(dpre2, split2(experts_ref[e]), NT)
    for q in range(features // LANES):
        rows_ref[q * samples : (q + 1) * samples, :] = dx[:, q * LANES : (q + 1) * LANES]
    rows_ref[features // LANES * samples :, :] = jnp.zeros((8, LANES), F32)
    small_at = tail_at + 32
    pad = jnp.zeros((1, 2 * hidden - 2 * tasks * tower - tasks), F32)
    line = jnp.concatenate(tower_bias_grads + out_weight_grads + task_bias_grads + [pad], axis=1)
    loss_row = jnp.where(iota((1, hidden), 1) == 0, jnp.sum(loss, axis=0, keepdims=True), 0.0)
    for e in range(experts):
        put_tail(small_at + e, expert_bias_grads[e])
    for i in range(line.shape[1] // hidden):
        put_tail(small_at + experts + i, line[:, i * hidden : (i + 1) * hidden])
    put_tail(small_at + 8, loss_row)


def dense(half_tail, stat, fields, pooled, experts_w, gates_w, towers_w, small):
    experts, features, hidden = experts_w.shape
    tasks, _, tower = towers_w.shape
    samples = fields.shape[1]
    vmem = pl.BlockSpec(memory_space=pltpu.VMEM)
    grads = jax.ShapeDtypeStruct((features + half_tail, hidden), F32)
    return pl.pallas_call(
        functools.partial(dense_kernel, (experts, hidden, tasks, tower, half_tail)),
        out_shape=(grads, grads, jax.ShapeDtypeStruct((features // LANES * samples + 8, LANES), F32)),
        in_specs=[pl.BlockSpec(memory_space=pltpu.SMEM)] + [vmem] * 6,
        out_specs=(vmem,) * 3,
        scratch_shapes=[pltpu.VMEM((samples, samples), F32)],
        compiler_params=pltpu.CompilerParams(vmem_limit_bytes=56 * 2**20),
        name="dense",
    )(
        stat, fields, pooled, experts_w,
        gates_w.transpose(0, 2, 1).reshape(tasks * experts, features),
        towers_w.transpose(0, 2, 1), small.reshape(1, -1),
    )


def update_kernel(
    sizes, lists_ref, more_ref, lines_ref, table_ref, first_ref, second_ref, extra_ref,
    table_new_ref, first_new_ref, second_new_ref, sums_even, sums_odd, extra_block, extra_sem,
):
    n, cap, per_table = sizes
    step = pl.program_id(0)
    width, block = table_ref.shape
    table_rows = block // 2
    rows_dev = sums_even.shape[0] - 8
    sums = (sums_even, sums_odd)

    @pl.when(step == 0)
    def _():
        def clear(i):
            for parity in range(2):
                at = pl.multiple_of((2 * i + parity) * table_rows, table_rows)
                sums[parity][pl.ds(at, table_rows), :] = jnp.zeros((table_rows, LANES), F32)

        for_range(0, rows_dev // block, clear)

        def source(s):
            count = jnp.minimum(jnp.maximum(lists_ref[s, 0, LANES - 1], lists_ref[s, 1, LANES - 1]), cap)

            def add(g):
                for i in range(4):
                    r = g * 4 + i
                    line = lines_ref[pl.ds(s * cap + r, 1), :]
                    even, odd = lists_ref[s, 0, r], lists_ref[s, 1, r]
                    sums_even[pl.ds(even, 1), :] += line
                    sums_odd[pl.ds(odd, 1), :] += line

            for_range(0, (count + 3) // 4, add)

        for_range(0, n, source)

    @pl.when(more_ref[0] > cap)
    def _():
        copy = pltpu.make_async_copy(
            extra_ref.at[:, pl.ds(pl.multiple_of(step * block, block), block)], extra_block, extra_sem
        )
        copy.start()
        copy.wait()

    for parity in range(2):
        for b in range(table_rows // LANES):
            at = parity * table_rows + b * LANES
            here = slice(at, at + LANES)
            rows = sums[parity][pl.ds(pl.multiple_of(step * block + at, LANES), LANES), :].T
            grad = rows[parity * width : (parity + 1) * width]
            grad = jnp.where(more_ref[0] > cap, grad + extra_block[:, here], grad)
            first = BETA_ONE * first_ref[:, here] + (1.0 - BETA_ONE) * grad
            mean = jnp.sum(grad * grad, axis=0, keepdims=True) * (1.0 / width)
            second = BETA_TWO * second_ref[:, here] + (1.0 - BETA_TWO) * mean
            rate = (RATE_ROWS / (1.0 - BETA_ONE**STEP)) / (
                jnp.sqrt(second * (1.0 / (1.0 - BETA_TWO**STEP))) + EPSILON
            )
            old = table_ref[:, here]
            table_new_ref[:, here] = old - (first * rate + (RATE_ROWS * DECAY) * old)
            first_new_ref[:, here] = first
            second_new_ref[:, here] = second


def update(n, cap, per_table, tables, lists, most, lines, table, table_m, table_v, extra):
    rows_dev, width = table.shape
    block = 2 * per_table * LANES
    wide = pl.BlockSpec((width, block), lambda i, *_: (0, i))
    thin = pl.BlockSpec((1, block), lambda i, *_: (0, i))
    smem = pl.BlockSpec(memory_space=pltpu.SMEM)
    table_new, first_new, second_new = pl.pallas_call(
        functools.partial(update_kernel, (n, cap, per_table)),
        grid=(rows_dev // block,),
        out_shape=(
            jax.ShapeDtypeStruct((width, rows_dev), F32), jax.ShapeDtypeStruct((width, rows_dev), F32),
            jax.ShapeDtypeStruct((1, rows_dev), F32),
        ),
        in_specs=[
            smem, smem, pl.BlockSpec(((n + 1) * cap, LANES), lambda i: (0, 0)),
            wide, wide, thin, pl.BlockSpec(memory_space=pl.ANY),
        ],
        out_specs=(wide, wide, thin),
        scratch_shapes=[
            pltpu.VMEM((rows_dev + 8, LANES), F32), pltpu.VMEM((rows_dev + 8, LANES), F32),
            pltpu.VMEM((width, block), F32), pltpu.SemaphoreType.DMA,
        ],
        compiler_params=pltpu.CompilerParams(vmem_limit_bytes=48 * 2**20),
        name="update_rows",
    )(lists, most, lines.reshape((n + 1) * cap, LANES), table.T, table_m.T, table_v.reshape(1, rows_dev), extra)
    return table_new.T, first_new.T, second_new.reshape(rows_dev)

def orders(n):
    bits = [1 << i for i in range(n.bit_length() - 1)]
    first, rest = bits[0], bits[1:]
    return ([first] + rest, [first] + [rest[1], rest[0]] + rest[2:])


def swap(x, n, bit):
    return lax.ppermute(x, "dev", [(i, i ^ bit) for i in range(n)])


def halve(x, me, n, bit):
    half = x.shape[-2] // 2
    mine = (me // bit) % 2
    keep = lax.dynamic_slice_in_dim(x, mine * half, half, x.ndim - 2)
    send = lax.dynamic_slice_in_dim(x, (1 - mine) * half, half, x.ndim - 2)
    return keep + swap(send, n, bit)


def double(x, me, n, bit):
    other = swap(x, n, bit)
    mine = (me // bit) % 2
    axis = x.ndim - 2
    return jnp.where(mine == 0, jnp.concatenate([x, other], axis), jnp.concatenate([other, x], axis))


def scatter_sum(x, me, n, order):
    for bit in order:
        x = halve(x, me, n, bit)
    return x


def gather_all(x, me, n, order):
    for bit in order[::-1]:
        x = double(x, me, n, bit)
    return x


def slice_of(x, me, order):
    rows = x.shape[-2]
    start = 0
    for bit in order:
        rows = rows // 2
        start = start + ((me // bit) % 2) * rows
    return lax.dynamic_slice_in_dim(x, start, rows, x.ndim - 2)


GAP = 16


def pack(experts, gates, towers, small, half_tail):
    hidden = experts.shape[2]
    tasks, features, count = gates.shape
    gates = gates.transpose(0, 2, 1).reshape(tasks * count, features)
    lines = jnp.pad(small, (0, 4 * hidden - small.shape[0])).reshape(4, hidden)
    tail = jnp.concatenate(
        [
            towers.transpose(0, 2, 1).reshape(-1, hidden),
            jnp.pad(gates[:, :hidden], ((0, GAP - tasks * count), (0, 0))),
            jnp.pad(gates[:, hidden:], ((0, GAP - tasks * count), (0, 0))),
            lines,
        ]
    )
    tail = jnp.pad(tail, ((0, 2 * half_tail - tail.shape[0]), (0, 0)))
    return (
        jnp.concatenate([experts[0], tail[:half_tail]]),
        jnp.concatenate([experts[1], tail[half_tail:]]),
    )


def unpack(a, b, shapes):
    experts_shape, gates_shape, towers_shape, small_size = shapes
    features = experts_shape[1]
    hidden = experts_shape[2]
    tasks, _, count = gates_shape
    experts = jnp.stack([a[:features], b[:features]])
    tail = jnp.concatenate([a[features:], b[features:]])
    tower_rows = tasks * towers_shape[2]
    towers = tail[:tower_rows].reshape(tasks, towers_shape[2], hidden).transpose(0, 2, 1)
    gates = jnp.concatenate(
        [tail[tower_rows : tower_rows + tasks * count], tail[tower_rows + GAP : tower_rows + GAP + tasks * count]], axis=1
    )
    gates = gates.reshape(tasks, count, features).transpose(0, 2, 1)
    at = tower_rows + 2 * GAP
    small = tail[at : at + 4].reshape(-1)[:small_size]
    return experts, gates, towers, small, tail[at + 8, 0]


def moments(first, second, grad):
    return (
        BETA_ONE * first + (1.0 - BETA_ONE) * grad,
        BETA_TWO * second + (1.0 - BETA_TWO) * grad * grad,
    )


def stepped(weight, first_new, second_new):
    first_hat = first_new / (1.0 - BETA_ONE**STEP)
    second_hat = second_new / (1.0 - BETA_TWO**STEP)
    return weight - RATE_DENSE * (first_hat / (jnp.sqrt(second_hat) + EPSILON) + DECAY * weight)


def late_requests(n, cap, k, owner, rank, local):
    rows, samples = owner.shape
    inside = (owner < n) & (rank >= k * cap) & (rank < (k + 1) * cap)
    parity = jnp.broadcast_to((jnp.arange(rows) // 4 % 2)[:, None], owner.shape)
    target = jnp.where(inside, owner, n)
    place = jnp.where(inside, rank - k * cap, 0)
    asked = jnp.zeros((n, 2, cap), I32).at[target, parity, place].set(local, mode="drop")
    asked = lax.all_to_all(asked.reshape(n, 2 * cap), "dev", 0, 0, tiled=True)
    return inside, parity, target, place, asked


def late_pool(n, cap, most, owner, rank, local, table, pooled):
    width = table.shape[1]
    rows, samples = owner.shape

    def body(k, pooled):
        inside, parity, target, place, asked = late_requests(n, cap, k, owner, rank, local)
        found = table[asked].reshape(n, 2 * cap * width)
        got = lax.all_to_all(found, "dev", 0, 0, tiled=True).reshape(n, 2, cap, width)
        slot_rows = jnp.where(inside[..., None], got[jnp.minimum(target, n - 1), parity, place], 0.0)
        bags = jnp.sum(slot_rows.reshape(rows // 4, 4, samples, width), axis=1)
        bags = bags.reshape(rows // 8, 2, samples, width).transpose(0, 2, 1, 3)
        return pooled + bags.reshape(rows // 8 * samples, 2 * width)

    return lax.fori_loop(1, (most + cap - 1) // cap, body, pooled)


def late_grads(n, cap, most, owner, rank, local, rows_grad, rows_dev, width):
    rows, samples = owner.shape
    tables = rows // 4

    def body(k, extra):
        inside, parity, target, place, asked = late_requests(n, cap, k, owner, rank, local)
        lines = rows_grad[: tables // 2 * samples].reshape(tables // 2, samples, 2, width)
        bags = lines.transpose(0, 2, 1, 3).reshape(tables, 1, samples, width)
        slot_grads = jnp.broadcast_to(bags, (tables, 4, samples, width)).reshape(rows, samples, width)
        out = jnp.zeros((n, 2, cap, width), F32).at[target, parity, place].set(slot_grads, mode="drop")
        valid = jnp.zeros((n, 2, cap), F32).at[target, parity, place].set(1.0, mode="drop")
        got = lax.all_to_all(out.reshape(n, -1), "dev", 0, 0, tiled=True).reshape(-1, width)
        valid = lax.all_to_all(valid.reshape(n, -1), "dev", 0, 0, tiled=True).reshape(-1, 1)
        return extra + jnp.zeros((rows_dev, width), F32).at[asked.reshape(-1)].add(got * valid).T

    return lax.fori_loop(1, (most + cap - 1) // cap, body, jnp.zeros((width, rows_dev), F32))


def per_device(
    row_ids, lengths, counts, mask, labels, row_home, mat_home, table, table_m, table_v,
    experts_w, gates_w, towers_w, small_params,
    experts_m, experts_v, gates_m, gates_v, towers_m, towers_v, small_m, small_v,
):
    n = lax.axis_size("dev")
    me = lax.axis_index("dev")
    samples, tables, bag = row_ids.shape
    rows_dev, width = table.shape
    per_table = row_home.shape[1] // n
    cap = max(8, (samples * tables * bag // n * 5 // 16 + 7) // 8 * 8)
    experts, features, hidden = experts_w.shape
    tasks = towers_w.shape[0]
    half_tail = 256
    order_a, order_b = orders(n)

    owned = mat_home == me
    own_experts = owned[:experts, None, None]
    own_gates = owned[experts : experts + tasks, None, None]
    own_towers = owned[experts + tasks : experts + 2 * tasks, None, None]
    own_small = owned[experts + 2 * tasks]
    firsts = (experts_m[0], gates_m[0], towers_m[0], small_m[0])
    seconds = (experts_v[0], gates_v[0], towers_v[0], small_v[0])
    owns = (own_experts, own_gates, own_towers, own_small)

    def kept(items):
        return tuple(jnp.where(own, item, 0.0) for own, item in zip(owns, items))

    first_a, first_b = pack(*kept(firsts), half_tail)
    second_a, second_b = pack(*kept(seconds), half_tail)
    moments_a = scatter_sum(jnp.stack([first_a, second_a]), me, n, order_a)
    moments_b = scatter_sum(jnp.stack([first_b, second_b]), me, n, order_b)

    fields, pos, owner, rank, local, mine, theirs, stat = route(
        n, cap, row_ids, lengths, counts, mask, labels, row_home, rows_dev
    )
    most, weight_count = stat[4, 0], stat[5, 0]
    lines = rows_exchange(n, cap, theirs, table.T, True, 1, "fetch_rows")
    pooled = pool(n, cap, tables, bag, pos, lines)
    pooled = late_pool(n, cap, most, owner, rank, local, table, pooled)
    grad_a, grad_b, rows_grad = dense(
        half_tail, weight_count[None], fields, pooled, experts_w, gates_w, towers_w, small_params
    )
    back = rows_exchange(n, cap, mine, rows_grad, False, 2, "return_grads")
    extra = late_grads(n, cap, most, owner, rank, local, rows_grad, rows_dev, width)
    table_new, table_m_new, table_v_new = update(
        n, cap, per_table, tables, theirs, most[None], back, table, table_m, table_v, extra
    )

    weights = pack(experts_w, gates_w, towers_w, small_params, half_tail)
    both = []
    for grad, moment, weight, order in (
        (grad_a, moments_a, weights[0], order_a), (grad_b, moments_b, weights[1], order_b)
    ):
        grad = scatter_sum(grad, me, n, order)
        first, second = moments(moment[0], moment[1], grad)
        new = stepped(slice_of(weight, me, order), first, second)
        both.append(gather_all(jnp.stack([new, grad]), me, n, order))
    shapes = (experts_w.shape, gates_w.shape, towers_w.shape, small_params.shape[0])
    experts_new, gates_new, towers_new, small_new, _ = unpack(both[0][0], both[1][0], shapes)
    *grads, loss_sum = unpack(both[0][1], both[1][1], shapes)
    outs_m, outs_v = [], []
    for own, first, second, grad in zip(owns, firsts, seconds, grads):
        first, second = moments(first, second, grad)
        outs_m.append(jnp.where(own, first, 0.0)[None])
        outs_v.append(jnp.where(own, second, 0.0)[None])
    return (
        loss_sum, weight_count.astype(F32), table_new, table_m_new, table_v_new,
        experts_new, gates_new, towers_new, small_new,
        outs_m[0], outs_v[0], outs_m[1], outs_v[1], outs_m[2], outs_v[2], outs_m[3], outs_v[3],
        experts_new.astype(BF16)[None], gates_new.astype(BF16)[None],
        towers_new.astype(BF16)[None], small_new.astype(BF16)[None],
    )


def solution(mesh):
    def split(dims):
        return P("dev", *(None,) * (dims - 1))

    by_device = split(4)
    return jax.shard_map(
        per_device,
        mesh=mesh,
        in_specs=(
            split(3), split(2), split(1), split(1), split(2), P(), P(), split(2), split(2), split(1),
            P(), P(), P(), P(),
        ) + (by_device,) * 6 + (split(2),) * 2,
        out_specs=(P(), P(), split(2), split(2), split(1), P(), P(), P(), P())
        + (by_device,) * 6 + (split(2),) * 2 + (by_device,) * 3 + (split(2),),
        check_vma=False,
    )
```

```python
import functools
import jax
import jax.numpy as jnp
from jax import lax
from jax.experimental import pallas as pl
from jax.experimental.pallas import tpu as pltpu
from jax.sharding import PartitionSpec as P

MESH = pl.DeviceIdType.MESH
F32, BF16, I32 = jnp.float32, jnp.bfloat16, jnp.int32
NN, NT, TN = (((1,), (0,)), ((), ())), (((1,), (1,)), ((), ())), (((0,), (0,)), ((), ()))
LANES = 128


def iota(shape, dim):
    return lax.broadcasted_iota(I32, shape, dim)


def dot(a, b, dims=NN):
    return lax.dot_general(a, b, dims, preferred_element_type=F32)


def split3(x):
    high = x.astype(BF16)
    rest = x - high.astype(F32)
    middle = rest.astype(BF16)
    low = (rest - middle.astype(F32)).astype(BF16)
    return high, middle, low


def greet_all(n, me):
    barrier = pltpu.get_barrier_semaphore()

    def signal(k, carry):
        pl.semaphore_signal(barrier, inc=1, device_id=(me ^ k,), device_id_type=MESH)
        return carry

    lax.fori_loop(1, n, signal, 0)
    pl.semaphore_wait(barrier, n - 1)


def exchange(n, me, source, target, sends, receives, k):
    peer = me ^ k
    return pltpu.make_async_remote_copy(
        src_ref=source.at[peer],
        dst_ref=target.at[me],
        send_sem=sends.at[k],
        recv_sem=receives.at[k],
        device_id=(peer,),
        device_id_type=MESH,
    )


def for_range(low, high, body):
    def step(k, carry):
        body(k)
        return carry

    lax.fori_loop(low, high, step, 0)

STEP = 5
BETA_ONE = 0.9
BETA_TWO = 0.999
EPSILON = 1e-08
DECAY = 0.01
RATE_DENSE = 0.02
RATE_ROWS = 0.3

def axis_orders(n):
    bits = [1 << i for i in range(n.bit_length() - 1)]
    core, rest = bits[:1], bits[1:]
    a = len(rest) // 3
    b = (len(rest) - a) // 2
    x, y, z = rest[:a], rest[a : a + b], rest[a + b :]
    return core + x + y + z, core + y + x + z, core + z + x + y, core + z + y + x


def bit_of(me, bit):
    return lax.rem(lax.div(me, bit), 2)


def start_of(me, order, rows):
    start = 0
    for bit in order:
        rows = rows // 2
        start = start + bit_of(me, bit) * rows
    return start


def rows_at(start, count):
    return pl.ds(pl.multiple_of(start, 8), count)


def halving(me, source, stages, sends, receives, chain, order, i):
    bit = order[i]
    before = source if i == 0 else stages[i - 1]
    half = stages[i].shape[-2]
    peer = me ^ bit
    at = rows_at((1 - bit_of(me, bit)) * half, half)
    return pltpu.make_async_remote_copy(
        src_ref=before.at[at] if len(before.shape) == 2 else before.at[:, at],
        dst_ref=stages[i],
        send_sem=sends.at[chain, i],
        recv_sem=receives.at[chain, i],
        device_id=(peer,),
        device_id_type=MESH,
    )


def forward_kernel(
    sizes,
    ids_ref, lengths_ref, counts_ref, mask_ref, labels_ref, homes_ref, table_ref,
    items_ref, experts_m_ref, experts_v_ref, tail_m_ref, tail_v_ref,
    fields_ref, pos_ref, owner_ref, rank_ref, local_ref, mine_ref, theirs_ref, stat_ref, lines_ref,
    moments_a_ref, moments_b_ref, moments_c_ref, moments_d_ref,
    outbox, inbox, message, replies, lists, field_scratch, asked_smem, rows_ref, rows_out,
    kept_a, kept_b, *rest,
):
    n, cap, tables, bag, tasks, experts, gap, per_table, block_rows, rows_dev = sizes
    levels = n.bit_length() - 1
    stages = [list(rest[c * (levels - 1) : (c + 1) * (levels - 1)]) for c in range(4)]
    for stage, final in zip(stages, (moments_a_ref, moments_b_ref, moments_c_ref, moments_d_ref)):
        stage.append(final)
    send_a, recv_a, send_b, recv_b, send_c, recv_c, send_m, recv_m, sems = rest[4 * (levels - 1) :]
    rows = tables * bag
    me = lax.axis_index("dev")
    shift = lax.rem(me * 13, n)
    per_pair = LANES // n
    orders = axis_orders(n)
    table_of = lax.div(iota((rows, LANES), 0), bag)
    slot_of = lax.rem(iota((rows, LANES), 0), bag)
    expand = jnp.where(lax.div(iota((rows, tables), 0), bag) == iota((rows, tables), 1), 1.0, 0.0).astype(BF16)
    used = dot(expand, lengths_ref[...].astype(F32).astype(BF16)).astype(I32)
    present = iota((1, LANES), 1) < counts_ref[0]
    live = present & (slot_of < used)
    field_scratch[0:rows, :] = jnp.where(live, ids_ref[...], -1).astype(F32)
    field_scratch[rows : rows + tasks, :] = labels_ref[...]
    field_scratch[rows + tasks : rows + tasks + 1, :] = jnp.where(present & (mask_ref[...] == 1), 1.0, 0.0)
    field_scratch[rows + tasks + 1 :, :] = jnp.zeros((LANES - rows - tasks - 1, LANES), F32)
    row = iota((n * 8, LANES), 0)
    peer_of, piece = lax.div(row, 8), lax.rem(row, 8)
    column = iota((n * 8, LANES), 1)
    pick = jnp.where((piece < per_pair) & (column == piece * n + lax.rem(peer_of - shift + n, n)), 1.0, 0.0).astype(BF16)
    high, middle, low = split3(field_scratch[...])
    spread = dot(pick, high, NT) + dot(pick, middle, NT) + dot(pick, low, NT)
    outbox[...] = spread.reshape(n, 8, LANES)
    greet_all(n, me)
    own_copy = pltpu.make_async_copy(outbox.at[me], inbox.at[me], sems.at[0])
    own_copy.start()
    for_range(1, n, lambda k: exchange(n, me, outbox, inbox, send_a, recv_a, k).start())
    sources = ((experts_m_ref, experts_v_ref), (tail_m_ref, tail_v_ref))
    parity = bit_of(me, 1)

    def first_hops():
        hops = []
        for c in range(4):
            half = stages[c][0].shape[1]
            for w in range(2):
                whole = sources[c // 2][w].at[c % 2]
                hops.append(
                    pltpu.make_async_remote_copy(
                        src_ref=whole.at[rows_at((1 - parity) * half, half)],
                        dst_ref=stages[c][0].at[w],
                        send_sem=send_m.at[c, levels + w],
                        recv_sem=recv_m.at[c, levels + w],
                        device_id=(me ^ 1,),
                        device_id_type=MESH,
                    )
                )
        return hops

    keeps = []
    for c, kept in ((0, kept_a), (1, kept_b)):
        half = kept.shape[1]
        for w in range(2):
            keeps.append(
                pltpu.make_async_copy(
                    sources[0][w].at[c, rows_at(parity * half, half)], kept.at[w], sems.at[1 + 2 * c + w]
                )
            )
    for copy in first_hops() + keeps:
        copy.start()

    def chosen(c, i, start, count):
        bit = orders[c][i]
        if c < 2:
            return bit_of(items_ref[c], bit) == bit_of(me, bit)
        towers = tasks * 64
        row = (c - 2) * tail_m_ref.shape[1] + start + iota((count, LANES), 0)
        item = lax.div(row, 64) + experts + tasks
        for part in range(2):
            inside = (row >= towers + part * gap) & (row < towers + part * gap + tasks * experts)
            item = jnp.where(inside, experts + lax.div(row - towers - part * gap, experts), item)
        item = jnp.where(row >= towers + 2 * gap, experts + 2 * tasks, item)
        home = jnp.zeros((count, LANES), I32)
        for k in range(experts, experts + 2 * tasks + 1):
            home = jnp.where(item == k, items_ref[k], home)
        return (bit_of(home, bit) == bit_of(me, bit))[:, :1]

    def settle(i):
        if i == 0:
            for copy in first_hops() + keeps:
                copy.wait()
        for c in range(4):
            order, stage = orders[c], stages[c]
            if i > 0:
                halving(me, None, stage, send_m, recv_m, c, order, i).wait()
            half = stage[i].shape[1]
            mine = rows_at(bit_of(me, order[i]) * half, half)
            total = 2 * stage[0].shape[1]
            flag = chosen(c, i, start_of(me, order[: i + 1], total), half)
            for w in range(2):
                if i > 0:
                    kept = stage[i - 1][w, mine, :]
                elif c < 2:
                    kept = (kept_a, kept_b)[c][w]
                else:
                    kept = sources[1][w][c - 2, mine, :]
                stage[i][w] = jnp.where(flag, kept, stage[i][w])
            if i + 1 < levels:
                halving(me, None, stage, send_m, recv_m, c, order, i + 1).start()

    homes = homes_ref[...]
    blocks = homes.shape[1]
    homes_rows = (
        dot(expand, (homes >> 5).astype(F32).astype(BF16)) * 32.0 + dot(expand, (homes & 31).astype(F32).astype(BF16))
    ).astype(I32)
    gather_back = jnp.where((piece < per_pair) & (column == peer_of * per_pair + piece), 1.0, 0.0).astype(BF16)
    before = jnp.where(iota((LANES, LANES), 0) < iota((LANES, LANES), 1), 1.0, 0.0).astype(BF16)
    ones = jnp.ones((LANES, LANES), BF16)
    r_out, r_in = iota((rows + 8, rows), 0), iota((rows + 8, rows), 1)
    parity_in = lax.rem(lax.div(r_in, bag), 2)
    earlier = (r_out < rows) & (r_in < r_out) & (parity_in == lax.rem(lax.div(r_out, bag), 2))
    totals = (r_out == rows + 2 + parity_in)
    above = jnp.where(earlier | totals, 1.0, 0.0).astype(BF16)
    for_range(1, n, lambda k: exchange(n, me, outbox, inbox, send_a, recv_a, k).wait())
    own_copy.wait()
    arrived = inbox[...].reshape(n * 8, LANES).T
    high, middle, low = split3(arrived)
    fields = dot(high, gather_back) + dot(middle, gather_back) + dot(low, gather_back)
    fields_ref[...] = fields[rows : rows + 8]
    ids = fields[0:rows].astype(I32)
    weight_count = jnp.sum(fields[rows + tasks : rows + tasks + 1], axis=1, keepdims=True).astype(I32)
    live = ids >= 0
    ids = jnp.maximum(ids, 0)
    block = lax.div(ids, block_rows)
    lane = block & (LANES - 1)
    home = jnp.zeros((rows, LANES), I32)
    for part in range(blocks // LANES):
        found = jnp.take_along_axis(homes_rows[:, part * LANES : (part + 1) * LANES], lane, axis=1, mode="promise_in_bounds")
        home = jnp.where(lax.div(block, LANES) == part, found, home)
    owner = jnp.where(live, lax.div(home, per_table), n)
    local = (table_of * per_table + lax.rem(home, per_table)) * block_rows + lax.rem(ids, block_rows)
    owner_ref[...] = owner
    local_ref[...] = local

    def rank_step(o, carry):
        rank, most = carry
        is_mine = owner == o
        flags = jnp.where(is_mine, 1.0, 0.0).astype(BF16)
        row_totals = dot(flags, ones).astype(BF16)
        bases = dot(above, row_totals)
        count = bases[rows : rows + 8].astype(I32)
        message[o] = count
        rank = jnp.where(is_mine, (dot(flags, before) + bases[0:rows]).astype(I32), rank)
        return rank, jnp.maximum(most, count)

    rank, most = lax.fori_loop(
        0, n, rank_step, (jnp.zeros((rows, LANES), I32), jnp.zeros((8, LANES), I32)), unroll=4
    )
    rank_ref[...] = rank
    most = jnp.max(most, axis=0, keepdims=True)
    pos_ref[...] = jnp.where(live, jnp.where(rank < cap, owner * cap + rank, n * cap + 1), n * cap)
    lists[...] = jnp.zeros_like(lists)
    device_row = iota((n, LANES), 0)
    rank_row = iota((LANES, LANES), 0)
    lane_value = (iota((n, LANES), 1)).astype(F32)

    def list_step(q, carry):
        for parity in range(2):
            picks, places = [], []
            for j in range(bag):
                r = (2 * q + parity) * bag + j
                owner_row = owner_ref[pl.ds(r, 1), :]
                local_row = local_ref[pl.ds(r, 1), :]
                hit = device_row == owner_row
                picks.append(
                    jnp.concatenate(
                        [
                            jnp.where(hit, ((local_row >> 7) + 1).astype(F32), 0.0),
                            jnp.where(hit, (local_row & 127).astype(F32), 0.0),
                            jnp.where(hit, (q + 1).astype(F32), 0.0),
                            jnp.where(hit, lane_value, 0.0),
                        ],
                        axis=0,
                    ).astype(BF16)
                )
                places.append(jnp.where(rank_row == rank_ref[pl.ds(r, 1), :], 1.0, 0.0).astype(BF16))
            lists[parity] += dot(jnp.concatenate(picks, axis=1), jnp.concatenate(places, axis=1), NT)
        return carry

    lax.fori_loop(0, tables // 2, list_step, 0)
    sub = iota((8, LANES), 0)
    is_last = iota((1, LANES), 1) == LANES - 1

    def post(k):
        o = me ^ k
        tile = message[o]
        rows_list = []
        for parity in range(2):
            count = tile[2 + parity : 3 + parity]
            got = [lists[parity, pl.ds(part * n + o, 1), :].astype(I32) for part in range(4)]
            asked = jnp.where(got[0] > 0, (got[0] - 1) * LANES + got[1], rows_dev)
            slot = jnp.where(got[0] > 0, (got[2] - 1) * LANES + got[3], tables // 2 * LANES)
            rows_list.append(jnp.where(is_last, count, asked))
            mine_ref[o, parity : parity + 1, :] = jnp.where(is_last, count, slot)
        tile = jnp.where(sub == 0, rows_list[0], jnp.where(sub == 1, rows_list[1], tile))
        message[o] = jnp.where(sub == 4, most, jnp.where(sub == 5, weight_count, tile))

    def post_and_send(k):
        post(k)
        exchange(n, me, message, replies, send_b, recv_b, k).start()

    for_range(1, n, post_and_send)
    post(0)
    own_copy = pltpu.make_async_copy(message.at[me], replies.at[me], sems.at[0])
    own_copy.start()
    settle(0)
    width = table_ref.shape[0]
    rows_ref[rows_dev:, :] = jnp.zeros((rows_ref.shape[0] - rows_dev, LANES), F32)

    def turn(b):
        at = pl.ds(pl.multiple_of(b * LANES, LANES), LANES)
        rows_ref[at, :] = jnp.concatenate([table_ref[:, at]] * (LANES // width), axis=0).T

    for_range(0, rows_dev // LANES, turn)
    for_range(1, n, lambda k: exchange(n, me, message, replies, send_b, recv_b, k).wait())
    own_copy.wait()

    def take(s, carry):
        most, total = carry
        tile = replies[s]
        theirs_ref[s] = jnp.clip(tile[0:2], 0, rows_dev)
        return jnp.maximum(most, tile), total + tile

    most, total = lax.fori_loop(0, n, take, (jnp.zeros((8, LANES), I32), jnp.zeros((8, LANES), I32)))
    stat_ref[...] = jnp.where(sub == 4, most, total)
    to_scalars = pltpu.make_async_copy(theirs_ref, asked_smem, sems.at[0])
    to_scalars.start()
    to_scalars.wait()
    lines_ref[n] = jnp.zeros((cap, LANES), F32)
    collect = collector(cap, asked_smem, rows_ref)

    def collect_and_send(i):
        k = n - i
        collect(me ^ k, rows_out, me ^ k)
        exchange(n, me, rows_out, lines_ref, send_c, recv_c, k).start()

    for_range(1, n // 2 + 1, collect_and_send)
    settle(1)
    for_range(n // 2 + 1, n, collect_and_send)
    collect(me, lines_ref, me)
    for i in range(2, levels):
        settle(i)
    for_range(1, n, lambda k: exchange(n, me, rows_out, lines_ref, send_c, recv_c, k).wait())


def collector(cap, lists_ref, rows_ref):
    left = iota((1, LANES), 1) < LANES // 2

    def collect(peer, target, slot):
        def lines(g):
            for i in range(8):
                r = g * 8 + i
                even = rows_ref[pl.ds(lists_ref[peer, 0, r], 1), :]
                odd = rows_ref[pl.ds(lists_ref[peer, 1, r], 1), :]
                target[slot, pl.ds(r, 1), :] = jnp.where(left, even, odd)

        for_range(0, cap // 8, lines)

    return collect


def chain_rows(features, half_tail):
    return features, features, half_tail, half_tail


def forward(n, cap, row_ids, lengths, counts, mask, labels, row_home, table, mat_home, experts_m, experts_v, tail_m, tail_v):
    samples, tables, bag = row_ids.shape
    rows_dev, width = table.shape
    tasks = labels.shape[1]
    experts, features, hidden = experts_m.shape
    half_tail = tail_m.shape[1]
    per_table = row_home.shape[1] // n
    block_rows = rows_dev // (tables * per_table)
    levels = n.bit_length() - 1
    sizes = (n, cap, tables, bag, tasks, experts, GAP, per_table, block_rows, rows_dev)
    ids = row_ids.transpose(1, 2, 0).reshape(tables * bag, samples)
    vmem = pl.BlockSpec(memory_space=pltpu.VMEM)
    smem = pl.BlockSpec(memory_space=pltpu.SMEM)
    hbm = pl.BlockSpec(memory_space=pl.ANY)
    slots = jax.ShapeDtypeStruct((tables * bag, LANES), I32)
    lists = jax.ShapeDtypeStruct((n, 2, LANES), I32)
    chains = chain_rows(features, half_tail)
    small = pltpu.VMEM((n, 8, LANES), F32)
    numbers = pltpu.VMEM((n, 8, LANES), I32)
    dma = pltpu.SemaphoreType.DMA((n,))
    hops = pltpu.SemaphoreType.DMA((4, levels + 2))
    return pl.pallas_call(
        functools.partial(forward_kernel, sizes),
        out_shape=(
            jax.ShapeDtypeStruct((8, LANES), F32), slots, slots, slots, slots, lists, lists,
            jax.ShapeDtypeStruct((8, LANES), I32), jax.ShapeDtypeStruct((n + 1, cap, LANES), F32),
        ) + tuple(jax.ShapeDtypeStruct((2, count // n, hidden), F32) for count in chains),
        in_specs=[vmem, vmem, smem, vmem, vmem, vmem, vmem, smem, hbm, hbm, vmem, vmem],
        out_specs=(vmem,) * 13,
        scratch_shapes=[
            small, small, numbers, numbers,
            pltpu.VMEM((2, 4 * n, LANES), F32), pltpu.VMEM((LANES, LANES), F32),
            pltpu.SMEM((n, 2, LANES), I32), pltpu.VMEM((rows_dev + 8, LANES), F32), pltpu.VMEM((n, cap, LANES), F32),
            pltpu.VMEM((2, features // 2, hidden), F32), pltpu.VMEM((2, features // 2, hidden), F32),
        ]
        + [pltpu.VMEM((2, count >> (i + 1), hidden), F32) for count in chains for i in range(levels - 1)]
        + [dma] * 6 + [hops] * 2 + [pltpu.SemaphoreType.DMA((8,))],
        compiler_params=pltpu.CompilerParams(collective_id=0, has_side_effects=True, vmem_limit_bytes=56 * 2**20),
        name="forward",
    )(
        ids, lengths.T, counts, mask.reshape(1, samples), labels.T, row_home, table.T,
        mat_home, experts_m, experts_v, tail_m, tail_v,
    )


def backward_kernel(n, cap, lists_ref, rows_ref, grad_a_ref, grad_b_ref, grad_tail_ref, lines_ref, *rest):
    levels = n.bit_length() - 1
    finals, rest = rest[:4], rest[4:]
    stages = [list(rest[c * (levels - 1) : (c + 1) * (levels - 1)]) + [finals[c]] for c in range(4)]
    rows_out, send_c, recv_c, sends, receives = rest[4 * (levels - 1) :]
    me = lax.axis_index("dev")
    orders = axis_orders(n)
    sources = (grad_a_ref, grad_b_ref, grad_tail_ref.at[0], grad_tail_ref.at[1])
    greet_all(n, me)

    def begin(i):
        for c in range(4):
            halving(me, sources[c], stages[c], sends, receives, c, orders[c], i).start()

    def settle(i):
        for c in range(4):
            halving(me, sources[c], stages[c], sends, receives, c, orders[c], i).wait()
            before = sources[c] if i == 0 else stages[c][i - 1]
            half = stages[c][i].shape[0]
            stages[c][i][...] += before[rows_at(bit_of(me, orders[c][i]) * half, half), :]
            if i + 1 < levels:
                halving(me, sources[c], stages[c], sends, receives, c, orders[c], i + 1).start()

    begin(0)
    lines_ref[n] = jnp.zeros((cap, LANES), F32)
    collect = collector(cap, lists_ref, rows_ref)

    def collect_and_send(i):
        k = n - i
        collect(me ^ k, rows_out, me ^ k)
        exchange(n, me, rows_out, lines_ref, send_c, recv_c, k).start()

    for_range(1, n // 4 + 1, collect_and_send)
    settle(0)
    for_range(n // 4 + 1, n // 2 + 1, collect_and_send)
    for_range(n // 2 + 1, n, collect_and_send)
    collect(me, lines_ref, me)
    for i in range(1, levels):
        settle(i)
    for_range(1, n, lambda k: exchange(n, me, rows_out, lines_ref, send_c, recv_c, k).wait())


def backward(n, cap, lists, rows, grad_a, grad_b, grad_tail):
    levels = n.bit_length() - 1
    features, hidden = grad_a.shape
    chains = chain_rows(features, grad_tail.shape[1])
    vmem = pl.BlockSpec(memory_space=pltpu.VMEM)
    return pl.pallas_call(
        functools.partial(backward_kernel, n, cap),
        out_shape=(jax.ShapeDtypeStruct((n + 1, cap, LANES), F32),)
        + tuple(jax.ShapeDtypeStruct((count // n, hidden), F32) for count in chains),
        in_specs=[pl.BlockSpec(memory_space=pltpu.SMEM)] + [vmem] * 4,
        out_specs=(vmem,) * 5,
        scratch_shapes=[pltpu.VMEM((count >> (i + 1), hidden), F32) for count in chains for i in range(levels - 1)]
        + [pltpu.VMEM((n, cap, LANES), F32)]
        + [pltpu.SemaphoreType.DMA((n,))] * 2 + [pltpu.SemaphoreType.DMA((4, levels))] * 2,
        compiler_params=pltpu.CompilerParams(collective_id=1, has_side_effects=True, vmem_limit_bytes=40 * 2**20),
        name="backward",
    )(lists, rows, grad_a, grad_b, grad_tail)


def spread_kernel(n, *refs):
    grads, moments_in, weights = refs[0:4], refs[4:8], refs[8:12]
    wholes = refs[12:16]
    news = refs[16:20]
    sends, receives, local = refs[20:]
    levels = n.bit_length() - 1
    me = lax.axis_index("dev")
    orders = axis_orders(n)
    copies = []
    starts = []
    for c in range(4):
        count = grads[c].shape[0]
        total = wholes[c].shape[1]
        start = start_of(me, orders[c], total)
        first, second = moments(moments_in[c][0], moments_in[c][1], grads[c][...])
        news[c][0] = stepped(weights[c][...], first, second)
        news[c][1] = grads[c][...]
        copies.append(pltpu.make_async_copy(news[c], wholes[c].at[:, rows_at(start, count)], local.at[c]))
    for copy in copies:
        copy.start()
    greet_bits(n, me)
    for copy in copies:
        copy.wait()

    def doubling(c, i):
        order = orders[c]
        total = wholes[c].shape[1]
        size = total >> (i + 1)
        at = rows_at(start_of(me, order[: i + 1], total), size)
        return pltpu.make_async_remote_copy(
            src_ref=wholes[c].at[:, at],
            dst_ref=wholes[c].at[:, at],
            send_sem=sends.at[c, i],
            recv_sem=receives.at[c, i],
            device_id=(me ^ order[i],),
            device_id_type=MESH,
        )

    for i in reversed(range(levels)):
        for c in range(4):
            if i + 1 < levels:
                doubling(c, i + 1).wait()
            doubling(c, i).start()
    for c in range(4):
        doubling(c, 0).wait()


def greet_bits(n, me):
    barrier = pltpu.get_barrier_semaphore()
    levels = n.bit_length() - 1
    for i in range(levels):
        pl.semaphore_signal(barrier, inc=1, device_id=(me ^ (1 << i),), device_id_type=MESH)
    pl.semaphore_wait(barrier, levels)


def spread(n, grads, moments_in, weights):
    levels = n.bit_length() - 1
    hidden = grads[0].shape[1]
    vmem = pl.BlockSpec(memory_space=pltpu.VMEM)
    return pl.pallas_call(
        functools.partial(spread_kernel, n),
        out_shape=tuple(jax.ShapeDtypeStruct((2, g.shape[0] * n, hidden), F32) for g in grads),
        in_specs=[vmem] * 12,
        out_specs=(vmem,) * 4,
        scratch_shapes=[pltpu.VMEM((2,) + g.shape, F32) for g in grads]
        + [pltpu.SemaphoreType.DMA((4, levels))] * 2 + [pltpu.SemaphoreType.DMA((4,))],
        compiler_params=pltpu.CompilerParams(collective_id=2, has_side_effects=True, vmem_limit_bytes=40 * 2**20),
        name="spread",
    )(*grads, *moments_in, *weights)

def pool_kernel(nothing, tables, bag, pos_ref, lines_ref, pooled_ref):
    samples = pos_ref.shape[1]
    pooled_ref[...] = jnp.zeros_like(pooled_ref)
    left = iota((1, LANES), 1) < LANES // 2

    def sample(s):
        @pl.when(pos_ref[0, s] != nothing)
        def _():
            for q in range(tables // 2):
                sums = []
                for parity in range(2):
                    base = (2 * q + parity) * bag
                    total = lines_ref[pl.ds(pos_ref[base, s], 1), :]
                    for j in range(1, bag):
                        total = total + lines_ref[pl.ds(pos_ref[base + j, s], 1), :]
                    sums.append(total)
                pooled_ref[pl.ds(q * samples + s, 1), :] = jnp.where(left, sums[0], sums[1])

    for_range(0, samples, sample)


def pool(n, cap, tables, bag, pos, lines):
    samples = pos.shape[1]
    return pl.pallas_call(
        functools.partial(pool_kernel, n * cap, tables, bag),
        out_shape=jax.ShapeDtypeStruct((tables // 2 * samples, LANES), F32),
        in_specs=[pl.BlockSpec(memory_space=pltpu.SMEM), pl.BlockSpec(memory_space=pltpu.VMEM)],
        out_specs=pl.BlockSpec(memory_space=pltpu.VMEM),
        compiler_params=pltpu.CompilerParams(vmem_limit_bytes=24 * 2**20),
        name="pool",
    )(pos, lines.reshape((n + 1) * cap, LANES))


def split2(x):
    high = x.astype(BF16)
    return high, (x - high.astype(F32)).astype(BF16)


def dot3(a, b, dims=NN):
    return dot(a[0], b[0], dims) + dot(a[0], b[1], dims) + dot(a[1], b[0], dims)


def sigmoid(x):
    return 1.0 / (1.0 + jnp.exp(-x))


def dense_kernel(
    sizes, stat_ref, fields_ref, pooled_ref, experts_ref, gates_ref, towers_ref, small_ref,
    grad_a_ref, grad_b_ref, tail_ref, rows_ref, side,
):
    experts, hidden, tasks, tower, half_tail = sizes
    samples = fields_ref.shape[1]
    features = pooled_ref.shape[0] // samples * LANES
    halves = (grad_a_ref, grad_b_ref)
    tail_ref[...] = jnp.zeros_like(tail_ref)

    def put_tail(row, value):
        count = value.shape[0]
        for part in range(2):
            first, last = max(part * half_tail, row), min((part + 1) * half_tail, row + count)
            if first < last:
                at = slice(first - part * half_tail, last - part * half_tail)
                tail_ref[part, at, :] = value[first - row : last - row]

    start = experts * hidden
    tower_at = start
    weight_at = start + tasks * tower
    bias_at = weight_at + tasks * tower
    side[0:8, :] = fields_ref[...]
    side[8:, :] = jnp.zeros((samples - 8, samples), F32)
    by_sample = side[...].T
    weight = by_sample[:, tasks : tasks + 1]
    scale = weight / stat_ref[0].astype(F32)
    x = jnp.concatenate([pooled_ref[q * samples : (q + 1) * samples] for q in range(features // LANES)], axis=1)
    x2 = split2(x)
    gate_w = gates_ref[...]
    gate_w2 = split2(gate_w)
    gate_logits = dot3(x2, gate_w2, NT)
    pres, sigs, hids = [], [], []
    for e in range(experts):
        pre = dot3(x2, split2(experts_ref[e])) + small_ref[0:1, e * hidden : (e + 1) * hidden]
        sig = sigmoid(pre)
        pres.append(pre)
        sigs.append(sig)
        hids.append(pre * sig)
    dhids = [jnp.zeros((samples, hidden), F32) for _ in range(experts)]
    dgate_logits = []
    loss = jnp.zeros((samples, 1), F32)
    small_rows = []
    tower_bias_grads, out_weight_grads, task_bias_grads = [], [], []
    for k in range(tasks):
        logits = [gate_logits[:, k * experts + e : k * experts + e + 1] for e in range(experts)]
        top = functools.reduce(jnp.maximum, logits)
        powers = [jnp.exp(v - top) for v in logits]
        whole = functools.reduce(jnp.add, powers)
        gates = [v / whole for v in powers]
        mix = functools.reduce(jnp.add, [gates[e] * hids[e] for e in range(experts)])
        mix2 = split2(mix)
        tower2 = split2(towers_ref[k])
        at = tower_at + k * tower
        pre = dot3(mix2, tower2, NT) + small_ref[0:1, at : at + tower]
        sig = sigmoid(pre)
        zed = pre * sig
        at = weight_at + k * tower
        out_weight = small_ref[0:1, at : at + tower]
        logit = jnp.sum(zed * out_weight, axis=1, keepdims=True) + small_ref[0:1, bias_at + k : bias_at + k + 1]
        label = by_sample[:, k : k + 1]
        softplus = jnp.maximum(logit, 0.0) + jnp.log1p(jnp.exp(-jnp.abs(logit)))
        loss = loss + weight * (softplus - label * logit)
        dlogit = scale * (sigmoid(logit) - label)
        task_bias_grads.append(jnp.sum(dlogit, axis=0, keepdims=True))
        out_weight_grads.append(jnp.sum(dlogit * zed, axis=0, keepdims=True))
        dpre = dlogit * out_weight * (sig * (1.0 + pre * (1.0 - sig)))
        tower_bias_grads.append(jnp.sum(dpre, axis=0, keepdims=True))
        dpre2 = split2(dpre)
        put_tail(k * tower, dot3(split2(dpre.T), mix2))
        dmix = dot3(dpre2, tower2)
        dgates = [jnp.sum(dmix * hids[e], axis=1, keepdims=True) for e in range(experts)]
        mean = functools.reduce(jnp.add, [gates[e] * dgates[e] for e in range(experts)])
        for e in range(experts):
            dgate_logits.append(gates[e] * (dgates[e] - mean))
            dhids[e] = dhids[e] + gates[e] * dmix
    lane = iota((samples, LANES), 1)
    dgl = jnp.zeros((samples, LANES), F32)
    for i, v in enumerate(dgate_logits):
        dgl = jnp.where(lane == i, v, dgl)
    count = tasks * experts
    dgl_t2 = split2(dgl.T[0:16])
    dgates_w = dot3(dgl_t2, x2)
    tail_at = tasks * tower
    put_tail(tail_at, dgates_w[:, :hidden])
    put_tail(tail_at + GAP, dgates_w[:, hidden:])
    x_t2 = split2(x.T)
    dx = dot3(split2(dgl[:, :count]), gate_w2)
    expert_bias_grads = []
    for e in range(experts):
        dpre = dhids[e] * (sigs[e] * (1.0 + pres[e] * (1.0 - sigs[e])))
        expert_bias_grads.append(jnp.sum(dpre, axis=0, keepdims=True))
        dpre2 = split2(dpre)
        halves[e][...] = dot3(x_t2, dpre2)
        dx = dx + dot3(dpre2, split2(experts_ref[e]), NT)
    for q in range(features // LANES):
        rows_ref[q * samples : (q + 1) * samples, :] = dx[:, q * LANES : (q + 1) * LANES]
    rows_ref[features // LANES * samples :, :] = jnp.zeros((8, LANES), F32)
    small_at = tail_at + 2 * GAP
    pad = jnp.zeros((1, 2 * hidden - 2 * tasks * tower - tasks), F32)
    line = jnp.concatenate(tower_bias_grads + out_weight_grads + task_bias_grads + [pad], axis=1)
    loss_row = jnp.where(iota((1, hidden), 1) == 0, jnp.sum(loss, axis=0, keepdims=True), 0.0)
    for e in range(experts):
        put_tail(small_at + e, expert_bias_grads[e])
    for i in range(line.shape[1] // hidden):
        put_tail(small_at + experts + i, line[:, i * hidden : (i + 1) * hidden])
    put_tail(small_at + 8, loss_row)


def dense(half_tail, stat, fields, pooled, experts_w, gates_w, towers_w, small):
    experts, features, hidden = experts_w.shape
    tasks, _, tower = towers_w.shape
    samples = fields.shape[1]
    vmem = pl.BlockSpec(memory_space=pltpu.VMEM)
    grads = jax.ShapeDtypeStruct((features, hidden), F32)
    tail = jax.ShapeDtypeStruct((2, half_tail, hidden), F32)
    return pl.pallas_call(
        functools.partial(dense_kernel, (experts, hidden, tasks, tower, half_tail)),
        out_shape=(grads, grads, tail, jax.ShapeDtypeStruct((features // LANES * samples + 8, LANES), F32)),
        in_specs=[pl.BlockSpec(memory_space=pltpu.SMEM)] + [vmem] * 6,
        out_specs=(vmem,) * 4,
        scratch_shapes=[pltpu.VMEM((samples, samples), F32)],
        compiler_params=pltpu.CompilerParams(vmem_limit_bytes=56 * 2**20),
        name="dense",
    )(
        stat, fields, pooled, experts_w,
        gates_w.transpose(0, 2, 1).reshape(tasks * experts, features),
        towers_w.transpose(0, 2, 1), small.reshape(1, -1),
    )


def update_kernel(
    sizes, lists_ref, more_ref, lines_ref, table_ref, first_ref, second_ref, extra_ref,
    table_new_ref, first_new_ref, second_new_ref, sums_even, sums_odd, extra_block, extra_sem,
):
    n, cap, per_table = sizes
    step = pl.program_id(0)
    width, block = table_ref.shape
    table_rows = block // 2
    rows_dev = sums_even.shape[0] - 8
    sums = (sums_even, sums_odd)

    @pl.when(step == 0)
    def _():
        def clear(i):
            for parity in range(2):
                at = pl.multiple_of((2 * i + parity) * table_rows, table_rows)
                sums[parity][pl.ds(at, table_rows), :] = jnp.zeros((table_rows, LANES), F32)

        for_range(0, rows_dev // block, clear)

        def source(s):
            count = jnp.minimum(jnp.maximum(lists_ref[s, 0, LANES - 1], lists_ref[s, 1, LANES - 1]), cap)

            def add(g):
                for i in range(4):
                    r = g * 4 + i
                    line = lines_ref[pl.ds(s * cap + r, 1), :]
                    even, odd = lists_ref[s, 0, r], lists_ref[s, 1, r]
                    sums_even[pl.ds(even, 1), :] += line
                    sums_odd[pl.ds(odd, 1), :] += line

            for_range(0, (count + 3) // 4, add)

        for_range(0, n, source)

    @pl.when(more_ref[0] > cap)
    def _():
        copy = pltpu.make_async_copy(
            extra_ref.at[:, pl.ds(pl.multiple_of(step * block, block), block)], extra_block, extra_sem
        )
        copy.start()
        copy.wait()

    for parity in range(2):
        for b in range(table_rows // LANES):
            at = parity * table_rows + b * LANES
            here = slice(at, at + LANES)
            rows = sums[parity][pl.ds(pl.multiple_of(step * block + at, LANES), LANES), :].T
            grad = rows[parity * width : (parity + 1) * width]
            grad = jnp.where(more_ref[0] > cap, grad + extra_block[:, here], grad)
            first = BETA_ONE * first_ref[:, here] + (1.0 - BETA_ONE) * grad
            mean = jnp.sum(grad * grad, axis=0, keepdims=True) * (1.0 / width)
            second = BETA_TWO * second_ref[:, here] + (1.0 - BETA_TWO) * mean
            rate = (RATE_ROWS / (1.0 - BETA_ONE**STEP)) / (
                jnp.sqrt(second * (1.0 / (1.0 - BETA_TWO**STEP))) + EPSILON
            )
            old = table_ref[:, here]
            table_new_ref[:, here] = old - (first * rate + (RATE_ROWS * DECAY) * old)
            first_new_ref[:, here] = first
            second_new_ref[:, here] = second


def update(n, cap, per_table, tables, lists, most, lines, table, table_m, table_v, extra):
    rows_dev, width = table.shape
    block = 2 * per_table * LANES
    wide = pl.BlockSpec((width, block), lambda i, *_: (0, i))
    thin = pl.BlockSpec((1, block), lambda i, *_: (0, i))
    smem = pl.BlockSpec(memory_space=pltpu.SMEM)
    table_new, first_new, second_new = pl.pallas_call(
        functools.partial(update_kernel, (n, cap, per_table)),
        grid=(rows_dev // block,),
        out_shape=(
            jax.ShapeDtypeStruct((width, rows_dev), F32), jax.ShapeDtypeStruct((width, rows_dev), F32),
            jax.ShapeDtypeStruct((1, rows_dev), F32),
        ),
        in_specs=[
            smem, smem, pl.BlockSpec(((n + 1) * cap, LANES), lambda i: (0, 0)),
            wide, wide, thin, pl.BlockSpec(memory_space=pl.ANY),
        ],
        out_specs=(wide, wide, thin),
        scratch_shapes=[
            pltpu.VMEM((rows_dev + 8, LANES), F32), pltpu.VMEM((rows_dev + 8, LANES), F32),
            pltpu.VMEM((width, block), F32), pltpu.SemaphoreType.DMA,
        ],
        compiler_params=pltpu.CompilerParams(vmem_limit_bytes=48 * 2**20),
        name="update_rows",
    )(lists, most, lines.reshape((n + 1) * cap, LANES), table.T, table_m.T, table_v.reshape(1, rows_dev), extra)
    return table_new.T, first_new.T, second_new.reshape(rows_dev)

GAP = 16


def pack_tail(gates, towers, small, half_tail):
    tasks, features, count = gates.shape
    hidden = towers.shape[1]
    gates = gates.transpose(0, 2, 1).reshape(tasks * count, features)
    lines = jnp.pad(small, (0, 4 * hidden - small.shape[0])).reshape(4, hidden)
    gap = ((0, GAP - tasks * count), (0, 0))
    tail = jnp.concatenate(
        [
            towers.transpose(0, 2, 1).reshape(-1, hidden),
            jnp.pad(gates[:, :hidden], gap),
            jnp.pad(gates[:, hidden:], gap),
            lines,
        ]
    )
    return jnp.pad(tail, ((0, 2 * half_tail - tail.shape[0]), (0, 0))).reshape(2, half_tail, hidden)


def unpack_tail(tail, gates_shape, towers_shape, small_size):
    tasks, features, count = gates_shape
    _, hidden, tower = towers_shape
    at = tasks * tower
    towers = tail[:at].reshape(tasks, tower, hidden).transpose(0, 2, 1)
    gates = jnp.concatenate([tail[at : at + tasks * count], tail[at + GAP : at + GAP + tasks * count]], axis=1)
    gates = gates.reshape(tasks, count, features).transpose(0, 2, 1)
    at = at + 2 * GAP
    return gates, towers, tail[at : at + 4].reshape(-1)[:small_size], tail[at + 8, 0]


def moments(first, second, grad):
    return (
        BETA_ONE * first + (1.0 - BETA_ONE) * grad,
        BETA_TWO * second + (1.0 - BETA_TWO) * grad * grad,
    )


def stepped(weight, first_new, second_new):
    first_hat = first_new / (1.0 - BETA_ONE**STEP)
    second_hat = second_new / (1.0 - BETA_TWO**STEP)
    return weight - RATE_DENSE * (first_hat / (jnp.sqrt(second_hat) + EPSILON) + DECAY * weight)


def late_requests(n, cap, k, owner, rank, local):
    rows, samples = owner.shape
    inside = (owner < n) & (rank >= k * cap) & (rank < (k + 1) * cap)
    parity = jnp.broadcast_to((jnp.arange(rows) // 4 % 2)[:, None], owner.shape)
    target = jnp.where(inside, owner, n)
    place = jnp.where(inside, rank - k * cap, 0)
    asked = jnp.zeros((n, 2, cap), I32).at[target, parity, place].set(local, mode="drop")
    asked = lax.all_to_all(asked.reshape(n, 2 * cap), "dev", 0, 0, tiled=True)
    return inside, parity, target, place, asked


def late_pool(n, cap, most, owner, rank, local, table, pooled):
    width = table.shape[1]
    rows, samples = owner.shape

    def body(k, pooled):
        inside, parity, target, place, asked = late_requests(n, cap, k, owner, rank, local)
        found = table[asked].reshape(n, 2 * cap * width)
        got = lax.all_to_all(found, "dev", 0, 0, tiled=True).reshape(n, 2, cap, width)
        slot_rows = jnp.where(inside[..., None], got[jnp.minimum(target, n - 1), parity, place], 0.0)
        bags = jnp.sum(slot_rows.reshape(rows // 4, 4, samples, width), axis=1)
        bags = bags.reshape(rows // 8, 2, samples, width).transpose(0, 2, 1, 3)
        return pooled + bags.reshape(rows // 8 * samples, 2 * width)

    return lax.fori_loop(1, (most + cap - 1) // cap, body, pooled)


def late_grads(n, cap, most, owner, rank, local, rows_grad, rows_dev, width):
    rows, samples = owner.shape
    tables = rows // 4

    def body(k, extra):
        inside, parity, target, place, asked = late_requests(n, cap, k, owner, rank, local)
        lines = rows_grad[: tables // 2 * samples].reshape(tables // 2, samples, 2, width)
        bags = lines.transpose(0, 2, 1, 3).reshape(tables, 1, samples, width)
        slot_grads = jnp.broadcast_to(bags, (tables, 4, samples, width)).reshape(rows, samples, width)
        out = jnp.zeros((n, 2, cap, width), F32).at[target, parity, place].set(slot_grads, mode="drop")
        valid = jnp.zeros((n, 2, cap), F32).at[target, parity, place].set(1.0, mode="drop")
        got = lax.all_to_all(out.reshape(n, -1), "dev", 0, 0, tiled=True).reshape(-1, width)
        valid = lax.all_to_all(valid.reshape(n, -1), "dev", 0, 0, tiled=True).reshape(-1, 1)
        return extra + jnp.zeros((rows_dev, width), F32).at[asked.reshape(-1)].add(got * valid).T

    return lax.fori_loop(1, (most + cap - 1) // cap, body, jnp.zeros((width, rows_dev), F32))


def blank(shape):
    return pl.pallas_call(
        lambda out_ref: None,
        out_shape=jax.ShapeDtypeStruct(shape, F32),
        out_specs=pl.BlockSpec(memory_space=pl.ANY),
        name="blank",
    )()


def per_device(
    row_ids, lengths, counts, mask, labels, row_home, mat_home, table, table_m, table_v,
    experts_w, gates_w, towers_w, small_params,
    experts_m, experts_v, gates_m, gates_v, towers_m, towers_v, small_m, small_v,
):
    n = lax.axis_size("dev")
    me = lax.axis_index("dev")
    samples, tables, bag = row_ids.shape
    rows_dev, width = table.shape
    per_table = row_home.shape[1] // n
    cap = max(8, (samples * tables * bag // n * 5 // 16 + 7) // 8 * 8)
    experts, features, hidden = experts_w.shape
    tasks = towers_w.shape[0]
    used_rows = tasks * towers_w.shape[2] + 2 * GAP + 16
    half_tail = -(-used_rows // 2 // (8 * n)) * 8 * n

    tail_m = pack_tail(gates_m[0], towers_m[0], small_m[0], half_tail)
    tail_v = pack_tail(gates_v[0], towers_v[0], small_v[0], half_tail)
    fields, pos, owner, rank, local, mine, theirs, stat, lines, *moment_slices = forward(
        n, cap, row_ids, lengths, counts, mask, labels, row_home, table, mat_home,
        experts_m[0], experts_v[0], tail_m, tail_v,
    )
    most, weight_count = stat[4, 0], stat[5, 0]
    more = most > cap
    pooled = pool(n, cap, tables, bag, pos, lines)
    pooled = lax.cond(
        more, lambda *args: late_pool(n, cap, *args), lambda *args: args[-1], most, owner, rank, local, table, pooled
    )
    grad_a, grad_b, grad_tail, rows_grad = dense(
        half_tail, weight_count[None], fields, pooled, experts_w, gates_w, towers_w, small_params
    )
    back, *grad_slices = backward(n, cap, mine, rows_grad, grad_a, grad_b, grad_tail)
    extra = lax.cond(
        more,
        lambda *args: late_grads(n, cap, *args, rows_dev, width),
        lambda *args: blank((width, rows_dev)),
        most, owner, rank, local, rows_grad,
    )
    table_new, table_m_new, table_v_new = update(
        n, cap, per_table, tables, theirs, most[None], back, table, table_m, table_v, extra
    )
    tail_w = pack_tail(gates_w, towers_w, small_params, half_tail)
    orders = axis_orders(n)
    weights = []
    for source, order in zip((experts_w[0], experts_w[1], tail_w[0], tail_w[1]), orders):
        rows = source.shape[0]
        weights.append(lax.dynamic_slice_in_dim(source, start_of(me, order, rows), rows // n, 0))
    wholes = spread(n, grad_slices, moment_slices, weights)
    experts_new = jnp.stack([wholes[0][0], wholes[1][0]])
    grad_experts = jnp.stack([wholes[0][1], wholes[1][1]])
    tails = jnp.concatenate([wholes[2], wholes[3]], axis=1)
    gates_new, towers_new, small_new, _ = unpack_tail(tails[0], gates_w.shape, towers_w.shape, small_params.shape[0])
    grad_gates, grad_towers, grad_small, loss_sum = unpack_tail(
        tails[1], gates_w.shape, towers_w.shape, small_params.shape[0]
    )
    owned = mat_home == me
    owns = (
        owned[:experts, None, None],
        owned[experts : experts + tasks, None, None],
        owned[experts + tasks : experts + 2 * tasks, None, None],
        owned[experts + 2 * tasks],
    )
    outs_m, outs_v = [], []
    for own, first, second, grad in zip(
        owns, (experts_m, gates_m, towers_m, small_m), (experts_v, gates_v, towers_v, small_v),
        (grad_experts, grad_gates, grad_towers, grad_small),
    ):
        first, second = moments(first[0], second[0], grad)
        outs_m.append(jnp.where(own, first, 0.0)[None])
        outs_v.append(jnp.where(own, second, 0.0)[None])
    return (
        loss_sum, weight_count.astype(F32), table_new, table_m_new, table_v_new,
        experts_new, gates_new, towers_new, small_new,
        outs_m[0], outs_v[0], outs_m[1], outs_v[1], outs_m[2], outs_v[2], outs_m[3], outs_v[3],
        experts_new.astype(BF16)[None], gates_new.astype(BF16)[None],
        towers_new.astype(BF16)[None], small_new.astype(BF16)[None],
    )


def solution(mesh):
    def split(dims):
        return P("dev", *(None,) * (dims - 1))

    by_device = split(4)
    return jax.shard_map(
        per_device,
        mesh=mesh,
        in_specs=(
            split(3), split(2), split(1), split(1), split(2), P(), P(), split(2), split(2), split(1),
            P(), P(), P(), P(),
        ) + (by_device,) * 6 + (split(2),) * 2,
        out_specs=(P(), P(), split(2), split(2), split(1), P(), P(), P(), P())
        + (by_device,) * 6 + (split(2),) * 2 + (by_device,) * 3 + (split(2),),
        check_vma=False,
    )
```

```python
import functools
import jax
import jax.numpy as jnp
from jax import lax
from jax.experimental import pallas as pl
from jax.experimental.pallas import tpu as pltpu
from jax.sharding import PartitionSpec as P

MESH = pl.DeviceIdType.MESH
F32, BF16, I32 = jnp.float32, jnp.bfloat16, jnp.int32
NN, NT, TN = (((1,), (0,)), ((), ())), (((1,), (1,)), ((), ())), (((0,), (0,)), ((), ()))
LANES = 128


def iota(shape, dim):
    return lax.broadcasted_iota(I32, shape, dim)


def dot(a, b, dims=NN):
    return lax.dot_general(a, b, dims, preferred_element_type=F32)


def split3(x):
    high = x.astype(BF16)
    rest = x - high.astype(F32)
    middle = rest.astype(BF16)
    low = (rest - middle.astype(F32)).astype(BF16)
    return high, middle, low


def greet_all(n, me):
    barrier = pltpu.get_barrier_semaphore()

    def signal(k, carry):
        pl.semaphore_signal(barrier, inc=1, device_id=(me ^ k,), device_id_type=MESH)
        return carry

    lax.fori_loop(1, n, signal, 0)
    pl.semaphore_wait(barrier, n - 1)


def exchange(n, me, source, target, sends, receives, k):
    peer = me ^ k
    return pltpu.make_async_remote_copy(
        src_ref=source.at[peer],
        dst_ref=target.at[me],
        send_sem=sends.at[k],
        recv_sem=receives.at[k],
        device_id=(peer,),
        device_id_type=MESH,
    )


def for_range(low, high, body):
    def step(k, carry):
        body(k)
        return carry

    lax.fori_loop(low, high, step, 0)

STEP = 5
BETA_ONE = 0.9
BETA_TWO = 0.999
EPSILON = 1e-08
DECAY = 0.01
RATE_DENSE = 0.02
RATE_ROWS = 0.3
GAP = 16

def axis_orders(n):
    bits = [1 << i for i in range(n.bit_length() - 1)]
    core, rest = bits[:1], bits[1:]
    a = len(rest) // 3
    b = (len(rest) - a) // 2
    x, y, z = rest[:a], rest[a : a + b], rest[a + b :]
    return core + x + y + z, core + y + x + z, core + z + x + y, core + z + y + x


def early_levels(n):
    rest = n.bit_length() - 2
    a = rest // 3
    return 1 + a + (rest - a) // 2


def bit_of(me, bit):
    return lax.rem(lax.div(me, bit), 2)


def start_of(me, order, rows):
    start = 0
    for bit in order:
        rows = rows // 2
        start = start + bit_of(me, bit) * rows
    return start


def rows_at(start, count):
    return pl.ds(pl.multiple_of(start, 8), count)


def plan(n, experts, features, tail_rows):
    unit = 8 * n
    along_x, along_y, along_z, along_w = axis_orders(n)
    chains = []
    for k in range(features // unit):
        for e in range(experts):
            chains.append((e, k * unit, along_y if e % 2 else along_x, k))
    for k in range(tail_rows // unit):
        chains.append((experts, k * unit, along_w if k % 2 else along_z, k // 2))
    return chains


def halving(me, source, stages, sends, receives, c, order, i, lane=0):
    bit = order[i]
    before = source if i == 0 else stages[i - 1].at[c]
    target = stages[i].at[c]
    half = stages[i].shape[-2]
    at = rows_at((1 - bit_of(me, bit)) * half, half)
    if i == 0 and len(stages[0].shape) == 4:
        target = target.at[lane]
        lane_sem = lane * len(order)
    else:
        lane_sem = i
    return pltpu.make_async_remote_copy(
        src_ref=before.at[at] if len(before.shape) == 2 else before.at[:, at],
        dst_ref=target,
        send_sem=sends.at[c, lane_sem],
        recv_sem=receives.at[c, lane_sem],
        device_id=(me ^ bit,),
        device_id_type=MESH,
    )


def fill_tail(tail, towers, gates, small):
    tasks, tower, hidden = towers.shape
    count = gates.shape[1]
    size = small.shape[1]
    tail[...] = jnp.zeros_like(tail)
    tail[0 : tasks * tower, :] = towers[...].reshape(tasks * tower, hidden)
    for part in range(2):
        for k in range(tasks):
            at = tasks * tower + part * GAP + k * count
            tail[at : at + count, :] = gates[k][:, part * hidden : (part + 1) * hidden]
    at = tasks * tower + 2 * GAP
    for i in range(-(-size // hidden)):
        last = min(size, (i + 1) * hidden)
        tail[at + i : at + i + 1, 0 : last - i * hidden] = small[0:1, i * hidden : last]


def owner_side(me, n, items_ref, experts, tasks, tower):
    def chosen(chain, i, count):
        array, first, order, _ = chain
        bit = order[i]
        if array < experts:
            return bit_of(items_ref[array], bit) == bit_of(me, bit)
        towers = tasks * tower
        row = first + start_of(me, order[: i + 1], 8 * n) + iota((count, LANES), 0)
        item = lax.div(row, tower) + experts + tasks
        for part in range(2):
            at = towers + part * GAP
            item = jnp.where((row >= at) & (row < at + tasks * experts), experts + lax.div(row - at, experts), item)
        item = jnp.where(row >= towers + 2 * GAP, experts + 2 * tasks, item)
        home = jnp.zeros((count, LANES), I32)
        for k in range(experts, experts + 2 * tasks + 1):
            home = jnp.where(item == k, items_ref[k], home)
        return (bit_of(home, bit) == bit_of(me, bit))[:, :1]

    return chosen


def forward_kernel(
    sizes,
    ids_ref, lengths_ref, counts_ref, mask_ref, labels_ref, homes_ref, table_ref, items_ref,
    experts_m_ref, experts_v_ref, towers_m_ref, towers_v_ref, gates_m_ref, gates_v_ref, small_m_ref, small_v_ref,
    fields_ref, pos_ref, mine_ref, theirs_ref, pairs_ref, stat_ref, lines_ref, moments_ref,
    outbox, inbox, message, replies, lists, field_scratch, owner_ref, rank_ref, local_ref, asked_smem, rows_ref, rows_out,
    tails, kept_ref, *rest,
):
    n, cap, tables, bag, tasks, experts, per_table, block_rows, rows_dev = sizes
    levels = early_levels(n)
    stages = list(rest[: levels - 1]) + [moments_ref]
    send_a, recv_a, send_b, recv_b, send_c, recv_c, send_m, recv_m, keep_sem, sems = rest[levels - 1 :]
    chains = plan(n, experts, experts_m_ref.shape[1], tails.shape[1])
    unit = 8 * n
    rows = tables * bag
    me = lax.axis_index("dev")
    shift = lax.rem(me * 13, n)
    per_pair = LANES // n
    table_of = lax.div(iota((rows, LANES), 0), bag)
    slot_of = lax.rem(iota((rows, LANES), 0), bag)
    expand = jnp.where(lax.div(iota((rows, tables), 0), bag) == iota((rows, tables), 1), 1.0, 0.0).astype(BF16)
    used = dot(expand, lengths_ref[...].astype(F32).astype(BF16)).astype(I32)
    present = iota((1, LANES), 1) < counts_ref[0]
    live = present & (slot_of < used)
    field_scratch[0:rows, :] = jnp.where(live, ids_ref[...], -1).astype(F32)
    field_scratch[rows : rows + tasks, :] = labels_ref[...]
    field_scratch[rows + tasks : rows + tasks + 1, :] = jnp.where(present & (mask_ref[...] == 1), 1.0, 0.0)
    field_scratch[rows + tasks + 1 :, :] = jnp.zeros((LANES - rows - tasks - 1, LANES), F32)
    row = iota((n * 8, LANES), 0)
    peer_of, piece = lax.div(row, 8), lax.rem(row, 8)
    column = iota((n * 8, LANES), 1)
    pick = jnp.where((piece < per_pair) & (column == piece * n + lax.rem(peer_of - shift + n, n)), 1.0, 0.0).astype(BF16)
    high, middle, low = split3(field_scratch[...])
    spread = dot(pick, high, NT) + dot(pick, middle, NT) + dot(pick, low, NT)
    outbox[...] = spread.reshape(n, 8, LANES)
    greet_all(n, me)
    own_copy = pltpu.make_async_copy(outbox.at[me], inbox.at[me], sems.at[0])
    own_copy.start()
    for_range(1, n, lambda k: exchange(n, me, outbox, inbox, send_a, recv_a, k).start())
    fill_tail(tails.at[0], towers_m_ref, gates_m_ref, small_m_ref)
    fill_tail(tails.at[1], towers_v_ref, gates_v_ref, small_v_ref)

    def whole(c, w):
        array, first, _, _ = chains[c]
        source = tails.at[w] if array == experts else (experts_m_ref, experts_v_ref)[w].at[array]
        return source.at[first : first + unit]

    def hop(c, i, lane=0):
        return halving(me, whole(c, lane) if i == 0 else None, stages, send_m, recv_m, c, chains[c][2], i, lane)

    def keep(c, w):
        at = rows_at(bit_of(me, 1) * (unit // 2), unit // 2)
        return pltpu.make_async_copy(whole(c, w).at[at], kept_ref.at[c, w], keep_sem.at[c, w])

    for c in range(len(chains)):
        for w in range(2):
            hop(c, 0, w).start()
            keep(c, w).start()

    chosen = owner_side(me, n, items_ref, experts, tasks, towers_m_ref.shape[1])

    def settle(c, i):
        order = chains[c][2]
        for w in range(2 if i == 0 else 1):
            hop(c, i, w).wait()
            if i == 0:
                keep(c, w).wait()
        half = stages[i].shape[2]
        mine = rows_at(bit_of(me, order[i]) * half, half)
        flag = chosen(chains[c], i, half)
        for w in range(2):
            kept = kept_ref[c, w] if i == 0 else stages[i - 1][c, w, mine, :]
            stages[i][c, w] = jnp.where(flag, kept, stages[i][c, w])
        if i + 1 < levels:
            hop(c, i + 1).start()

    steps = len(set(chain[3] for chain in chains)) + levels - 1

    def settle_step(s):
        for c, chain in enumerate(chains):
            if 0 <= s - chain[3] < levels:
                settle(c, s - chain[3])

    homes = homes_ref[...]
    blocks = homes.shape[1]
    homes_rows = (
        dot(expand, (homes >> 5).astype(F32).astype(BF16)) * 32.0 + dot(expand, (homes & 31).astype(F32).astype(BF16))
    ).astype(I32)
    gather_back = jnp.where((piece < per_pair) & (column == peer_of * per_pair + piece), 1.0, 0.0).astype(BF16)
    before = jnp.where(iota((LANES, LANES), 0) < iota((LANES, LANES), 1), 1.0, 0.0).astype(BF16)
    ones = jnp.ones((LANES, LANES), BF16)
    r_out, r_in = iota((rows + 8, rows), 0), iota((rows + 8, rows), 1)
    parity_in = lax.rem(lax.div(r_in, bag), 2)
    earlier = (r_out < rows) & (r_in < r_out) & (parity_in == lax.rem(lax.div(r_out, bag), 2))
    totals = (r_out == rows + 2 + parity_in)
    above = jnp.where(earlier | totals, 1.0, 0.0).astype(BF16)
    for_range(1, n, lambda k: exchange(n, me, outbox, inbox, send_a, recv_a, k).wait())
    own_copy.wait()
    settle_step(0)
    arrived = inbox[...].reshape(n * 8, LANES).T
    high, middle, low = split3(arrived)
    fields = dot(high, gather_back) + dot(middle, gather_back) + dot(low, gather_back)
    fields_ref[...] = fields[rows : rows + 8]
    ids = fields[0:rows].astype(I32)
    weight_count = jnp.sum(fields[rows + tasks : rows + tasks + 1], axis=1, keepdims=True).astype(I32)
    live = ids >= 0
    ids = jnp.maximum(ids, 0)
    block = lax.div(ids, block_rows)
    lane = block & (LANES - 1)
    home = jnp.zeros((rows, LANES), I32)
    for part in range(blocks // LANES):
        found = jnp.take_along_axis(homes_rows[:, part * LANES : (part + 1) * LANES], lane, axis=1, mode="promise_in_bounds")
        home = jnp.where(lax.div(block, LANES) == part, found, home)
    owner = jnp.where(live, lax.div(home, per_table), n)
    local = (table_of * per_table + lax.rem(home, per_table)) * block_rows + lax.rem(ids, block_rows)
    owner_ref[...] = owner
    local_ref[...] = local

    def rank_step(o, carry):
        rank, most = carry
        is_mine = owner == o
        flags = jnp.where(is_mine, 1.0, 0.0).astype(BF16)
        row_totals = dot(flags, ones).astype(BF16)
        bases = dot(above, row_totals)
        count = bases[rows : rows + 8].astype(I32)
        message[o] = count
        rank = jnp.where(is_mine, (dot(flags, before) + bases[0:rows]).astype(I32), rank)
        return rank, jnp.maximum(most, count)

    rank, most = lax.fori_loop(
        0, n, rank_step, (jnp.zeros((rows, LANES), I32), jnp.zeros((8, LANES), I32)), unroll=4
    )
    rank_ref[...] = rank
    settle_step(1)
    most = jnp.max(most, axis=0, keepdims=True)
    pos_ref[...] = jnp.where(live, jnp.where(rank < cap, owner * cap + rank, n * cap + 1), n * cap)
    lists[...] = jnp.zeros_like(lists)
    device_row = iota((n, LANES), 0)
    rank_row = iota((LANES, LANES), 0)
    lane_value = (iota((n, LANES), 1)).astype(F32)

    def list_step(q, carry):
        for parity in range(2):
            picks, places = [], []
            for j in range(bag):
                r = (2 * q + parity) * bag + j
                owner_row = owner_ref[pl.ds(r, 1), :]
                local_row = local_ref[pl.ds(r, 1), :]
                hit = device_row == owner_row
                picks.append(
                    jnp.concatenate(
                        [
                            jnp.where(hit, ((local_row >> 7) + 1).astype(F32), 0.0),
                            jnp.where(hit, (local_row & 127).astype(F32), 0.0),
                            jnp.where(hit, (q + 1).astype(F32), 0.0),
                            jnp.where(hit, lane_value, 0.0),
                        ],
                        axis=0,
                    ).astype(BF16)
                )
                places.append(jnp.where(rank_row == rank_ref[pl.ds(r, 1), :], 1.0, 0.0).astype(BF16))
            lists[parity] += dot(jnp.concatenate(picks, axis=1), jnp.concatenate(places, axis=1), NT)
        return carry

    lax.fori_loop(0, tables // 2, list_step, 0)
    sub = iota((8, LANES), 0)
    is_last = iota((1, LANES), 1) == LANES - 1

    def post(k):
        o = me ^ k
        tile = message[o]
        rows_list = []
        for parity in range(2):
            count = tile[2 + parity : 3 + parity]
            got = [lists[parity, pl.ds(part * n + o, 1), :].astype(I32) for part in range(4)]
            asked = jnp.where(got[0] > 0, (got[0] - 1) * LANES + got[1], rows_dev)
            slot = jnp.where(got[0] > 0, (got[2] - 1) * LANES + got[3], tables // 2 * LANES)
            rows_list.append(jnp.where(is_last, count, asked))
            mine_ref[o, parity : parity + 1, :] = jnp.where(is_last, count, slot)
        tile = jnp.where(sub == 0, rows_list[0], jnp.where(sub == 1, rows_list[1], tile))
        message[o] = jnp.where(sub == 4, most, jnp.where(sub == 5, weight_count, tile))

    def post_and_send(k):
        post(k)
        exchange(n, me, message, replies, send_b, recv_b, k).start()

    for_range(1, n, post_and_send)
    post(0)
    own_copy = pltpu.make_async_copy(message.at[me], replies.at[me], sems.at[0])
    own_copy.start()
    settle_step(2)
    width = table_ref.shape[0]
    rows_ref[rows_dev:, :] = jnp.zeros((rows_ref.shape[0] - rows_dev, LANES), F32)

    def turn(b):
        at = pl.ds(pl.multiple_of(b * LANES, LANES), LANES)
        rows_ref[at, :] = jnp.concatenate([table_ref[:, at]] * (LANES // width), axis=0).T

    for_range(0, rows_dev // LANES, turn)
    settle_step(3)
    for_range(1, n, lambda k: exchange(n, me, message, replies, send_b, recv_b, k).wait())
    own_copy.wait()

    def take(s, carry):
        most, total = carry
        tile = replies[s]
        asked = jnp.clip(tile[0:2], 0, rows_dev)
        theirs_ref[s] = asked
        table_rows = per_table * block_rows
        paired = lax.div(asked, 2 * table_rows) * table_rows + lax.rem(asked, table_rows)
        pairs_ref[s] = jnp.where(is_last, asked, paired)
        return jnp.maximum(most, tile), total + tile

    most, total = lax.fori_loop(0, n, take, (jnp.zeros((8, LANES), I32), jnp.zeros((8, LANES), I32)))
    stat_ref[...] = jnp.where(sub == 4, most, total)
    to_scalars = pltpu.make_async_copy(theirs_ref, asked_smem, sems.at[0])
    to_scalars.start()
    to_scalars.wait()
    lines_ref[n] = jnp.zeros((cap, LANES), F32)
    collect = collector(cap, asked_smem, rows_ref)

    def collect_and_send(i):
        k = n - i
        collect(me ^ k, rows_out, me ^ k)
        exchange(n, me, rows_out, lines_ref, send_c, recv_c, k).start()

    group = n // 4
    for s in range(1, 4):
        for_range((s - 1) * group + 1, s * group + 1, collect_and_send)
        settle_step(3 + s)
    for_range(3 * group + 1, n, collect_and_send)
    collect(me, lines_ref, me)
    for s in range(7, steps):
        settle_step(s)
    for_range(1, n, lambda k: exchange(n, me, rows_out, lines_ref, send_c, recv_c, k).wait())


def collector(cap, lists_ref, rows_ref):
    left = iota((1, LANES), 1) < LANES // 2

    def collect(peer, target, slot):
        def lines(g):
            for i in range(8):
                r = g * 8 + i
                even = rows_ref[pl.ds(lists_ref[peer, 0, r], 1), :]
                odd = rows_ref[pl.ds(lists_ref[peer, 1, r], 1), :]
                target[slot, pl.ds(r, 1), :] = jnp.where(left, even, odd)

        for_range(0, cap // 8, lines)

    return collect


def forward(
    n, cap, tail_rows, row_ids, lengths, counts, mask, labels, row_home, table, mat_home,
    experts_m, experts_v, towers_m, towers_v, gates_m, gates_v, small_m, small_v,
):
    samples, tables, bag = row_ids.shape
    rows_dev, width = table.shape
    tasks = labels.shape[1]
    experts, features, hidden = experts_m.shape
    per_table = row_home.shape[1] // n
    block_rows = rows_dev // (tables * per_table)
    levels = early_levels(n)
    sizes = (n, cap, tables, bag, tasks, experts, per_table, block_rows, rows_dev)
    ids = row_ids.transpose(1, 2, 0).reshape(tables * bag, samples)
    vmem = pl.BlockSpec(memory_space=pltpu.VMEM)
    smem = pl.BlockSpec(memory_space=pltpu.SMEM)
    hbm = pl.BlockSpec(memory_space=pl.ANY)
    slots = jax.ShapeDtypeStruct((tables * bag, LANES), I32)
    lists = jax.ShapeDtypeStruct((n, 2, LANES), I32)
    count = len(plan(n, experts, features, tail_rows))
    small = pltpu.VMEM((n, 8, LANES), F32)
    numbers = pltpu.VMEM((n, 8, LANES), I32)
    slot_scratch = pltpu.VMEM((tables * bag, LANES), I32)
    dma = pltpu.SemaphoreType.DMA((n,))
    hops = pltpu.SemaphoreType.DMA((count, n.bit_length()))
    return pl.pallas_call(
        functools.partial(forward_kernel, sizes),
        out_shape=(
            jax.ShapeDtypeStruct((8, LANES), F32), slots, lists, lists, lists,
            jax.ShapeDtypeStruct((8, LANES), I32), jax.ShapeDtypeStruct((n + 1, cap, LANES), F32),
            jax.ShapeDtypeStruct((count, 2, 8 * n >> levels, hidden), F32),
        ),
        in_specs=[vmem, vmem, smem, vmem, vmem, vmem, vmem, smem, hbm, hbm] + [vmem] * 6,
        out_specs=(vmem,) * 8,
        scratch_shapes=[
            small, small, numbers, numbers,
            pltpu.VMEM((2, 4 * n, LANES), F32), pltpu.VMEM((LANES, LANES), F32),
            slot_scratch, slot_scratch, slot_scratch,
            pltpu.SMEM((n, 2, LANES), I32), pltpu.VMEM((rows_dev + 8, LANES), F32), pltpu.VMEM((n, cap, LANES), F32),
            pltpu.VMEM((2, tail_rows, hidden), F32), pltpu.VMEM((count, 2, 4 * n, hidden), F32),
        ]
        + [pltpu.VMEM((count, 2, 4 * n >> i, hidden), F32) for i in range(levels - 1)]
        + [dma] * 6 + [hops] * 2 + [pltpu.SemaphoreType.DMA((count, 2)), pltpu.SemaphoreType.DMA((2,))],
        compiler_params=pltpu.CompilerParams(collective_id=0, has_side_effects=True, vmem_limit_bytes=56 * 2**20),
        name="forward",
    )(
        ids, lengths.T, counts, mask.reshape(1, samples), labels.T, row_home, table.T, mat_home, experts_m, experts_v,
        towers_m.transpose(0, 2, 1), towers_v.transpose(0, 2, 1), gates_m.transpose(0, 2, 1), gates_v.transpose(0, 2, 1),
        small_m, small_v,
    )


def backward_kernel(
    sizes, lists_ref, stat_ref, items_ref, fields_ref, pooled_ref, moments_ref, experts_ref, gates_ref, towers_ref, small_ref,
    lines_ref, experts_out, tail_out, *rest,
):
    n, cap, tail_rows = sizes
    levels, early = n.bit_length() - 1, early_levels(n)
    stages, rest = list(rest[:levels]), rest[levels:]
    late_stages, rest = [moments_ref] + list(rest[: levels - early]), rest[levels - early :]
    grads, tail, tail_w, news, rows_ref, side, rows_out = rest[:7]
    send_c, recv_c, sends, receives, send_m, recv_m, send_w, recv_w, local = rest[7:]
    experts, features, hidden = experts_ref.shape
    tasks, tower, _ = towers_ref.shape
    chains = plan(n, experts, features, tail_rows)
    unit = 8 * n
    me = lax.axis_index("dev")
    greet_all(n, me)

    def late_hop(c, i):
        order = chains[c][2]
        bit = order[early + i]
        half = late_stages[i + 1].shape[2]
        at = rows_at((1 - bit_of(me, bit)) * half, half)
        return pltpu.make_async_remote_copy(
            src_ref=late_stages[i].at[c, :, at],
            dst_ref=late_stages[i + 1].at[c],
            send_sem=send_m.at[c, i],
            recv_sem=recv_m.at[c, i],
            device_id=(me ^ bit,),
            device_id_type=MESH,
        )

    chosen = owner_side(me, n, items_ref, experts, tasks, tower)

    def late_settle(i):
        for c, chain in enumerate(chains):
            late_hop(c, i).wait()
            half = late_stages[i + 1].shape[2]
            mine = rows_at(bit_of(me, chain[2][early + i]) * half, half)
            flag = chosen(chain, early + i, half)
            for w in range(2):
                late_stages[i + 1][c, w] = jnp.where(flag, late_stages[i][c, w, mine, :], late_stages[i + 1][c, w])
            if i + 1 < levels - early:
                late_hop(c, i + 1).start()

    for c in range(len(chains)):
        late_hop(c, 0).start()
    lines_ref[n] = jnp.zeros((cap, LANES), F32)
    fill_tail(tail_w, towers_ref, gates_ref, small_ref)

    def hop(c, i):
        array, first, order, _ = chains[c]
        source = tail if array == experts else grads.at[array]
        return halving(me, source.at[first : first + unit], stages, sends, receives, c, order, i)

    def settle(c, i):
        array, first, order, _ = chains[c]
        hop(c, i).wait()
        half = stages[i].shape[1]
        at = bit_of(me, order[i]) * half
        if i > 0:
            kept = stages[i - 1][c, rows_at(at, half), :]
        elif array == experts:
            kept = tail[rows_at(first + at, half), :]
        else:
            kept = grads[array, rows_at(first + at, half), :]
        stages[i][c] += kept
        if i + 1 < levels:
            hop(c, i + 1).start()

    def region(c, i):
        array, first, order, _ = chains[c]
        at = rows_at(first + start_of(me, order[: i + 1], unit), unit >> (i + 1))
        return tail_out.at[:, at] if array == experts else experts_out.at[array, :, at]

    def doubling(c, i):
        return pltpu.make_async_remote_copy(
            src_ref=region(c, i),
            dst_ref=region(c, i),
            send_sem=send_w.at[c, i],
            recv_sem=recv_w.at[c, i],
            device_id=(me ^ chains[c][2][i],),
            device_id_type=MESH,
        )

    def renew(c):
        array, first, order, _ = chains[c]
        at = rows_at(first + start_of(me, order, unit), 8)
        weight = tail_w[at, :] if array == experts else experts_ref[array, at, :]
        moment = late_stages[-1]
        grad = stages[-1][c]
        news[c, 0] = stepped(weight, *moments(moment[c, 0], moment[c, 1], grad))
        news[c, 1] = grad
        copy = pltpu.make_async_copy(news.at[c], region(c, levels - 1), local.at[c])
        copy.start()
        copy.wait()

    steps = len(set(chain[3] for chain in chains)) + 2 * levels

    def step(s):
        for c, chain in enumerate(chains):
            j = s - chain[3]
            if 0 <= j < levels:
                settle(c, j)
            if j == levels - 1:
                renew(c)
                doubling(c, levels - 1).start()
            i = 2 * levels - 2 - j
            if 0 <= i < levels - 1:
                doubling(c, i + 1).wait()
                doubling(c, i).start()
            if j == 2 * levels - 1:
                doubling(c, 0).wait()

    def ready(array):
        for c, chain in enumerate(chains):
            if chain[0] == array:
                hop(c, 0).start()

    dense_pass(
        ready, stat_ref, fields_ref, pooled_ref, experts_ref, tail_w, towers_ref, small_ref, grads, tail, rows_ref, side
    )
    collect = collector(cap, lists_ref, rows_ref)

    def collect_and_send(i):
        k = n - i
        collect(me ^ k, rows_out, me ^ k)
        exchange(n, me, rows_out, lines_ref, send_c, recv_c, k).start()

    group = n // 8
    for s in range(1, 8):
        for_range((s - 1) * group + 1, s * group + 1, collect_and_send)
        if s <= levels - early:
            late_settle(s - 1)
        step(s - 1)
    for_range(7 * group + 1, n, collect_and_send)
    collect(me, lines_ref, me)
    for s in range(7, steps):
        step(s)
    for_range(1, n, lambda k: exchange(n, me, rows_out, lines_ref, send_c, recv_c, k).wait())


def backward(n, cap, tail_rows, lists, stat, items, fields, pooled, moment_slices, experts_w, gates_w, towers_w, small):
    experts, features, hidden = experts_w.shape
    samples = fields.shape[1]
    levels, early = n.bit_length() - 1, early_levels(n)
    count = len(plan(n, experts, features, tail_rows))
    vmem = pl.BlockSpec(memory_space=pltpu.VMEM)
    smem = pl.BlockSpec(memory_space=pltpu.SMEM)
    dma = pltpu.SemaphoreType.DMA((n,))
    hops = pltpu.SemaphoreType.DMA((count, levels))
    return pl.pallas_call(
        functools.partial(backward_kernel, (n, cap, tail_rows)),
        out_shape=(
            jax.ShapeDtypeStruct((n + 1, cap, LANES), F32),
            jax.ShapeDtypeStruct((experts, 2, features, hidden), F32),
            jax.ShapeDtypeStruct((2, tail_rows, hidden), F32),
        ),
        in_specs=[smem, smem, smem] + [vmem] * 7,
        out_specs=(vmem, pl.BlockSpec(memory_space=pl.ANY), vmem),
        scratch_shapes=[pltpu.VMEM((count, 4 * n >> i, hidden), F32) for i in range(levels)]
        + [pltpu.VMEM((count, 2, 8 * n >> (early + i + 1), hidden), F32) for i in range(levels - early)]
        + [
            pltpu.VMEM((experts, features, hidden), F32), pltpu.VMEM((tail_rows, hidden), F32),
            pltpu.VMEM((tail_rows, hidden), F32), pltpu.VMEM((count, 2, 8, hidden), F32),
            pltpu.VMEM((features // LANES * samples + 8, LANES), F32), pltpu.VMEM((samples, samples), F32),
            pltpu.VMEM((n, cap, LANES), F32),
        ]
        + [dma] * 2 + [hops] * 6 + [pltpu.SemaphoreType.DMA((count,))],
        compiler_params=pltpu.CompilerParams(collective_id=1, has_side_effects=True, vmem_limit_bytes=56 * 2**20),
        name="backward",
    )(lists, stat, items, fields, pooled, moment_slices, experts_w, gates_w, towers_w, small)


def finish_kernel(
    owned_ref, whole_ref, first_ref, second_ref, tail_ref, towers_m_ref, towers_v_ref, gates_m_ref, gates_v_ref,
    small_m_ref, small_v_ref,
    new_ref, low_ref, first_new_ref, second_new_ref,
    towers_ref, towers_low_ref, towers_m_new_ref, towers_v_new_ref, gates_ref, gates_m_new_ref, gates_v_new_ref,
    small_ref, small_m_new_ref, small_v_new_ref, loss_ref,
):
    e, b = pl.program_id(0), pl.program_id(1)
    new = whole_ref[0, 0]
    new_ref[0] = new
    low_ref[0] = new.astype(BF16)

    @pl.when(owned_ref[e] == 1)
    def _():
        first_new_ref[0], second_new_ref[0] = moments(first_ref[0], second_ref[0], whole_ref[0, 1])

    @pl.when(owned_ref[e] != 1)
    def _():
        first_new_ref[...] = jnp.zeros_like(first_new_ref)
        second_new_ref[...] = jnp.zeros_like(second_new_ref)

    @pl.when((e == 0) & (b == 0))
    def _():
        experts = pl.num_programs(0)
        tasks, tower, hidden = towers_ref.shape
        count = gates_ref.shape[1]

        def mine(item, pair):
            own = jnp.full((1, 1), owned_ref[item], I32) == 1
            return [jnp.where(own, x, 0.0) for x in pair]

        for k in range(tasks):
            at = slice(k * tower, (k + 1) * tower)
            towers_ref[k] = tail_ref[0, at]
            towers_low_ref[k] = tail_ref[0, at].astype(BF16)
            towers_m_new_ref[k], towers_v_new_ref[k] = mine(
                experts + tasks + k, moments(towers_m_ref[k], towers_v_ref[k], tail_ref[1, at])
            )
            for part in range(2):
                row = tasks * tower + part * GAP + k * count
                at = slice(row, row + count)
                to = slice(part * hidden, (part + 1) * hidden)
                gates_ref[k, :, to] = tail_ref[0, at]
                gates_m_new_ref[k, :, to], gates_v_new_ref[k, :, to] = mine(
                    experts + k, moments(gates_m_ref[k, :, to], gates_v_ref[k, :, to], tail_ref[1, at])
                )
        base = tasks * tower + 2 * GAP
        size = small_ref.shape[1]
        for i in range(-(-size // hidden)):
            last = min(size, (i + 1) * hidden)
            to = slice(i * hidden, last)
            line = slice(0, last - i * hidden)
            small_ref[0:1, to] = tail_ref[0, base + i : base + i + 1, line]
            small_m_new_ref[0:1, to], small_v_new_ref[0:1, to] = mine(
                experts + 2 * tasks,
                moments(small_m_ref[0:1, to], small_v_ref[0:1, to], tail_ref[1, base + i : base + i + 1, line]),
            )
        loss_ref[...] = tail_ref[1, base + 8 : base + 9, 0:LANES]


def finish(owned, whole, tail, experts_m, experts_v, towers_m, towers_v, gates_m, gates_v, small_m, small_v):
    experts, features, hidden = experts_m.shape
    rows = min(features, 512)
    here = lambda e, b, owned: (e, b, 0)
    only_owner = lambda e, b, owned: (e, jnp.where(owned[e] == 1, b, 0), 0)
    block = pl.BlockSpec((1, rows, hidden), here)
    owners = pl.BlockSpec((1, rows, hidden), only_owner)

    def full(x):
        return pl.BlockSpec(x.shape, lambda e, b, owned: (0,) * len(x.shape))

    small_size = small_m.shape[1]
    towers = jax.ShapeDtypeStruct(towers_m.shape, F32)
    gates = jax.ShapeDtypeStruct(gates_m.shape, F32)
    small = jax.ShapeDtypeStruct((1, small_size), F32)
    wide = jax.ShapeDtypeStruct(experts_m.shape, F32)
    tail_shapes = (
        towers, jax.ShapeDtypeStruct(towers_m.shape, BF16), towers, towers, gates, gates, gates, small, small, small,
        jax.ShapeDtypeStruct((1, LANES), F32),
    )
    return pl.pallas_call(
        finish_kernel,
        grid_spec=pltpu.PrefetchScalarGridSpec(
            num_scalar_prefetch=1,
            grid=(experts, features // rows),
            in_specs=[
                pl.BlockSpec((1, 2, rows, hidden), lambda e, b, owned: (e, 0, b, 0)), owners, owners,
                full(tail), full(towers_m), full(towers_v), full(gates_m), full(gates_v), full(small_m), full(small_v),
            ],
            out_specs=[block, block, block, block] + [full(x) for x in tail_shapes],
        ),
        out_shape=(wide, jax.ShapeDtypeStruct(experts_m.shape, BF16), wide, wide) + tail_shapes,
        compiler_params=pltpu.CompilerParams(vmem_limit_bytes=40 * 2**20),
        name="finish",
    )(owned, whole, experts_m, experts_v, tail, towers_m, towers_v, gates_m, gates_v, small_m, small_v)

def pool_kernel(nothing, tables, bag, pos_ref, lines_ref, pooled_ref):
    samples = pos_ref.shape[1]
    pooled_ref[...] = jnp.zeros_like(pooled_ref)
    left = iota((1, LANES), 1) < LANES // 2

    def sample(s):
        @pl.when(pos_ref[0, s] != nothing)
        def _():
            for q in range(tables // 2):
                sums = []
                for parity in range(2):
                    base = (2 * q + parity) * bag
                    total = lines_ref[pl.ds(pos_ref[base, s], 1), :]
                    for j in range(1, bag):
                        total = total + lines_ref[pl.ds(pos_ref[base + j, s], 1), :]
                    sums.append(total)
                pooled_ref[pl.ds(q * samples + s, 1), :] = jnp.where(left, sums[0], sums[1])

    for_range(0, samples, sample)


def pool(n, cap, tables, bag, pos, lines):
    samples = pos.shape[1]
    return pl.pallas_call(
        functools.partial(pool_kernel, n * cap, tables, bag),
        out_shape=jax.ShapeDtypeStruct((tables // 2 * samples, LANES), F32),
        in_specs=[pl.BlockSpec(memory_space=pltpu.SMEM), pl.BlockSpec(memory_space=pltpu.VMEM)],
        out_specs=pl.BlockSpec(memory_space=pltpu.VMEM),
        compiler_params=pltpu.CompilerParams(vmem_limit_bytes=24 * 2**20),
        name="pool",
    )(pos, lines.reshape((n + 1) * cap, LANES))


def split2(x):
    high = x.astype(BF16)
    return high, (x - high.astype(F32)).astype(BF16)


def dot3(a, b, dims=NN):
    return dot(a[0], b[0], dims) + dot(a[0], b[1], dims) + dot(a[1], b[0], dims)


def sigmoid(x):
    return 1.0 / (1.0 + jnp.exp(-x))


def dense_pass(
    ready, stat_ref, fields_ref, pooled_ref, experts_ref, tail_w, towers_ref, small_ref, grads, tail, rows_ref, side
):
    samples = fields_ref.shape[1]
    experts, features, hidden = experts_ref.shape
    tasks, tower, _ = towers_ref.shape
    tail[...] = jnp.zeros_like(tail)

    def put_tail(row, value):
        tail[row : row + value.shape[0], :] = value

    start = experts * hidden
    tower_at = start
    weight_at = start + tasks * tower
    bias_at = weight_at + tasks * tower
    side[0:8, :] = fields_ref[...]
    side[8:, :] = jnp.zeros((samples - 8, samples), F32)
    by_sample = side[...].T
    weight = by_sample[:, tasks : tasks + 1]
    scale = weight / stat_ref[0].astype(F32)
    x = jnp.concatenate([pooled_ref[q * samples : (q + 1) * samples] for q in range(features // LANES)], axis=1)
    x2 = split2(x)
    at = tasks * tower
    gate_w = jnp.concatenate([tail_w[at + k * GAP : at + k * GAP + tasks * experts, :] for k in range(2)], axis=1)
    gate_w2 = split2(gate_w)
    gate_logits = dot3(x2, gate_w2, NT)
    pres, sigs, hids = [], [], []
    for e in range(experts):
        pre = dot3(x2, split2(experts_ref[e])) + small_ref[0:1, e * hidden : (e + 1) * hidden]
        sig = sigmoid(pre)
        pres.append(pre)
        sigs.append(sig)
        hids.append(pre * sig)
    dhids = [jnp.zeros((samples, hidden), F32) for _ in range(experts)]
    dgate_logits = []
    loss = jnp.zeros((samples, 1), F32)
    tower_bias_grads, out_weight_grads, task_bias_grads = [], [], []
    for k in range(tasks):
        logits = [gate_logits[:, k * experts + e : k * experts + e + 1] for e in range(experts)]
        top = functools.reduce(jnp.maximum, logits)
        powers = [jnp.exp(v - top) for v in logits]
        whole = functools.reduce(jnp.add, powers)
        gates = [v / whole for v in powers]
        mix = functools.reduce(jnp.add, [gates[e] * hids[e] for e in range(experts)])
        mix2 = split2(mix)
        tower2 = split2(towers_ref[k])
        at = tower_at + k * tower
        pre = dot3(mix2, tower2, NT) + small_ref[0:1, at : at + tower]
        sig = sigmoid(pre)
        zed = pre * sig
        at = weight_at + k * tower
        out_weight = small_ref[0:1, at : at + tower]
        logit = jnp.sum(zed * out_weight, axis=1, keepdims=True) + small_ref[0:1, bias_at + k : bias_at + k + 1]
        label = by_sample[:, k : k + 1]
        softplus = jnp.maximum(logit, 0.0) + jnp.log1p(jnp.exp(-jnp.abs(logit)))
        loss = loss + weight * (softplus - label * logit)
        dlogit = scale * (sigmoid(logit) - label)
        task_bias_grads.append(jnp.sum(dlogit, axis=0, keepdims=True))
        out_weight_grads.append(jnp.sum(dlogit * zed, axis=0, keepdims=True))
        dpre = dlogit * out_weight * (sig * (1.0 + pre * (1.0 - sig)))
        tower_bias_grads.append(jnp.sum(dpre, axis=0, keepdims=True))
        dpre2 = split2(dpre)
        put_tail(k * tower, dot3(split2(dpre.T), mix2))
        dmix = dot3(dpre2, tower2)
        dgates = [jnp.sum(dmix * hids[e], axis=1, keepdims=True) for e in range(experts)]
        mean = functools.reduce(jnp.add, [gates[e] * dgates[e] for e in range(experts)])
        for e in range(experts):
            dgate_logits.append(gates[e] * (dgates[e] - mean))
            dhids[e] = dhids[e] + gates[e] * dmix
    lane = iota((samples, LANES), 1)
    dgl = jnp.zeros((samples, LANES), F32)
    for i, v in enumerate(dgate_logits):
        dgl = jnp.where(lane == i, v, dgl)
    count = tasks * experts
    dgl_t2 = split2(dgl.T[0:16])
    dgates_w = dot3(dgl_t2, x2)
    tail_at = tasks * tower
    put_tail(tail_at, dgates_w[:, :hidden])
    put_tail(tail_at + GAP, dgates_w[:, hidden:])
    dx = dot3(split2(dgl[:, :count]), gate_w2)
    expert_bias_grads, dpres = [], []
    for e in range(experts):
        dpre = dhids[e] * (sigs[e] * (1.0 + pres[e] * (1.0 - sigs[e])))
        expert_bias_grads.append(jnp.sum(dpre, axis=0, keepdims=True))
        dpres.append(split2(dpre))
        dx = dx + dot3(dpres[e], split2(experts_ref[e]), NT)
    for q in range(features // LANES):
        rows_ref[q * samples : (q + 1) * samples, :] = dx[:, q * LANES : (q + 1) * LANES]
    rows_ref[features // LANES * samples :, :] = jnp.zeros((8, LANES), F32)
    small_at = tail_at + 2 * GAP
    pad = jnp.zeros((1, 2 * hidden - 2 * tasks * tower - tasks), F32)
    line = jnp.concatenate(tower_bias_grads + out_weight_grads + task_bias_grads + [pad], axis=1)
    loss_row = jnp.where(iota((1, hidden), 1) == 0, jnp.sum(loss, axis=0, keepdims=True), 0.0)
    for e in range(experts):
        put_tail(small_at + e, expert_bias_grads[e])
    for i in range(line.shape[1] // hidden):
        put_tail(small_at + experts + i, line[:, i * hidden : (i + 1) * hidden])
    put_tail(small_at + 8, loss_row)
    ready(experts)
    x_t2 = split2(x.T)
    for e in range(experts):
        grads[e] = dot3(x_t2, dpres[e])
        ready(e)


def update_kernel(
    sizes, pairs_ref, lines_ref, table_ref, first_ref, second_ref,
    table_new_ref, first_new_ref, second_new_ref, sums_even, sums_odd,
):
    n, cap = sizes
    step = pl.program_id(0)
    width, block = table_ref.shape
    half = block // 2
    rows = sums_even.shape[0] - 8

    @pl.when(step == 0)
    def _():
        def clear(i):
            at = pl.ds(pl.multiple_of(i * half, half), half)
            sums_even[at, :] = jnp.zeros((half, LANES), F32)
            sums_odd[at, :] = jnp.zeros((half, LANES), F32)

        for_range(0, rows // half, clear)

        def source(s):
            count = jnp.minimum(jnp.maximum(pairs_ref[s, 0, LANES - 1], pairs_ref[s, 1, LANES - 1]), cap)

            def add(g):
                for i in range(4):
                    r = g * 4 + i
                    line = lines_ref[pl.ds(s * cap + r, 1), :]
                    sums_even[pl.ds(pairs_ref[s, 0, r], 1), :] += line
                    sums_odd[pl.ds(pairs_ref[s, 1, r], 1), :] += line

            for_range(0, (count + 3) // 4, add)

        for_range(0, n, source)

    left = iota((LANES, LANES), 1) < width
    for b in range(half // LANES):
        at = pl.ds(pl.multiple_of(step * half + b * LANES, LANES), LANES)
        both = jnp.where(left, sums_even[at, :], sums_odd[at, :]).T
        for parity in range(2):
            here = slice(parity * half + b * LANES, parity * half + (b + 1) * LANES)
            grad = both[parity * width : (parity + 1) * width]
            first = BETA_ONE * first_ref[:, here] + (1.0 - BETA_ONE) * grad
            mean = jnp.sum(grad * grad, axis=0, keepdims=True) * (1.0 / width)
            second = BETA_TWO * second_ref[:, here] + (1.0 - BETA_TWO) * mean
            rate = (RATE_ROWS / (1.0 - BETA_ONE**STEP)) / (
                jnp.sqrt(second * (1.0 / (1.0 - BETA_TWO**STEP))) + EPSILON
            )
            old = table_ref[:, here]
            table_new_ref[:, here] = old - (first * rate + (RATE_ROWS * DECAY) * old)
            first_new_ref[:, here] = first
            second_new_ref[:, here] = second


def update(n, cap, table_rows, pairs, lines, table, table_m, table_v):
    rows_dev, width = table.shape
    block = 2 * table_rows
    wide = pl.BlockSpec((width, block), lambda i: (0, i))
    thin = pl.BlockSpec((1, block), lambda i: (0, i))
    sums = pltpu.VMEM((rows_dev // 2 + 8, LANES), F32)
    table_new, first_new, second_new = pl.pallas_call(
        functools.partial(update_kernel, (n, cap)),
        grid=(rows_dev // block,),
        out_shape=(
            jax.ShapeDtypeStruct((width, rows_dev), F32), jax.ShapeDtypeStruct((width, rows_dev), F32),
            jax.ShapeDtypeStruct((1, rows_dev), F32),
        ),
        in_specs=[
            pl.BlockSpec(memory_space=pltpu.SMEM), pl.BlockSpec(((n + 1) * cap, LANES), lambda i: (0, 0)), wide, wide, thin,
        ],
        out_specs=(wide, wide, thin),
        scratch_shapes=[sums, sums],
        compiler_params=pltpu.CompilerParams(vmem_limit_bytes=48 * 2**20),
        name="update_rows",
    )(pairs, lines.reshape((n + 1) * cap, LANES), table.T, table_m.T, table_v.reshape(1, rows_dev))
    return table_new.T, first_new.T, second_new.reshape(rows_dev)

def moments(first, second, grad):
    return (
        BETA_ONE * first + (1.0 - BETA_ONE) * grad,
        BETA_TWO * second + (1.0 - BETA_TWO) * grad * grad,
    )


def stepped(weight, first_new, second_new):
    first_hat = first_new / (1.0 - BETA_ONE**STEP)
    second_hat = second_new / (1.0 - BETA_TWO**STEP)
    return weight - RATE_DENSE * (first_hat / (jnp.sqrt(second_hat) + EPSILON) + DECAY * weight)


def all_sum(tree, axis):
    n = lax.axis_size(axis)
    bit = 1
    while bit < n:
        pairs = [(i, i ^ bit) for i in range(n)]
        tree = jax.tree.map(lambda x: x + lax.ppermute(x, axis, pairs), tree)
        bit *= 2
    return tree


def from_root(block, axis, source):
    block = jnp.where(lax.axis_index(axis) == source, block, jnp.zeros_like(block))
    return all_sum(block, axis)


def dense_forward(params, pooled, labels, weights):
    experts_w, gates_w, towers_w, small = params
    n_experts, _, hidden = experts_w.shape
    tasks, _, tower = towers_w.shape
    start = n_experts * hidden
    expert_bias = small[:start].reshape(n_experts, hidden)
    tower_bias = small[start : start + tasks * tower].reshape(tasks, tower)
    start = start + tasks * tower
    out_weight = small[start : start + tasks * tower].reshape(tasks, tower)
    task_bias = small[start + tasks * tower :]
    hidden_act = jax.nn.silu(
        jnp.einsum("si,eih->seh", pooled, experts_w, precision=lax.Precision.HIGHEST) + expert_bias
    )
    gate = jax.nn.softmax(jnp.einsum("si,kie->ske", pooled, gates_w, precision=lax.Precision.HIGHEST), axis=-1)
    mixed = jnp.einsum("ske,seh->skh", gate, hidden_act, precision=lax.Precision.HIGHEST)
    zed = jax.nn.silu(jnp.einsum("skh,khc->skc", mixed, towers_w, precision=lax.Precision.HIGHEST) + tower_bias)
    logit = jnp.sum(zed * out_weight, axis=-1) + task_bias
    losses = jax.nn.softplus(logit) - labels * logit
    return jnp.sum(weights[:, None] * losses)


def adam_step(weight, first, second, grad, rate):
    first_new = BETA_ONE * first + (1.0 - BETA_ONE) * grad
    second_new = BETA_TWO * second + (1.0 - BETA_TWO) * grad * grad
    first_hat = first_new / (1.0 - BETA_ONE**STEP)
    second_hat = second_new / (1.0 - BETA_TWO**STEP)
    weight_new = weight - rate * (first_hat / (jnp.sqrt(second_hat) + EPSILON) + DECAY * weight)
    return (weight_new, first_new, second_new)


def plain_step(
    row_ids,
    lengths,
    counts,
    mask,
    labels,
    row_home,
    mat_home,
    table,
    table_m,
    table_v,
    experts_w,
    gates_w,
    towers_w,
    small_params,
    experts_m,
    experts_v,
    gates_m,
    gates_v,
    towers_m,
    towers_v,
    small_m,
    small_v,
):
    devices = lax.axis_size("dev")
    myself = lax.axis_index("dev")
    samples, tables, bag_slots = row_ids.shape
    rows_dev, width = table.shape
    per_table = row_home.shape[1] // devices
    block_rows = rows_dev // (tables * per_table)
    slots = samples * tables * bag_slots
    average = slots // devices
    capacity = average + average // 2
    present = jnp.arange(samples) < counts[0]
    weights = jnp.where(present & (mask == 1), 1.0, 0.0).astype(jnp.float32)
    live = present[:, None, None] & (jnp.arange(bag_slots)[None, None, :] < lengths[:, :, None])
    table_of = jnp.broadcast_to(jnp.arange(tables)[None, :, None], row_ids.shape)
    homes = row_home[table_of, row_ids // block_rows]
    owners = (homes // per_table).reshape(-1)
    local_rows = (
        (table_of * per_table + homes % per_table) * block_rows + row_ids % block_rows
    ).reshape(-1)
    live_flat = live.reshape(-1)
    live_float = live_flat.astype(jnp.float32)
    targets = jnp.where(live_flat, owners, devices)
    order = jnp.argsort(targets, stable=True)
    sorted_targets = targets[order]
    starts = jnp.searchsorted(sorted_targets, jnp.arange(devices + 1), side="left")
    sorted_rank = jnp.arange(slots, dtype=jnp.int32) - starts[sorted_targets]
    slot_rank = jnp.zeros(slots, jnp.int32).at[order].set(sorted_rank)
    slot_rank = jnp.where(live_flat, slot_rank, 0)
    requests = (
        jnp.zeros((devices, capacity), jnp.int32)
        .at[targets, slot_rank]
        .set(local_rows, mode="drop")
    )
    asked_rows = lax.all_to_all(requests, "dev", split_axis=0, concat_axis=0, tiled=True)
    found = table[asked_rows]
    arrived = lax.all_to_all(found, "dev", split_axis=0, concat_axis=0, tiled=True)
    safe_owner = jnp.minimum(owners, devices - 1)
    slot_rows = arrived[safe_owner, slot_rank] * live_float[:, None]
    pooled = jnp.sum(slot_rows.reshape(samples, tables, bag_slots, width), axis=2).reshape(
        samples, tables * width
    )
    params = (experts_w, gates_w, towers_w, small_params)
    local_loss, pull = jax.vjp(
        lambda dense, features: dense_forward(dense, features, labels, weights), params, pooled
    )
    loss_sum, weight_sum = all_sum((local_loss, jnp.sum(weights)), "dev")
    local_grads, pooled_grad = pull(1.0 / weight_sum)
    slot_grads = (
        jnp.broadcast_to(
            pooled_grad.reshape(samples, tables, 1, width), (samples, tables, bag_slots, width)
        ).reshape(slots, width)
        * live_float[:, None]
    )
    outgoing = (
        jnp.zeros((devices, capacity, width), jnp.float32)
        .at[targets, slot_rank]
        .set(slot_grads, mode="drop")
    )
    incoming = lax.all_to_all(outgoing, "dev", split_axis=0, concat_axis=0, tiled=True)
    grad_table = (
        jnp.zeros((rows_dev, width), jnp.float32)
        .at[asked_rows.reshape(-1)]
        .add(incoming.reshape(-1, width))
    )
    table_m_new = BETA_ONE * table_m + (1.0 - BETA_ONE) * grad_table
    table_v_new = BETA_TWO * table_v + (1.0 - BETA_TWO) * jnp.mean(grad_table * grad_table, axis=1)
    first_hat = table_m_new / (1.0 - BETA_ONE**STEP)
    second_hat = table_v_new / (1.0 - BETA_TWO**STEP)
    table_new = table - RATE_ROWS * (
        first_hat / (jnp.sqrt(second_hat)[:, None] + EPSILON) + DECAY * table
    )
    grad_experts, grad_gates, grad_towers, grad_small = local_grads
    grad_experts, grad_gates, grad_towers, grad_small = all_sum(
        (grad_experts, grad_gates, grad_towers, grad_small), "dev"
    )
    kinds = (
        (experts_w, experts_m[0], experts_v[0], grad_experts),
        (gates_w, gates_m[0], gates_v[0], grad_gates),
        (towers_w, towers_m[0], towers_v[0], grad_towers),
        (small_params[None], small_m, small_v, grad_small[None]),
    )
    finals = []
    first_outs = []
    second_outs = []
    base = 0
    for stack, firsts, seconds, grad in kinds:
        kind_weights = []
        kind_firsts = []
        kind_seconds = []
        for position in range(stack.shape[0]):
            owner_id = mat_home[base + position]
            is_owner = owner_id == myself
            weight_new, first_new, second_new = adam_step(
                stack[position], firsts[position], seconds[position], grad[position], RATE_DENSE
            )
            kind_firsts.append(jnp.where(is_owner, first_new, 0.0))
            kind_seconds.append(jnp.where(is_owner, second_new, 0.0))
            kept = jnp.where(is_owner, weight_new, stack[position])
            kind_weights.append(from_root(kept, "dev", owner_id))
        base = base + stack.shape[0]
        finals.append(jnp.stack(kind_weights))
        first_outs.append(jnp.stack(kind_firsts)[None])
        second_outs.append(jnp.stack(kind_seconds)[None])
    experts_new, gates_new, towers_new, small_stack = finals
    small_new = small_stack[0]
    return (
        loss_sum,
        weight_sum,
        table_new,
        table_m_new,
        table_v_new,
        experts_new,
        gates_new,
        towers_new,
        small_new,
        first_outs[0],
        second_outs[0],
        first_outs[1],
        second_outs[1],
        first_outs[2],
        second_outs[2],
        first_outs[3][0],
        second_outs[3][0],
        experts_new.astype(jnp.bfloat16)[None],
        gates_new.astype(jnp.bfloat16)[None],
        towers_new.astype(jnp.bfloat16)[None],
        small_new.astype(jnp.bfloat16)[None],
    )


def per_device(*args):
    (
        row_ids, lengths, counts, mask, labels, row_home, mat_home, table, table_m, table_v,
        experts_w, gates_w, towers_w, small_params,
        experts_m, experts_v, gates_m, gates_v, towers_m, towers_v, small_m, small_v,
    ) = args
    n = lax.axis_size("dev")
    me = lax.axis_index("dev")
    samples, tables, bag = row_ids.shape
    rows_dev, width = table.shape
    cap = max(8, (samples * tables * bag // n * 5 // 16 + 7) // 8 * 8)
    experts, features, hidden = experts_w.shape
    tasks, _, tower = towers_w.shape
    tail_rows = -(-(tasks * tower + 2 * GAP + 16) // (8 * n)) * 8 * n
    fields, pos, mine, theirs, pairs, stat, lines, moment_slices = forward(
        n, cap, tail_rows, row_ids, lengths, counts, mask, labels, row_home, table, mat_home,
        experts_m[0], experts_v[0], towers_m[0], towers_v[0], gates_m[0], gates_v[0], small_m, small_v,
    )
    most, weight_count = stat[4, 0], stat[5, 0]

    def usual(fields, pos, mine, pairs, lines, moment_slices, weight_count, *args):
        (
            _, _, _, _, _, _, mat_home, table, table_m, table_v, experts_w, gates_w, towers_w, small_params,
            experts_m, experts_v, gates_m, gates_v, towers_m, towers_v, small_m, small_v,
        ) = args

        def turned(x):
            return x.transpose(0, 2, 1)

        gates_t, towers_t, small = turned(gates_w), turned(towers_w), small_params.reshape(1, -1)
        pooled = pool(n, cap, tables, bag, pos, lines)
        back, whole, tail = backward(
            n, cap, tail_rows, mine, weight_count[None], mat_home, fields, pooled, moment_slices,
            experts_w, gates_t, towers_t, small,
        )
        rows_new = update(n, cap, rows_dev // tables, pairs, back, table, table_m, table_v)
        (
            experts_new, experts_low, experts_m_new, experts_v_new,
            towers_new, towers_low, towers_m_new, towers_v_new, gates_new, gates_m_new, gates_v_new,
            small_new, small_m_new, small_v_new, loss,
        ) = finish(
            (mat_home == me).astype(I32), whole, tail, experts_m[0], experts_v[0], turned(towers_m[0]), turned(towers_v[0]),
            turned(gates_m[0]), turned(gates_v[0]), small_m, small_v,
        )
        gates_new = turned(gates_new)
        small_new = small_new.reshape(-1)
        return (
            loss[0, 0], weight_count.astype(F32), *rows_new, experts_new, gates_new, turned(towers_new), small_new,
            experts_m_new[None], experts_v_new[None], turned(gates_m_new)[None], turned(gates_v_new)[None],
            turned(towers_m_new)[None], turned(towers_v_new)[None], small_m_new, small_v_new,
            experts_low[None], gates_new.astype(BF16)[None], turned(towers_low)[None], small_new.astype(BF16)[None],
        )

    def crowded(fields, pos, mine, pairs, lines, moment_slices, weight_count, *args):
        return plain_step(*args)

    return lax.cond(
        most <= cap, usual, crowded, fields, pos, mine, pairs, lines, moment_slices, weight_count, *args
    )


def solution(mesh):
    def split(dims):
        return P("dev", *(None,) * (dims - 1))

    by_device = split(4)
    return jax.shard_map(
        per_device,
        mesh=mesh,
        in_specs=(
            split(3), split(2), split(1), split(1), split(2), P(), P(), split(2), split(2), split(1),
            P(), P(), P(), P(),
        ) + (by_device,) * 6 + (split(2),) * 2,
        out_specs=(P(), P(), split(2), split(2), split(1), P(), P(), P(), P())
        + (by_device,) * 6 + (split(2),) * 2 + (by_device,) * 3 + (split(2),),
        check_vma=False,
    )
```

```python
import functools
import jax
import jax.numpy as jnp
from jax import lax
from jax.experimental import pallas as pl
from jax.experimental.pallas import tpu as pltpu
from jax.sharding import PartitionSpec as P

MESH = pl.DeviceIdType.MESH
F32, BF16, I32 = jnp.float32, jnp.bfloat16, jnp.int32
NN, NT, TN = (((1,), (0,)), ((), ())), (((1,), (1,)), ((), ())), (((0,), (0,)), ((), ()))
LANES = 128


def iota(shape, dim):
    return lax.broadcasted_iota(I32, shape, dim)


def dot(a, b, dims=NN):
    return lax.dot_general(a, b, dims, preferred_element_type=F32)


def split3(x):
    high = x.astype(BF16)
    rest = x - high.astype(F32)
    middle = rest.astype(BF16)
    low = (rest - middle.astype(F32)).astype(BF16)
    return high, middle, low


def greet_all(n, me):
    barrier = pltpu.get_barrier_semaphore()

    def signal(k, carry):
        pl.semaphore_signal(barrier, inc=1, device_id=(me ^ k,), device_id_type=MESH)
        return carry

    lax.fori_loop(1, n, signal, 0)


def await_all(n):
    pl.semaphore_wait(pltpu.get_barrier_semaphore(), n - 1)


def exchange(n, me, source, target, sends, receives, k):
    peer = me ^ k
    return pltpu.make_async_remote_copy(
        src_ref=source.at[peer],
        dst_ref=target.at[me],
        send_sem=sends.at[k],
        recv_sem=receives.at[k],
        device_id=(peer,),
        device_id_type=MESH,
    )


def for_range(low, high, body):
    def step(k, carry):
        body(k)
        return carry

    lax.fori_loop(low, high, step, 0)

STEP = 5
BETA_ONE = 0.9
BETA_TWO = 0.999
EPSILON = 1e-08
DECAY = 0.01
RATE_DENSE = 0.02
RATE_ROWS = 0.3
GAP = 16

def axis_orders(n):
    bits = [1 << i for i in range(n.bit_length() - 1)]
    core, rest = bits[:1], bits[1:]
    a = len(rest) // 3
    b = (len(rest) - a) // 2
    x, y, z = rest[:a], rest[a : a + b], rest[a + b :]
    return core + x + y + z, core + y + x + z, core + z + x + y, core + z + y + x


def early_levels(n):
    rest = n.bit_length() - 2
    a = rest // 3
    return 1 + a + (rest - a) // 2


def bit_of(me, bit):
    return lax.rem(lax.div(me, bit), 2)


def start_of(me, order, rows):
    start = 0
    for bit in order:
        rows = rows // 2
        start = start + bit_of(me, bit) * rows
    return start


def rows_at(start, count):
    return pl.ds(pl.multiple_of(start, 8), count)


def plan(n, experts, features, tail_rows):
    unit = 8 * n
    along_x, along_y, along_z, along_w = axis_orders(n)
    chains = []
    for k in range(features // unit):
        for e in range(experts):
            chains.append((e, k * unit, along_y if e % 2 else along_x, k))
    for k in range(tail_rows // unit):
        chains.append((experts, k * unit, along_w if k % 2 else along_z, k // 2))
    return chains


def halving(me, source, stages, sends, receives, c, order, i, lane=0):
    bit = order[i]
    before = source if i == 0 else stages[i - 1].at[c]
    target = stages[i].at[c]
    half = stages[i].shape[-2]
    at = rows_at((1 - bit_of(me, bit)) * half, half)
    if i == 0 and len(stages[0].shape) == 4:
        target = target.at[lane]
        lane_sem = lane * len(order)
    else:
        lane_sem = i
    return pltpu.make_async_remote_copy(
        src_ref=before.at[at] if len(before.shape) == 2 else before.at[:, at],
        dst_ref=target,
        send_sem=sends.at[c, lane_sem],
        recv_sem=receives.at[c, lane_sem],
        device_id=(me ^ bit,),
        device_id_type=MESH,
    )


def fill_tail(tail, towers, gates, small):
    tasks, tower, hidden = towers.shape
    count = gates.shape[1]
    size = small.shape[1]
    tail[...] = jnp.zeros_like(tail)
    tail[0 : tasks * tower, :] = towers[...].reshape(tasks * tower, hidden)
    for part in range(2):
        for k in range(tasks):
            at = tasks * tower + part * GAP + k * count
            tail[at : at + count, :] = gates[k][:, part * hidden : (part + 1) * hidden]
    at = tasks * tower + 2 * GAP
    for i in range(-(-size // hidden)):
        last = min(size, (i + 1) * hidden)
        tail[at + i : at + i + 1, 0 : last - i * hidden] = small[0:1, i * hidden : last]


def owner_side(me, n, items_ref, experts, tasks, tower):
    def chosen(chain, i, count):
        array, first, order, _ = chain
        bit = order[i]
        if array < experts:
            return bit_of(items_ref[array], bit) == bit_of(me, bit)
        towers = tasks * tower
        row = first + start_of(me, order[: i + 1], 8 * n) + iota((count, LANES), 0)
        item = lax.div(row, tower) + experts + tasks
        for part in range(2):
            at = towers + part * GAP
            item = jnp.where((row >= at) & (row < at + tasks * experts), experts + lax.div(row - at, experts), item)
        item = jnp.where(row >= towers + 2 * GAP, experts + 2 * tasks, item)
        home = jnp.zeros((count, LANES), I32)
        for k in range(experts, experts + 2 * tasks + 1):
            home = jnp.where(item == k, items_ref[k], home)
        return (bit_of(home, bit) == bit_of(me, bit))[:, :1]

    return chosen


def forward_kernel(
    sizes,
    ids_ref, lengths_ref, counts_ref, mask_ref, labels_ref, homes_ref, table_ref, items_ref,
    experts_m_ref, experts_v_ref, towers_m_ref, towers_v_ref, gates_m_ref, gates_v_ref, small_m_ref, small_v_ref,
    fields_ref, pos_ref, mine_ref, theirs_ref, pairs_ref, stat_ref, lines_ref, moments_ref,
    outbox, inbox, message, replies, lists, field_scratch, owner_ref, rank_ref, local_ref, asked_smem, rows_ref, rows_out,
    tails, kept_ref, *rest,
):
    n, cap, tables, bag, tasks, experts, per_table, block_rows, rows_dev = sizes
    levels = early_levels(n)
    stages = list(rest[: levels - 1]) + [moments_ref]
    send_a, recv_a, send_b, recv_b, send_c, recv_c, send_m, recv_m, keep_sem, sems = rest[levels - 1 :]
    chains = plan(n, experts, experts_m_ref.shape[1], tails.shape[1])
    unit = 8 * n
    rows = tables * bag
    me = lax.axis_index("dev")
    shift = lax.rem(me * 13, n)
    per_pair = LANES // n
    greet_all(n, me)
    table_of = lax.div(iota((rows, LANES), 0), bag)
    slot_of = lax.rem(iota((rows, LANES), 0), bag)
    expand = jnp.where(lax.div(iota((rows, tables), 0), bag) == iota((rows, tables), 1), 1.0, 0.0).astype(BF16)
    used = dot(expand, lengths_ref[...].astype(F32).astype(BF16)).astype(I32)
    present = iota((1, LANES), 1) < counts_ref[0]
    live = present & (slot_of < used)
    field_scratch[0:rows, :] = jnp.where(live, ids_ref[...], -1).astype(F32)
    field_scratch[rows : rows + tasks, :] = labels_ref[...]
    field_scratch[rows + tasks : rows + tasks + 1, :] = jnp.where(present & (mask_ref[...] == 1), 1.0, 0.0)
    field_scratch[rows + tasks + 1 :, :] = jnp.zeros((LANES - rows - tasks - 1, LANES), F32)
    row = iota((n * 8, LANES), 0)
    peer_of, piece = lax.div(row, 8), lax.rem(row, 8)
    column = iota((n * 8, LANES), 1)
    pick = jnp.where((piece < per_pair) & (column == piece * n + lax.rem(peer_of - shift + n, n)), 1.0, 0.0).astype(BF16)
    high, middle, low = split3(field_scratch[...])
    spread = dot(pick, high, NT) + dot(pick, middle, NT) + dot(pick, low, NT)
    outbox[...] = spread.reshape(n, 8, LANES)
    await_all(n)
    own_copy = pltpu.make_async_copy(outbox.at[me], inbox.at[me], sems.at[0])
    own_copy.start()
    for_range(1, n, lambda k: exchange(n, me, outbox, inbox, send_a, recv_a, k).start())
    fill_tail(tails.at[0], towers_m_ref, gates_m_ref, small_m_ref)
    fill_tail(tails.at[1], towers_v_ref, gates_v_ref, small_v_ref)

    def whole(c, w):
        array, first, _, _ = chains[c]
        source = tails.at[w] if array == experts else (experts_m_ref, experts_v_ref)[w].at[array]
        return source.at[first : first + unit]

    def hop(c, i, lane=0):
        return halving(me, whole(c, lane) if i == 0 else None, stages, send_m, recv_m, c, chains[c][2], i, lane)

    def keep(c, w):
        at = rows_at(bit_of(me, 1) * (unit // 2), unit // 2)
        return pltpu.make_async_copy(whole(c, w).at[at], kept_ref.at[c, w], keep_sem.at[c, w])

    for c in range(len(chains)):
        for w in range(2):
            hop(c, 0, w).start()
            keep(c, w).start()

    chosen = owner_side(me, n, items_ref, experts, tasks, towers_m_ref.shape[1])

    def settle(c, i):
        order = chains[c][2]
        for w in range(2 if i == 0 else 1):
            hop(c, i, w).wait()
            if i == 0:
                keep(c, w).wait()
        half = stages[i].shape[2]
        mine = rows_at(bit_of(me, order[i]) * half, half)
        flag = chosen(chains[c], i, half)
        for w in range(2):
            kept = kept_ref[c, w] if i == 0 else stages[i - 1][c, w, mine, :]
            stages[i][c, w] = jnp.where(flag, kept, stages[i][c, w])
        if i + 1 < levels:
            hop(c, i + 1).start()

    events = [(c, j) for t in range(16) for c, chain in enumerate(chains) for j in (t - chain[3],) if 0 <= j < levels]
    done = [0]

    def settle_some(count):
        for c, j in events[done[0] : done[0] + count]:
            settle(c, j)
        done[0] += count

    homes = homes_ref[...]
    blocks = homes.shape[1]
    homes_rows = (
        dot(expand, (homes >> 5).astype(F32).astype(BF16)) * 32.0 + dot(expand, (homes & 31).astype(F32).astype(BF16))
    ).astype(I32)
    gather_back = jnp.where((piece < per_pair) & (column == peer_of * per_pair + piece), 1.0, 0.0).astype(BF16)
    before = jnp.where(iota((LANES, LANES), 0) < iota((LANES, LANES), 1), 1.0, 0.0).astype(BF16)
    ones = jnp.ones((LANES, LANES), BF16)
    r_out, r_in = iota((rows + 8, rows), 0), iota((rows + 8, rows), 1)
    parity_in = lax.rem(lax.div(r_in, bag), 2)
    earlier = (r_out < rows) & (r_in < r_out) & (parity_in == lax.rem(lax.div(r_out, bag), 2))
    totals = (r_out == rows + 2 + parity_in)
    above = jnp.where(earlier | totals, 1.0, 0.0).astype(BF16)
    for_range(1, n, lambda k: exchange(n, me, outbox, inbox, send_a, recv_a, k).wait())
    own_copy.wait()
    settle_some(4)
    arrived = inbox[...].reshape(n * 8, LANES).T
    high, middle, low = split3(arrived)
    fields = dot(high, gather_back) + dot(middle, gather_back) + dot(low, gather_back)
    fields_ref[...] = fields[rows : rows + 8]
    ids = fields[0:rows].astype(I32)
    weight_count = jnp.sum(fields[rows + tasks : rows + tasks + 1], axis=1, keepdims=True).astype(I32)
    live = ids >= 0
    ids = jnp.maximum(ids, 0)
    block = lax.div(ids, block_rows)
    lane = block & (LANES - 1)
    home = jnp.zeros((rows, LANES), I32)
    for part in range(blocks // LANES):
        found = jnp.take_along_axis(homes_rows[:, part * LANES : (part + 1) * LANES], lane, axis=1, mode="promise_in_bounds")
        home = jnp.where(lax.div(block, LANES) == part, found, home)
    owner = jnp.where(live, lax.div(home, per_table), n)
    local = (table_of * per_table + lax.rem(home, per_table)) * block_rows + lax.rem(ids, block_rows)
    owner_ref[...] = owner
    local_ref[...] = local

    def rank_step(o, carry):
        rank, most = carry
        is_mine = owner == o
        flags = jnp.where(is_mine, 1.0, 0.0).astype(BF16)
        row_totals = dot(flags, ones).astype(BF16)
        bases = dot(above, row_totals)
        count = bases[rows : rows + 8].astype(I32)
        message[o] = count
        rank = jnp.where(is_mine, (dot(flags, before) + bases[0:rows]).astype(I32), rank)
        return rank, jnp.maximum(most, count)

    rank, most = jnp.zeros((rows, LANES), I32), jnp.zeros((8, LANES), I32)
    for part in range(4):
        rank, most = lax.fori_loop(part * n // 4, (part + 1) * n // 4, rank_step, (rank, most), unroll=4)
        settle_some(1)
    rank_ref[...] = rank
    most = jnp.max(most, axis=0, keepdims=True)
    pos_ref[...] = jnp.where(live, jnp.where(rank < cap, owner * cap + rank, n * cap + 1), n * cap)
    lists[...] = jnp.zeros_like(lists)
    device_row = iota((n, LANES), 0)
    rank_row = iota((LANES, LANES), 0)
    lane_value = (iota((n, LANES), 1)).astype(F32)

    def list_step(q, carry):
        for parity in range(2):
            picks, places = [], []
            for j in range(bag):
                r = (2 * q + parity) * bag + j
                owner_row = owner_ref[pl.ds(r, 1), :]
                local_row = local_ref[pl.ds(r, 1), :]
                hit = device_row == owner_row
                picks.append(
                    jnp.concatenate(
                        [
                            jnp.where(hit, ((local_row >> 7) + 1).astype(F32), 0.0),
                            jnp.where(hit, (local_row & 127).astype(F32), 0.0),
                            jnp.where(hit, (q + 1).astype(F32), 0.0),
                            jnp.where(hit, lane_value, 0.0),
                        ],
                        axis=0,
                    ).astype(BF16)
                )
                places.append(jnp.where(rank_row == rank_ref[pl.ds(r, 1), :], 1.0, 0.0).astype(BF16))
            lists[parity] += dot(jnp.concatenate(picks, axis=1), jnp.concatenate(places, axis=1), NT)
        return carry

    for part in range(2):
        lax.fori_loop(part * tables // 4, (part + 1) * tables // 4, list_step, 0)
        settle_some(1)
    sub = iota((8, LANES), 0)
    is_last = iota((1, LANES), 1) == LANES - 1

    def post(k):
        o = me ^ k
        tile = message[o]
        rows_list = []
        for parity in range(2):
            count = tile[2 + parity : 3 + parity]
            got = [lists[parity, pl.ds(part * n + o, 1), :].astype(I32) for part in range(4)]
            asked = jnp.where(got[0] > 0, (got[0] - 1) * LANES + got[1], rows_dev)
            slot = jnp.where(got[0] > 0, (got[2] - 1) * LANES + got[3], tables // 2 * LANES)
            rows_list.append(jnp.where(is_last, count, asked))
            mine_ref[o, parity : parity + 1, :] = jnp.where(is_last, count, slot)
        tile = jnp.where(sub == 0, rows_list[0], jnp.where(sub == 1, rows_list[1], tile))
        message[o] = jnp.where(sub == 4, most, jnp.where(sub == 5, weight_count, tile))

    def post_and_send(k):
        post(k)
        exchange(n, me, message, replies, send_b, recv_b, k).start()

    for_range(1, n, post_and_send)
    post(0)
    own_copy = pltpu.make_async_copy(message.at[me], replies.at[me], sems.at[0])
    own_copy.start()
    settle_some(2)
    width = table_ref.shape[0]
    rows_ref[rows_dev:, :] = jnp.zeros((rows_ref.shape[0] - rows_dev, LANES), F32)

    def turn(b):
        at = pl.ds(pl.multiple_of(b * LANES, LANES), LANES)
        rows_ref[at, :] = jnp.concatenate([table_ref[:, at]] * (LANES // width), axis=0).T

    for part in range(4):
        for_range(part * (rows_dev // LANES // 4), (part + 1) * (rows_dev // LANES // 4), turn)
        settle_some(2)
    for_range(1, n, lambda k: exchange(n, me, message, replies, send_b, recv_b, k).wait())
    own_copy.wait()

    def take(s, carry):
        most, total = carry
        tile = replies[s]
        asked = jnp.clip(tile[0:2], 0, rows_dev)
        theirs_ref[s] = asked
        table_rows = per_table * block_rows
        paired = lax.div(asked, 2 * table_rows) * table_rows + lax.rem(asked, table_rows)
        pairs_ref[s] = jnp.where(is_last, asked, paired)
        return jnp.maximum(most, tile), total + tile

    most, total = lax.fori_loop(0, n, take, (jnp.zeros((8, LANES), I32), jnp.zeros((8, LANES), I32)))
    stat_ref[...] = jnp.where(sub == 4, most, total)
    to_scalars = pltpu.make_async_copy(theirs_ref, asked_smem, sems.at[0])
    to_scalars.start()
    to_scalars.wait()
    lines_ref[n] = jnp.zeros((cap, LANES), F32)
    collect = collector(cap, asked_smem, rows_ref)

    def collect_and_send(i):
        k = n - i
        collect(me ^ k, rows_out, me ^ k)
        exchange(n, me, rows_out, lines_ref, send_c, recv_c, k).start()

    for part in range(8):
        for_range(part * n // 8 + (part == 0), (part + 1) * n // 8, collect_and_send)
        settle_some(3)
    collect(me, lines_ref, me)
    settle_some(len(events) - done[0])
    for_range(1, n, lambda k: exchange(n, me, rows_out, lines_ref, send_c, recv_c, k).wait())


def collector(cap, lists_ref, rows_ref):
    left = iota((1, LANES), 1) < LANES // 2

    def collect(peer, target, slot):
        def lines(g):
            for i in range(8):
                r = g * 8 + i
                even = rows_ref[pl.ds(lists_ref[peer, 0, r], 1), :]
                odd = rows_ref[pl.ds(lists_ref[peer, 1, r], 1), :]
                target[slot, pl.ds(r, 1), :] = jnp.where(left, even, odd)

        for_range(0, cap // 8, lines)

    return collect


def forward(
    n, cap, tail_rows, row_ids, lengths, counts, mask, labels, row_home, table, mat_home,
    experts_m, experts_v, towers_m, towers_v, gates_m, gates_v, small_m, small_v,
):
    samples, tables, bag = row_ids.shape
    rows_dev, width = table.shape
    tasks = labels.shape[1]
    experts, features, hidden = experts_m.shape
    per_table = row_home.shape[1] // n
    block_rows = rows_dev // (tables * per_table)
    levels = early_levels(n)
    sizes = (n, cap, tables, bag, tasks, experts, per_table, block_rows, rows_dev)
    ids = row_ids.transpose(1, 2, 0).reshape(tables * bag, samples)
    vmem = pl.BlockSpec(memory_space=pltpu.VMEM)
    smem = pl.BlockSpec(memory_space=pltpu.SMEM)
    hbm = pl.BlockSpec(memory_space=pl.ANY)
    slots = jax.ShapeDtypeStruct((tables * bag, LANES), I32)
    lists = jax.ShapeDtypeStruct((n, 2, LANES), I32)
    count = len(plan(n, experts, features, tail_rows))
    small = pltpu.VMEM((n, 8, LANES), F32)
    numbers = pltpu.VMEM((n, 8, LANES), I32)
    slot_scratch = pltpu.VMEM((tables * bag, LANES), I32)
    dma = pltpu.SemaphoreType.DMA((n,))
    hops = pltpu.SemaphoreType.DMA((count, n.bit_length()))
    return pl.pallas_call(
        functools.partial(forward_kernel, sizes),
        out_shape=(
            jax.ShapeDtypeStruct((8, LANES), F32), slots, lists, lists, lists,
            jax.ShapeDtypeStruct((8, LANES), I32), jax.ShapeDtypeStruct((n + 1, cap, LANES), F32),
            jax.ShapeDtypeStruct((count, 2, 8 * n >> levels, hidden), F32),
        ),
        in_specs=[vmem, vmem, smem, vmem, vmem, vmem, vmem, smem, hbm, hbm] + [vmem] * 6,
        out_specs=(vmem,) * 8,
        scratch_shapes=[
            small, small, numbers, numbers,
            pltpu.VMEM((2, 4 * n, LANES), F32), pltpu.VMEM((LANES, LANES), F32),
            slot_scratch, slot_scratch, slot_scratch,
            pltpu.SMEM((n, 2, LANES), I32), pltpu.VMEM((rows_dev + 8, LANES), F32), pltpu.VMEM((n, cap, LANES), F32),
            pltpu.VMEM((2, tail_rows, hidden), F32), pltpu.VMEM((count, 2, 4 * n, hidden), F32),
        ]
        + [pltpu.VMEM((count, 2, 4 * n >> i, hidden), F32) for i in range(levels - 1)]
        + [dma] * 6 + [hops] * 2 + [pltpu.SemaphoreType.DMA((count, 2)), pltpu.SemaphoreType.DMA((2,))],
        compiler_params=pltpu.CompilerParams(collective_id=0, has_side_effects=True, vmem_limit_bytes=56 * 2**20),
        name="forward",
    )(
        ids, lengths.T, counts, mask.reshape(1, samples), labels.T, row_home, table.T, mat_home, experts_m, experts_v,
        towers_m.transpose(0, 2, 1), towers_v.transpose(0, 2, 1), gates_m.transpose(0, 2, 1), gates_v.transpose(0, 2, 1),
        small_m, small_v,
    )


def backward_kernel(
    sizes, lists_ref, stat_ref, items_ref, fields_ref, pooled_ref, moments_ref, experts_ref, gates_ref, towers_ref, small_ref,
    lines_ref, experts_out, tail_out, *rest,
):
    n, cap, tail_rows = sizes
    levels, early = n.bit_length() - 1, early_levels(n)
    stages, rest = list(rest[:levels]), rest[levels:]
    late_stages, rest = [moments_ref] + list(rest[: levels - early]), rest[levels - early :]
    grads, tail, tail_w, news, rows_ref, side, rows_out = rest[:7]
    send_c, recv_c, sends, receives, send_m, recv_m, send_w, recv_w, local = rest[7:]
    experts, features, hidden = experts_ref.shape
    tasks, tower, _ = towers_ref.shape
    chains = plan(n, experts, features, tail_rows)
    unit = 8 * n
    me = lax.axis_index("dev")
    greet_all(n, me)
    await_all(n)

    def late_hop(c, i):
        order = chains[c][2]
        bit = order[early + i]
        half = late_stages[i + 1].shape[2]
        at = rows_at((1 - bit_of(me, bit)) * half, half)
        return pltpu.make_async_remote_copy(
            src_ref=late_stages[i].at[c, :, at],
            dst_ref=late_stages[i + 1].at[c],
            send_sem=send_m.at[c, i],
            recv_sem=recv_m.at[c, i],
            device_id=(me ^ bit,),
            device_id_type=MESH,
        )

    chosen = owner_side(me, n, items_ref, experts, tasks, tower)

    def late_settle(i):
        for c, chain in enumerate(chains):
            late_hop(c, i).wait()
            half = late_stages[i + 1].shape[2]
            mine = rows_at(bit_of(me, chain[2][early + i]) * half, half)
            flag = chosen(chain, early + i, half)
            for w in range(2):
                late_stages[i + 1][c, w] = jnp.where(flag, late_stages[i][c, w, mine, :], late_stages[i + 1][c, w])
            if i + 1 < levels - early:
                late_hop(c, i + 1).start()

    for c in range(len(chains)):
        late_hop(c, 0).start()
    lines_ref[n] = jnp.zeros((cap, LANES), F32)
    fill_tail(tail_w, towers_ref, gates_ref, small_ref)

    def hop(c, i):
        array, first, order, _ = chains[c]
        source = tail if array == experts else grads.at[array]
        return halving(me, source.at[first : first + unit], stages, sends, receives, c, order, i)

    def settle(c, i):
        array, first, order, _ = chains[c]
        hop(c, i).wait()
        half = stages[i].shape[1]
        at = bit_of(me, order[i]) * half
        if i > 0:
            kept = stages[i - 1][c, rows_at(at, half), :]
        elif array == experts:
            kept = tail[rows_at(first + at, half), :]
        else:
            kept = grads[array, rows_at(first + at, half), :]
        stages[i][c] += kept
        if i + 1 < levels:
            hop(c, i + 1).start()

    def region(c, i):
        array, first, order, _ = chains[c]
        at = rows_at(first + start_of(me, order[: i + 1], unit), unit >> (i + 1))
        return tail_out.at[:, at] if array == experts else experts_out.at[array, :, at]

    def doubling(c, i):
        return pltpu.make_async_remote_copy(
            src_ref=news.at[c] if i == levels - 1 else region(c, i),
            dst_ref=region(c, i),
            send_sem=send_w.at[c, i],
            recv_sem=recv_w.at[c, i],
            device_id=(me ^ chains[c][2][i],),
            device_id_type=MESH,
        )

    def place(c):
        return pltpu.make_async_copy(news.at[c], region(c, levels - 1), local.at[c])

    def renew(c):
        array, first, order, _ = chains[c]
        at = rows_at(first + start_of(me, order, unit), 8)
        weight = tail_w[at, :] if array == experts else experts_ref[array, at, :]
        moment = late_stages[-1]
        grad = stages[-1][c]
        news[c, 0] = stepped(weight, *moments(moment[c, 0], moment[c, 1], grad))
        news[c, 1] = grad
        place(c).start()

    steps = len(set(chain[3] for chain in chains)) + 2 * levels

    def step(s):
        for c, chain in enumerate(chains):
            j = s - chain[3]
            if 0 <= j < levels:
                settle(c, j)
            if j == levels - 1:
                renew(c)
                doubling(c, levels - 1).start()
            i = 2 * levels - 2 - j
            if i == levels - 2:
                place(c).wait()
            if 0 <= i < levels - 1:
                doubling(c, i + 1).wait()
                doubling(c, i).start()
            if j == 2 * levels - 1:
                doubling(c, 0).wait()

    def ready(array):
        for c, chain in enumerate(chains):
            if chain[0] == array:
                hop(c, 0).start()
        if array == experts:
            late_settle(0)

    dense_pass(
        ready, stat_ref, fields_ref, pooled_ref, experts_ref, tail_w, towers_ref, small_ref, grads, tail, rows_ref, side
    )
    collect = collector(cap, lists_ref, rows_ref)

    def collect_and_send(i):
        k = n - i
        collect(me ^ k, rows_out, me ^ k)
        exchange(n, me, rows_out, lines_ref, send_c, recv_c, k).start()

    group = n // 8
    for s in range(1, 8):
        for_range((s - 1) * group + 1, s * group + 1, collect_and_send)
        if 3 <= s <= 1 + levels - early:
            late_settle(s - 2)
        step(s - 1)
    for_range(7 * group + 1, n, collect_and_send)
    collect(me, lines_ref, me)
    for s in range(7, steps):
        step(s)
    for_range(1, n, lambda k: exchange(n, me, rows_out, lines_ref, send_c, recv_c, k).wait())


def backward(n, cap, tail_rows, lists, stat, items, fields, pooled, moment_slices, experts_w, gates_w, towers_w, small):
    experts, features, hidden = experts_w.shape
    samples = fields.shape[1]
    levels, early = n.bit_length() - 1, early_levels(n)
    count = len(plan(n, experts, features, tail_rows))
    vmem = pl.BlockSpec(memory_space=pltpu.VMEM)
    smem = pl.BlockSpec(memory_space=pltpu.SMEM)
    dma = pltpu.SemaphoreType.DMA((n,))
    hops = pltpu.SemaphoreType.DMA((count, levels))
    return pl.pallas_call(
        functools.partial(backward_kernel, (n, cap, tail_rows)),
        out_shape=(
            jax.ShapeDtypeStruct((n + 1, cap, LANES), F32),
            jax.ShapeDtypeStruct((experts, 2, features, hidden), F32),
            jax.ShapeDtypeStruct((2, tail_rows, hidden), F32),
        ),
        in_specs=[smem, smem, smem] + [vmem] * 7,
        out_specs=(vmem, pl.BlockSpec(memory_space=pl.ANY), vmem),
        scratch_shapes=[pltpu.VMEM((count, 4 * n >> i, hidden), F32) for i in range(levels)]
        + [pltpu.VMEM((count, 2, 8 * n >> (early + i + 1), hidden), F32) for i in range(levels - early)]
        + [
            pltpu.VMEM((experts, features, hidden), F32), pltpu.VMEM((tail_rows, hidden), F32),
            pltpu.VMEM((tail_rows, hidden), F32), pltpu.VMEM((count, 2, 8, hidden), F32),
            pltpu.VMEM((features // LANES * samples + 8, LANES), F32), pltpu.VMEM((samples, samples), F32),
            pltpu.VMEM((n, cap, LANES), F32),
        ]
        + [dma] * 2 + [hops] * 6 + [pltpu.SemaphoreType.DMA((count,))],
        compiler_params=pltpu.CompilerParams(collective_id=1, has_side_effects=True, vmem_limit_bytes=56 * 2**20),
        name="backward",
    )(lists, stat, items, fields, pooled, moment_slices, experts_w, gates_w, towers_w, small)


def close_kernel(
    sizes,
    owned_ref, pairs_ref, lines_ref, table_ref, row_first_ref, row_second_ref,
    whole_ref, first_ref, second_ref, tail_ref, towers_m_ref, towers_v_ref, gates_m_ref, gates_v_ref, small_m_ref, small_v_ref,
    table_new_ref, row_first_new_ref, row_second_new_ref, new_ref, low_ref, first_new_ref, second_new_ref,
    towers_ref, towers_low_ref, towers_m_new_ref, towers_v_new_ref, gates_ref, gates_m_new_ref, gates_v_new_ref,
    small_ref, small_m_new_ref, small_v_new_ref, loss_ref,
    sums_even, sums_odd,
):
    n, cap, experts, first_steps, steps_each = sizes
    step = pl.program_id(0)
    width, block = table_ref.shape
    half = block // 2
    rows = sums_even.shape[0] - 8

    @pl.when(step == 0)
    def _():
        def clear(i):
            at = pl.ds(pl.multiple_of(i * half, half), half)
            sums_even[at, :] = jnp.zeros((half, LANES), F32)
            sums_odd[at, :] = jnp.zeros((half, LANES), F32)

        for_range(0, rows // half, clear)
        finish_tail(
            owned_ref, experts, tail_ref, towers_m_ref, towers_v_ref, gates_m_ref, gates_v_ref, small_m_ref, small_v_ref,
            towers_ref, towers_low_ref, towers_m_new_ref, towers_v_new_ref, gates_ref, gates_m_new_ref, gates_v_new_ref,
            small_ref, small_m_new_ref, small_v_new_ref, loss_ref,
        )

    @pl.when(step < first_steps)
    def _():
        e = lax.div(step, steps_each)
        new = whole_ref[0, 0]
        new_ref[0] = new
        low_ref[0] = new.astype(BF16)

        @pl.when(owned_ref[e] == 1)
        def _():
            first_new_ref[0], second_new_ref[0] = moments(first_ref[0], second_ref[0], whole_ref[0, 1])

        @pl.when(owned_ref[e] != 1)
        def _():
            first_new_ref[...] = jnp.zeros_like(first_new_ref)
            second_new_ref[...] = jnp.zeros_like(second_new_ref)

        def source(s):
            count = jnp.minimum(jnp.maximum(pairs_ref[s, 0, LANES - 1], pairs_ref[s, 1, LANES - 1]), cap)

            def add(g):
                for i in range(8):
                    r = g * 8 + i
                    line = lines_ref[pl.ds(s * cap + r, 1), :]
                    sums_even[pl.ds(pairs_ref[s, 0, r], 1), :] += line
                    sums_odd[pl.ds(pairs_ref[s, 1, r], 1), :] += line

            for_range(0, (count + 7) // 8, add)

        for_range(step * n // first_steps, (step + 1) * n // first_steps, source)

    @pl.when(step >= first_steps)
    def _():
        left = iota((LANES, LANES), 1) < width
        for b in range(half // LANES):
            at = pl.ds(pl.multiple_of((step - first_steps) * half + b * LANES, LANES), LANES)
            both = jnp.where(left, sums_even[at, :], sums_odd[at, :]).T
            for parity in range(2):
                here = slice(parity * half + b * LANES, parity * half + (b + 1) * LANES)
                grad = both[parity * width : (parity + 1) * width]
                first = BETA_ONE * row_first_ref[:, here] + (1.0 - BETA_ONE) * grad
                mean = jnp.sum(grad * grad, axis=0, keepdims=True) * (1.0 / width)
                second = BETA_TWO * row_second_ref[:, here] + (1.0 - BETA_TWO) * mean
                rate = (RATE_ROWS / (1.0 - BETA_ONE**STEP)) / (
                    jnp.sqrt(second * (1.0 / (1.0 - BETA_TWO**STEP))) + EPSILON
                )
                old = table_ref[:, here]
                table_new_ref[:, here] = old - (first * rate + (RATE_ROWS * DECAY) * old)
                row_first_new_ref[:, here] = first
                row_second_new_ref[:, here] = second


def finish_tail(
    owned_ref, experts, tail_ref, towers_m_ref, towers_v_ref, gates_m_ref, gates_v_ref, small_m_ref, small_v_ref,
    towers_ref, towers_low_ref, towers_m_new_ref, towers_v_new_ref, gates_ref, gates_m_new_ref, gates_v_new_ref,
    small_ref, small_m_new_ref, small_v_new_ref, loss_ref,
):
    tasks, tower, hidden = towers_ref.shape
    count = gates_ref.shape[1]

    def mine(item, pair):
        own = jnp.full((1, 1), owned_ref[item], I32) == 1
        return [jnp.where(own, x, 0.0) for x in pair]

    for k in range(tasks):
        at = slice(k * tower, (k + 1) * tower)
        towers_ref[k] = tail_ref[0, at]
        towers_low_ref[k] = tail_ref[0, at].astype(BF16)
        towers_m_new_ref[k], towers_v_new_ref[k] = mine(
            experts + tasks + k, moments(towers_m_ref[k], towers_v_ref[k], tail_ref[1, at])
        )
        for part in range(2):
            row = tasks * tower + part * GAP + k * count
            at = slice(row, row + count)
            to = slice(part * hidden, (part + 1) * hidden)
            gates_ref[k, :, to] = tail_ref[0, at]
            gates_m_new_ref[k, :, to], gates_v_new_ref[k, :, to] = mine(
                experts + k, moments(gates_m_ref[k, :, to], gates_v_ref[k, :, to], tail_ref[1, at])
            )
    base = tasks * tower + 2 * GAP
    size = small_ref.shape[1]
    for i in range(-(-size // hidden)):
        last = min(size, (i + 1) * hidden)
        to = slice(i * hidden, last)
        line = slice(0, last - i * hidden)
        small_ref[0:1, to] = tail_ref[0, base + i : base + i + 1, line]
        small_m_new_ref[0:1, to], small_v_new_ref[0:1, to] = mine(
            experts + 2 * tasks,
            moments(small_m_ref[0:1, to], small_v_ref[0:1, to], tail_ref[1, base + i : base + i + 1, line]),
        )
    loss_ref[...] = tail_ref[1, base + 8 : base + 9, 0:LANES]


def close(
    n, cap, table_rows, pairs, lines, table, table_m, table_v,
    owned, whole, tail, experts_m, experts_v, towers_m, towers_v, gates_m, gates_v, small_m, small_v,
):
    rows_dev, width = table.shape
    experts, features, hidden = experts_m.shape
    block = 2 * table_rows
    rows = 256
    steps_each = features // rows
    first_steps = experts * steps_each
    update_steps = rows_dev // block

    def late(i, *_):
        return (0, jnp.maximum(i - first_steps, 0))

    def place(i):
        i = jnp.minimum(i, first_steps - 1)
        return lax.div(i, steps_each), lax.rem(i, steps_each)

    def here(i, owned):
        e, b = place(i)
        return e, b, 0

    def only_owner(i, owned):
        e, b = place(i)
        return e, jnp.where(owned[e] == 1, b, 0), 0

    def both(i, owned):
        e, b = place(i)
        return e, 0, b, 0

    wide, thin = pl.BlockSpec((width, block), late), pl.BlockSpec((1, block), late)
    out_block, owners = pl.BlockSpec((1, rows, hidden), here), pl.BlockSpec((1, rows, hidden), only_owner)

    def full(x):
        return pl.BlockSpec(x.shape, lambda i, owned: (0,) * len(x.shape))

    sums = pltpu.VMEM((rows_dev // 2 + 8, LANES), F32)
    lines = lines.reshape((n + 1) * cap, LANES)
    towers = jax.ShapeDtypeStruct(towers_m.shape, F32)
    gates = jax.ShapeDtypeStruct(gates_m.shape, F32)
    small = jax.ShapeDtypeStruct(small_m.shape, F32)
    tail_shapes = (
        towers, jax.ShapeDtypeStruct(towers_m.shape, BF16), towers, towers, gates, gates, gates, small, small, small,
        jax.ShapeDtypeStruct((1, LANES), F32),
    )
    dense_shape = jax.ShapeDtypeStruct(experts_m.shape, F32)
    rows_shape = jax.ShapeDtypeStruct((width, rows_dev), F32)
    out_shape = (
        rows_shape, rows_shape, jax.ShapeDtypeStruct((1, rows_dev), F32),
        dense_shape, jax.ShapeDtypeStruct(experts_m.shape, BF16), dense_shape, dense_shape,
    ) + tail_shapes
    table_new, first_new, second_new, *others = pl.pallas_call(
        functools.partial(close_kernel, (n, cap, experts, first_steps, steps_each)),
        grid_spec=pltpu.PrefetchScalarGridSpec(
            num_scalar_prefetch=1,
            grid=(first_steps + update_steps,),
            in_specs=[
                pl.BlockSpec(memory_space=pltpu.SMEM), full(lines), wide, wide, thin,
                pl.BlockSpec((1, 2, rows, hidden), both), owners, owners,
                full(tail), full(towers_m), full(towers_v), full(gates_m), full(gates_v), full(small_m), full(small_v),
            ],
            out_specs=[wide, wide, thin] + [out_block] * 4 + [full(x) for x in tail_shapes],
            scratch_shapes=[sums, sums],
        ),
        out_shape=out_shape,
        compiler_params=pltpu.CompilerParams(vmem_limit_bytes=58 * 2**20),
        name="close",
    )(
        owned, pairs, lines, table.T, table_m.T, table_v.reshape(1, rows_dev),
        whole, experts_m, experts_v, tail, towers_m, towers_v, gates_m, gates_v, small_m, small_v,
    )
    return (table_new.T, first_new.T, second_new.reshape(rows_dev)), others


def pool_kernel(nothing, tables, bag, pos_ref, lines_ref, pooled_ref):
    samples = pos_ref.shape[1]
    pooled_ref[...] = jnp.zeros_like(pooled_ref)
    left = iota((1, LANES), 1) < LANES // 2

    def sample(s):
        @pl.when(pos_ref[0, s] != nothing)
        def _():
            for q in range(tables // 2):
                sums = []
                for parity in range(2):
                    base = (2 * q + parity) * bag
                    total = lines_ref[pl.ds(pos_ref[base, s], 1), :]
                    for j in range(1, bag):
                        total = total + lines_ref[pl.ds(pos_ref[base + j, s], 1), :]
                    sums.append(total)
                pooled_ref[pl.ds(q * samples + s, 1), :] = jnp.where(left, sums[0], sums[1])

    for_range(0, samples, sample)


def pool(n, cap, tables, bag, pos, lines):
    samples = pos.shape[1]
    return pl.pallas_call(
        functools.partial(pool_kernel, n * cap, tables, bag),
        out_shape=jax.ShapeDtypeStruct((tables // 2 * samples, LANES), F32),
        in_specs=[pl.BlockSpec(memory_space=pltpu.SMEM), pl.BlockSpec(memory_space=pltpu.VMEM)],
        out_specs=pl.BlockSpec(memory_space=pltpu.VMEM),
        compiler_params=pltpu.CompilerParams(vmem_limit_bytes=24 * 2**20),
        name="pool",
    )(pos, lines.reshape((n + 1) * cap, LANES))


def split2(x):
    high = x.astype(BF16)
    return high, (x - high.astype(F32)).astype(BF16)


def dot3(a, b, dims=NN):
    return dot(a[0], b[0], dims) + dot(a[0], b[1], dims) + dot(a[1], b[0], dims)


def sigmoid(x):
    return 1.0 / (1.0 + jnp.exp(-x))


def dense_pass(
    ready, stat_ref, fields_ref, pooled_ref, experts_ref, tail_w, towers_ref, small_ref, grads, tail, rows_ref, side
):
    samples = fields_ref.shape[1]
    experts, features, hidden = experts_ref.shape
    tasks, tower, _ = towers_ref.shape
    tail[...] = jnp.zeros_like(tail)

    def put_tail(row, value):
        tail[row : row + value.shape[0], :] = value

    start = experts * hidden
    tower_at = start
    weight_at = start + tasks * tower
    bias_at = weight_at + tasks * tower
    side[0:8, :] = fields_ref[...]
    side[8:, :] = jnp.zeros((samples - 8, samples), F32)
    by_sample = side[...].T
    weight = by_sample[:, tasks : tasks + 1]
    scale = weight / stat_ref[0].astype(F32)
    x = jnp.concatenate([pooled_ref[q * samples : (q + 1) * samples] for q in range(features // LANES)], axis=1)
    x2 = split2(x)
    at = tasks * tower
    gate_w = jnp.concatenate([tail_w[at + k * GAP : at + k * GAP + tasks * experts, :] for k in range(2)], axis=1)
    gate_w2 = split2(gate_w)
    gate_logits = dot3(x2, gate_w2, NT)
    pres, sigs, hids = [], [], []
    for e in range(experts):
        pre = dot3(x2, split2(experts_ref[e])) + small_ref[0:1, e * hidden : (e + 1) * hidden]
        sig = sigmoid(pre)
        pres.append(pre)
        sigs.append(sig)
        hids.append(pre * sig)
    dhids = [jnp.zeros((samples, hidden), F32) for _ in range(experts)]
    dgate_logits = []
    loss = jnp.zeros((samples, 1), F32)
    tower_bias_grads, out_weight_grads, task_bias_grads = [], [], []
    for k in range(tasks):
        logits = [gate_logits[:, k * experts + e : k * experts + e + 1] for e in range(experts)]
        top = functools.reduce(jnp.maximum, logits)
        powers = [jnp.exp(v - top) for v in logits]
        whole = functools.reduce(jnp.add, powers)
        gates = [v / whole for v in powers]
        mix = functools.reduce(jnp.add, [gates[e] * hids[e] for e in range(experts)])
        mix2 = split2(mix)
        tower2 = split2(towers_ref[k])
        at = tower_at + k * tower
        pre = dot3(mix2, tower2, NT) + small_ref[0:1, at : at + tower]
        sig = sigmoid(pre)
        zed = pre * sig
        at = weight_at + k * tower
        out_weight = small_ref[0:1, at : at + tower]
        logit = jnp.sum(zed * out_weight, axis=1, keepdims=True) + small_ref[0:1, bias_at + k : bias_at + k + 1]
        label = by_sample[:, k : k + 1]
        softplus = jnp.maximum(logit, 0.0) + jnp.log1p(jnp.exp(-jnp.abs(logit)))
        loss = loss + weight * (softplus - label * logit)
        dlogit = scale * (sigmoid(logit) - label)
        task_bias_grads.append(jnp.sum(dlogit, axis=0, keepdims=True))
        out_weight_grads.append(jnp.sum(dlogit * zed, axis=0, keepdims=True))
        dpre = dlogit * out_weight * (sig * (1.0 + pre * (1.0 - sig)))
        tower_bias_grads.append(jnp.sum(dpre, axis=0, keepdims=True))
        dpre2 = split2(dpre)
        put_tail(k * tower, dot3(split2(dpre.T), mix2))
        dmix = dot3(dpre2, tower2)
        dgates = [jnp.sum(dmix * hids[e], axis=1, keepdims=True) for e in range(experts)]
        mean = functools.reduce(jnp.add, [gates[e] * dgates[e] for e in range(experts)])
        for e in range(experts):
            dgate_logits.append(gates[e] * (dgates[e] - mean))
            dhids[e] = dhids[e] + gates[e] * dmix
    lane = iota((samples, LANES), 1)
    dgl = jnp.zeros((samples, LANES), F32)
    for i, v in enumerate(dgate_logits):
        dgl = jnp.where(lane == i, v, dgl)
    count = tasks * experts
    dgl_t2 = split2(dgl.T[0:16])
    dgates_w = dot3(dgl_t2, x2)
    tail_at = tasks * tower
    put_tail(tail_at, dgates_w[:, :hidden])
    put_tail(tail_at + GAP, dgates_w[:, hidden:])
    expert_bias_grads, dpres = [], []
    for e in range(experts):
        dpre = dhids[e] * (sigs[e] * (1.0 + pres[e] * (1.0 - sigs[e])))
        expert_bias_grads.append(jnp.sum(dpre, axis=0, keepdims=True))
        dpres.append(split2(dpre))
    small_at = tail_at + 2 * GAP
    pad = jnp.zeros((1, 2 * hidden - 2 * tasks * tower - tasks), F32)
    line = jnp.concatenate(tower_bias_grads + out_weight_grads + task_bias_grads + [pad], axis=1)
    loss_row = jnp.where(iota((1, hidden), 1) == 0, jnp.sum(loss, axis=0, keepdims=True), 0.0)
    for e in range(experts):
        put_tail(small_at + e, expert_bias_grads[e])
    for i in range(line.shape[1] // hidden):
        put_tail(small_at + experts + i, line[:, i * hidden : (i + 1) * hidden])
    put_tail(small_at + 8, loss_row)
    ready(experts)
    x_t2 = split2(x.T)
    for e in range(experts):
        grads[e] = dot3(x_t2, dpres[e])
        ready(e)
    dx = dot3(split2(dgl[:, :count]), gate_w2)
    for e in range(experts):
        dx = dx + dot3(dpres[e], split2(experts_ref[e]), NT)
    for q in range(features // LANES):
        rows_ref[q * samples : (q + 1) * samples, :] = dx[:, q * LANES : (q + 1) * LANES]
    rows_ref[features // LANES * samples :, :] = jnp.zeros((8, LANES), F32)


def moments(first, second, grad):
    return (
        BETA_ONE * first + (1.0 - BETA_ONE) * grad,
        BETA_TWO * second + (1.0 - BETA_TWO) * grad * grad,
    )


def stepped(weight, first_new, second_new):
    first_hat = first_new / (1.0 - BETA_ONE**STEP)
    second_hat = second_new / (1.0 - BETA_TWO**STEP)
    return weight - RATE_DENSE * (first_hat / (jnp.sqrt(second_hat) + EPSILON) + DECAY * weight)


def all_sum(tree, axis):
    n = lax.axis_size(axis)
    bit = 1
    while bit < n:
        pairs = [(i, i ^ bit) for i in range(n)]
        tree = jax.tree.map(lambda x: x + lax.ppermute(x, axis, pairs), tree)
        bit *= 2
    return tree


def from_root(block, axis, source):
    block = jnp.where(lax.axis_index(axis) == source, block, jnp.zeros_like(block))
    return all_sum(block, axis)


def dense_forward(params, pooled, labels, weights):
    experts_w, gates_w, towers_w, small = params
    n_experts, _, hidden = experts_w.shape
    tasks, _, tower = towers_w.shape
    start = n_experts * hidden
    expert_bias = small[:start].reshape(n_experts, hidden)
    tower_bias = small[start : start + tasks * tower].reshape(tasks, tower)
    start = start + tasks * tower
    out_weight = small[start : start + tasks * tower].reshape(tasks, tower)
    task_bias = small[start + tasks * tower :]
    hidden_act = jax.nn.silu(
        jnp.einsum("si,eih->seh", pooled, experts_w, precision=lax.Precision.HIGHEST) + expert_bias
    )
    gate = jax.nn.softmax(jnp.einsum("si,kie->ske", pooled, gates_w, precision=lax.Precision.HIGHEST), axis=-1)
    mixed = jnp.einsum("ske,seh->skh", gate, hidden_act, precision=lax.Precision.HIGHEST)
    zed = jax.nn.silu(jnp.einsum("skh,khc->skc", mixed, towers_w, precision=lax.Precision.HIGHEST) + tower_bias)
    logit = jnp.sum(zed * out_weight, axis=-1) + task_bias
    losses = jax.nn.softplus(logit) - labels * logit
    return jnp.sum(weights[:, None] * losses)


def adam_step(weight, first, second, grad, rate):
    first_new = BETA_ONE * first + (1.0 - BETA_ONE) * grad
    second_new = BETA_TWO * second + (1.0 - BETA_TWO) * grad * grad
    first_hat = first_new / (1.0 - BETA_ONE**STEP)
    second_hat = second_new / (1.0 - BETA_TWO**STEP)
    weight_new = weight - rate * (first_hat / (jnp.sqrt(second_hat) + EPSILON) + DECAY * weight)
    return (weight_new, first_new, second_new)


def plain_step(
    row_ids,
    lengths,
    counts,
    mask,
    labels,
    row_home,
    mat_home,
    table,
    table_m,
    table_v,
    experts_w,
    gates_w,
    towers_w,
    small_params,
    experts_m,
    experts_v,
    gates_m,
    gates_v,
    towers_m,
    towers_v,
    small_m,
    small_v,
):
    devices = lax.axis_size("dev")
    myself = lax.axis_index("dev")
    samples, tables, bag_slots = row_ids.shape
    rows_dev, width = table.shape
    per_table = row_home.shape[1] // devices
    block_rows = rows_dev // (tables * per_table)
    slots = samples * tables * bag_slots
    average = slots // devices
    capacity = average + average // 2
    present = jnp.arange(samples) < counts[0]
    weights = jnp.where(present & (mask == 1), 1.0, 0.0).astype(jnp.float32)
    live = present[:, None, None] & (jnp.arange(bag_slots)[None, None, :] < lengths[:, :, None])
    table_of = jnp.broadcast_to(jnp.arange(tables)[None, :, None], row_ids.shape)
    homes = row_home[table_of, row_ids // block_rows]
    owners = (homes // per_table).reshape(-1)
    local_rows = (
        (table_of * per_table + homes % per_table) * block_rows + row_ids % block_rows
    ).reshape(-1)
    live_flat = live.reshape(-1)
    live_float = live_flat.astype(jnp.float32)
    targets = jnp.where(live_flat, owners, devices)
    order = jnp.argsort(targets, stable=True)
    sorted_targets = targets[order]
    starts = jnp.searchsorted(sorted_targets, jnp.arange(devices + 1), side="left")
    sorted_rank = jnp.arange(slots, dtype=jnp.int32) - starts[sorted_targets]
    slot_rank = jnp.zeros(slots, jnp.int32).at[order].set(sorted_rank)
    slot_rank = jnp.where(live_flat, slot_rank, 0)
    requests = (
        jnp.zeros((devices, capacity), jnp.int32)
        .at[targets, slot_rank]
        .set(local_rows, mode="drop")
    )
    asked_rows = lax.all_to_all(requests, "dev", split_axis=0, concat_axis=0, tiled=True)
    found = table[asked_rows]
    arrived = lax.all_to_all(found, "dev", split_axis=0, concat_axis=0, tiled=True)
    safe_owner = jnp.minimum(owners, devices - 1)
    slot_rows = arrived[safe_owner, slot_rank] * live_float[:, None]
    pooled = jnp.sum(slot_rows.reshape(samples, tables, bag_slots, width), axis=2).reshape(
        samples, tables * width
    )
    params = (experts_w, gates_w, towers_w, small_params)
    local_loss, pull = jax.vjp(
        lambda dense, features: dense_forward(dense, features, labels, weights), params, pooled
    )
    loss_sum, weight_sum = all_sum((local_loss, jnp.sum(weights)), "dev")
    local_grads, pooled_grad = pull(1.0 / weight_sum)
    slot_grads = (
        jnp.broadcast_to(
            pooled_grad.reshape(samples, tables, 1, width), (samples, tables, bag_slots, width)
        ).reshape(slots, width)
        * live_float[:, None]
    )
    outgoing = (
        jnp.zeros((devices, capacity, width), jnp.float32)
        .at[targets, slot_rank]
        .set(slot_grads, mode="drop")
    )
    incoming = lax.all_to_all(outgoing, "dev", split_axis=0, concat_axis=0, tiled=True)
    grad_table = (
        jnp.zeros((rows_dev, width), jnp.float32)
        .at[asked_rows.reshape(-1)]
        .add(incoming.reshape(-1, width))
    )
    table_m_new = BETA_ONE * table_m + (1.0 - BETA_ONE) * grad_table
    table_v_new = BETA_TWO * table_v + (1.0 - BETA_TWO) * jnp.mean(grad_table * grad_table, axis=1)
    first_hat = table_m_new / (1.0 - BETA_ONE**STEP)
    second_hat = table_v_new / (1.0 - BETA_TWO**STEP)
    table_new = table - RATE_ROWS * (
        first_hat / (jnp.sqrt(second_hat)[:, None] + EPSILON) + DECAY * table
    )
    grad_experts, grad_gates, grad_towers, grad_small = local_grads
    grad_experts, grad_gates, grad_towers, grad_small = all_sum(
        (grad_experts, grad_gates, grad_towers, grad_small), "dev"
    )
    kinds = (
        (experts_w, experts_m[0], experts_v[0], grad_experts),
        (gates_w, gates_m[0], gates_v[0], grad_gates),
        (towers_w, towers_m[0], towers_v[0], grad_towers),
        (small_params[None], small_m, small_v, grad_small[None]),
    )
    finals = []
    first_outs = []
    second_outs = []
    base = 0
    for stack, firsts, seconds, grad in kinds:
        kind_weights = []
        kind_firsts = []
        kind_seconds = []
        for position in range(stack.shape[0]):
            owner_id = mat_home[base + position]
            is_owner = owner_id == myself
            weight_new, first_new, second_new = adam_step(
                stack[position], firsts[position], seconds[position], grad[position], RATE_DENSE
            )
            kind_firsts.append(jnp.where(is_owner, first_new, 0.0))
            kind_seconds.append(jnp.where(is_owner, second_new, 0.0))
            kept = jnp.where(is_owner, weight_new, stack[position])
            kind_weights.append(from_root(kept, "dev", owner_id))
        base = base + stack.shape[0]
        finals.append(jnp.stack(kind_weights))
        first_outs.append(jnp.stack(kind_firsts)[None])
        second_outs.append(jnp.stack(kind_seconds)[None])
    experts_new, gates_new, towers_new, small_stack = finals
    small_new = small_stack[0]
    return (
        loss_sum,
        weight_sum,
        table_new,
        table_m_new,
        table_v_new,
        experts_new,
        gates_new,
        towers_new,
        small_new,
        first_outs[0],
        second_outs[0],
        first_outs[1],
        second_outs[1],
        first_outs[2],
        second_outs[2],
        first_outs[3][0],
        second_outs[3][0],
        experts_new.astype(jnp.bfloat16)[None],
        gates_new.astype(jnp.bfloat16)[None],
        towers_new.astype(jnp.bfloat16)[None],
        small_new.astype(jnp.bfloat16)[None],
    )


def per_device(*args):
    (
        row_ids, lengths, counts, mask, labels, row_home, mat_home, table, table_m, table_v,
        experts_w, gates_w, towers_w, small_params,
        experts_m, experts_v, gates_m, gates_v, towers_m, towers_v, small_m, small_v,
    ) = args
    n = lax.axis_size("dev")
    me = lax.axis_index("dev")
    samples, tables, bag = row_ids.shape
    rows_dev, width = table.shape
    cap = max(8, (samples * tables * bag // n * 5 // 16 + 7) // 8 * 8)
    experts, features, hidden = experts_w.shape
    tasks, _, tower = towers_w.shape
    tail_rows = -(-(tasks * tower + 2 * GAP + 16) // (8 * n)) * 8 * n
    fields, pos, mine, theirs, pairs, stat, lines, moment_slices = forward(
        n, cap, tail_rows, row_ids, lengths, counts, mask, labels, row_home, table, mat_home,
        experts_m[0], experts_v[0], towers_m[0], towers_v[0], gates_m[0], gates_v[0], small_m, small_v,
    )
    most, weight_count = stat[4, 0], stat[5, 0]

    def usual(fields, pos, mine, pairs, lines, moment_slices, weight_count, *args):
        (
            _, _, _, _, _, _, mat_home, table, table_m, table_v, experts_w, gates_w, towers_w, small_params,
            experts_m, experts_v, gates_m, gates_v, towers_m, towers_v, small_m, small_v,
        ) = args

        def turned(x):
            return x.transpose(0, 2, 1)

        gates_t, towers_t, small = turned(gates_w), turned(towers_w), small_params.reshape(1, -1)
        pooled = pool(n, cap, tables, bag, pos, lines)
        back, whole, tail = backward(
            n, cap, tail_rows, mine, weight_count[None], mat_home, fields, pooled, moment_slices,
            experts_w, gates_t, towers_t, small,
        )
        rows_new, (
            experts_new, experts_low, experts_m_new, experts_v_new,
            towers_new, towers_low, towers_m_new, towers_v_new, gates_new, gates_m_new, gates_v_new,
            small_new, small_m_new, small_v_new, loss,
        ) = close(
            n, cap, rows_dev // tables, pairs, back, table, table_m, table_v,
            (mat_home == me).astype(I32), whole, tail, experts_m[0], experts_v[0], turned(towers_m[0]), turned(towers_v[0]),
            turned(gates_m[0]), turned(gates_v[0]), small_m, small_v,
        )
        gates_new = turned(gates_new)
        small_new = small_new.reshape(-1)
        return (
            loss[0, 0], weight_count.astype(F32), *rows_new, experts_new, gates_new, turned(towers_new), small_new,
            experts_m_new[None], experts_v_new[None], turned(gates_m_new)[None], turned(gates_v_new)[None],
            turned(towers_m_new)[None], turned(towers_v_new)[None], small_m_new, small_v_new,
            experts_low[None], gates_new.astype(BF16)[None], turned(towers_low)[None], small_new.astype(BF16)[None],
        )

    def crowded(fields, pos, mine, pairs, lines, moment_slices, weight_count, *args):
        return plain_step(*args)

    return lax.cond(
        most <= cap, usual, crowded, fields, pos, mine, pairs, lines, moment_slices, weight_count, *args
    )


def solution(mesh):
    def split(dims):
        return P("dev", *(None,) * (dims - 1))

    by_device = split(4)
    return jax.shard_map(
        per_device,
        mesh=mesh,
        in_specs=(
            split(3), split(2), split(1), split(1), split(2), P(), P(), split(2), split(2), split(1),
            P(), P(), P(), P(),
        ) + (by_device,) * 6 + (split(2),) * 2,
        out_specs=(P(), P(), split(2), split(2), split(1), P(), P(), P(), P())
        + (by_device,) * 6 + (split(2),) * 2 + (by_device,) * 3 + (split(2),),
        check_vma=False,
    )
```

```python
import functools
import jax
import jax.numpy as jnp
from jax import lax
from jax.experimental import pallas as pl
from jax.experimental.pallas import tpu as pltpu
from jax.sharding import PartitionSpec as P

MESH = pl.DeviceIdType.MESH
F32, BF16, I32 = jnp.float32, jnp.bfloat16, jnp.int32
NN, NT, TN = (((1,), (0,)), ((), ())), (((1,), (1,)), ((), ())), (((0,), (0,)), ((), ()))
LANES = 128


def iota(shape, dim):
    return lax.broadcasted_iota(I32, shape, dim)


def dot(a, b, dims=NN):
    return lax.dot_general(a, b, dims, preferred_element_type=F32)


def split3(x):
    high = x.astype(BF16)
    rest = x - high.astype(F32)
    middle = rest.astype(BF16)
    low = (rest - middle.astype(F32)).astype(BF16)
    return high, middle, low


def greet_all(n, me):
    barrier = pltpu.get_barrier_semaphore()

    def signal(k, carry):
        pl.semaphore_signal(barrier, inc=1, device_id=(me ^ k,), device_id_type=MESH)
        return carry

    lax.fori_loop(1, n, signal, 0)


def await_all(n):
    pl.semaphore_wait(pltpu.get_barrier_semaphore(), n - 1)


def exchange(n, me, source, target, sends, receives, k):
    peer = me ^ k
    return pltpu.make_async_remote_copy(
        src_ref=source.at[peer],
        dst_ref=target.at[me],
        send_sem=sends.at[k],
        recv_sem=receives.at[k],
        device_id=(peer,),
        device_id_type=MESH,
    )


def for_range(low, high, body):
    def step(k, carry):
        body(k)
        return carry

    lax.fori_loop(low, high, step, 0)

STEP = 5
BETA_ONE = 0.9
BETA_TWO = 0.999
EPSILON = 1e-08
DECAY = 0.01
RATE_DENSE = 0.02
RATE_ROWS = 0.3
GAP = 16

def axis_orders(n):
    bits = [1 << i for i in range(n.bit_length() - 1)]
    core, rest = bits[:1], bits[1:]
    a = len(rest) // 3
    b = (len(rest) - a) // 2
    x, y, z = rest[:a], rest[a : a + b], rest[a + b :]
    return core + x + y + z, core + y + x + z, core + z + x + y, core + z + y + x


def early_levels(n):
    rest = n.bit_length() - 2
    a = rest // 3
    return 1 + a + (rest - a) // 2


def bit_of(me, bit):
    return lax.rem(lax.div(me, bit), 2)


def start_of(me, order, rows):
    start = 0
    for bit in order:
        rows = rows // 2
        start = start + bit_of(me, bit) * rows
    return start


def rows_at(start, count):
    return pl.ds(pl.multiple_of(start, 8), count)


def plan(n, experts, features, tail_rows):
    unit = 8 * n
    along_x, along_y, along_z, along_w = axis_orders(n)
    chains = []
    for k in range(features // unit):
        for e in range(experts):
            chains.append((e, k * unit, along_y if e % 2 else along_x, k))
    for k in range(tail_rows // unit):
        chains.append((experts, k * unit, along_w if k % 2 else along_z, k // 2))
    return chains


def halving(me, source, stages, sends, receives, c, order, i, lane=0):
    bit = order[i]
    before = source if i == 0 else stages[i - 1].at[c]
    target = stages[i].at[c]
    half = stages[i].shape[-2]
    at = rows_at((1 - bit_of(me, bit)) * half, half)
    if i == 0 and len(stages[0].shape) == 4:
        target = target.at[lane]
        lane_sem = lane * len(order)
    else:
        lane_sem = i
    return pltpu.make_async_remote_copy(
        src_ref=before.at[at] if len(before.shape) == 2 else before.at[:, at],
        dst_ref=target,
        send_sem=sends.at[c, lane_sem],
        recv_sem=receives.at[c, lane_sem],
        device_id=(me ^ bit,),
        device_id_type=MESH,
    )


def fill_tail(tail, towers, gates, small):
    tasks, tower, hidden = towers.shape
    count = gates.shape[1]
    size = small.shape[1]
    tail[...] = jnp.zeros_like(tail)
    tail[0 : tasks * tower, :] = towers[...].reshape(tasks * tower, hidden)
    for part in range(2):
        for k in range(tasks):
            at = tasks * tower + part * GAP + k * count
            tail[at : at + count, :] = gates[k][:, part * hidden : (part + 1) * hidden]
    at = tasks * tower + 2 * GAP
    for i in range(-(-size // hidden)):
        last = min(size, (i + 1) * hidden)
        tail[at + i : at + i + 1, 0 : last - i * hidden] = small[0:1, i * hidden : last]


def owner_side(me, n, items_ref, experts, tasks, tower):
    def chosen(chain, i, count):
        array, first, order, _ = chain
        bit = order[i]
        if array < experts:
            return bit_of(items_ref[array], bit) == bit_of(me, bit)
        towers = tasks * tower
        row = first + start_of(me, order[: i + 1], 8 * n) + iota((count, LANES), 0)
        item = lax.div(row, tower) + experts + tasks
        for part in range(2):
            at = towers + part * GAP
            item = jnp.where((row >= at) & (row < at + tasks * experts), experts + lax.div(row - at, experts), item)
        item = jnp.where(row >= towers + 2 * GAP, experts + 2 * tasks, item)
        home = jnp.zeros((count, LANES), I32)
        for k in range(experts, experts + 2 * tasks + 1):
            home = jnp.where(item == k, items_ref[k], home)
        return (bit_of(home, bit) == bit_of(me, bit))[:, :1]

    return chosen


def forward_kernel(
    sizes,
    ids_ref, lengths_ref, counts_ref, mask_ref, labels_ref, homes_ref, table_hbm, items_ref,
    experts_m_ref, experts_v_ref, towers_m_ref, towers_v_ref, gates_m_ref, gates_v_ref, small_m_ref, small_v_ref,
    fields_ref, pos_ref, mine_ref, theirs_ref, pairs_ref, stat_ref, lines_ref, moments_ref,
    outbox, inbox, message, replies, lists, field_scratch, owner_ref, rank_ref, local_ref, asked_smem, rows_ref, rows_out,
    tails, kept_ref, table_ref, *rest,
):
    n, cap, tables, bag, tasks, experts, per_table, block_rows, rows_dev = sizes
    levels = early_levels(n)
    stages = list(rest[: levels - 1]) + [moments_ref]
    send_a, recv_a, send_b, recv_b, send_c, recv_c, send_m, recv_m, keep_sem, sems = rest[levels - 1 :]
    chains = plan(n, experts, experts_m_ref.shape[1], tails.shape[1])
    unit = 8 * n
    rows = tables * bag
    me = lax.axis_index("dev")
    shift = lax.rem(me * 13, n)
    per_pair = LANES // n
    greet_all(n, me)
    table_copy = pltpu.make_async_copy(table_hbm, table_ref, sems.at[1])
    table_copy.start()
    table_of = lax.div(iota((rows, LANES), 0), bag)
    slot_of = lax.rem(iota((rows, LANES), 0), bag)
    expand = jnp.where(lax.div(iota((rows, tables), 0), bag) == iota((rows, tables), 1), 1.0, 0.0).astype(BF16)
    used = dot(expand, lengths_ref[...].astype(F32).astype(BF16)).astype(I32)
    present = iota((1, LANES), 1) < counts_ref[0]
    live = present & (slot_of < used)
    field_scratch[0:rows, :] = jnp.where(live, ids_ref[...], -1).astype(F32)
    field_scratch[rows : rows + tasks, :] = labels_ref[...]
    field_scratch[rows + tasks : rows + tasks + 1, :] = jnp.where(present & (mask_ref[...] == 1), 1.0, 0.0)
    field_scratch[rows + tasks + 1 :, :] = jnp.zeros((LANES - rows - tasks - 1, LANES), F32)
    row = iota((n * 8, LANES), 0)
    peer_of, piece = lax.div(row, 8), lax.rem(row, 8)
    column = iota((n * 8, LANES), 1)
    pick = jnp.where((piece < per_pair) & (column == piece * n + lax.rem(peer_of - shift + n, n)), 1.0, 0.0).astype(BF16)
    high, middle, low = split3(field_scratch[...])
    spread = dot(pick, high, NT) + dot(pick, middle, NT) + dot(pick, low, NT)
    outbox[...] = spread.reshape(n, 8, LANES)
    await_all(n)
    own_copy = pltpu.make_async_copy(outbox.at[me], inbox.at[me], sems.at[0])
    own_copy.start()
    for_range(1, n, lambda k: exchange(n, me, outbox, inbox, send_a, recv_a, k).start())
    fill_tail(tails.at[0], towers_m_ref, gates_m_ref, small_m_ref)
    fill_tail(tails.at[1], towers_v_ref, gates_v_ref, small_v_ref)

    def whole(c, w):
        array, first, _, _ = chains[c]
        source = tails.at[w] if array == experts else (experts_m_ref, experts_v_ref)[w].at[array]
        return source.at[first : first + unit]

    def hop(c, i, lane=0):
        return halving(me, whole(c, lane) if i == 0 else None, stages, send_m, recv_m, c, chains[c][2], i, lane)

    def keep(c, w):
        at = rows_at(bit_of(me, 1) * (unit // 2), unit // 2)
        return pltpu.make_async_copy(whole(c, w).at[at], kept_ref.at[c, w], keep_sem.at[c, w])

    for c in range(len(chains)):
        for w in range(2):
            hop(c, 0, w).start()
            keep(c, w).start()

    chosen = owner_side(me, n, items_ref, experts, tasks, towers_m_ref.shape[1])

    def settle(c, i):
        order = chains[c][2]
        for w in range(2 if i == 0 else 1):
            hop(c, i, w).wait()
            if i == 0:
                keep(c, w).wait()
        half = stages[i].shape[2]
        mine = rows_at(bit_of(me, order[i]) * half, half)
        flag = chosen(chains[c], i, half)
        for w in range(2):
            kept = kept_ref[c, w] if i == 0 else stages[i - 1][c, w, mine, :]
            stages[i][c, w] = jnp.where(flag, kept, stages[i][c, w])
        if i + 1 < levels:
            hop(c, i + 1).start()

    events = [(c, j) for t in range(16) for c, chain in enumerate(chains) for j in (t - chain[3],) if 0 <= j < levels]
    done = [0]

    def settle_some(count):
        for c, j in events[done[0] : done[0] + count]:
            settle(c, j)
        done[0] += count

    homes = homes_ref[...]
    blocks = homes.shape[1]
    homes_rows = (
        dot(expand, (homes >> 5).astype(F32).astype(BF16)) * 32.0 + dot(expand, (homes & 31).astype(F32).astype(BF16))
    ).astype(I32)
    gather_back = jnp.where((piece < per_pair) & (column == peer_of * per_pair + piece), 1.0, 0.0).astype(BF16)
    before = jnp.where(iota((LANES, LANES), 0) < iota((LANES, LANES), 1), 1.0, 0.0).astype(BF16)
    ones = jnp.ones((LANES, LANES), BF16)
    r_out, r_in = iota((rows + 8, rows), 0), iota((rows + 8, rows), 1)
    parity_in = lax.rem(lax.div(r_in, bag), 2)
    earlier = (r_out < rows) & (r_in < r_out) & (parity_in == lax.rem(lax.div(r_out, bag), 2))
    totals = (r_out == rows + 2 + parity_in)
    above = jnp.where(earlier | totals, 1.0, 0.0).astype(BF16)
    for_range(1, n, lambda k: exchange(n, me, outbox, inbox, send_a, recv_a, k).wait())
    own_copy.wait()
    settle_some(4)
    arrived = inbox[...].reshape(n * 8, LANES).T
    high, middle, low = split3(arrived)
    fields = dot(high, gather_back) + dot(middle, gather_back) + dot(low, gather_back)
    fields_ref[...] = fields[rows : rows + 8]
    ids = fields[0:rows].astype(I32)
    weight_count = jnp.sum(fields[rows + tasks : rows + tasks + 1], axis=1, keepdims=True).astype(I32)
    live = ids >= 0
    ids = jnp.maximum(ids, 0)
    block = lax.div(ids, block_rows)
    lane = block & (LANES - 1)
    home = jnp.zeros((rows, LANES), I32)
    for part in range(blocks // LANES):
        found = jnp.take_along_axis(homes_rows[:, part * LANES : (part + 1) * LANES], lane, axis=1, mode="promise_in_bounds")
        home = jnp.where(lax.div(block, LANES) == part, found, home)
    owner = jnp.where(live, lax.div(home, per_table), n)
    local = (table_of * per_table + lax.rem(home, per_table)) * block_rows + lax.rem(ids, block_rows)
    owner_ref[...] = owner
    local_ref[...] = local

    def rank_step(o, carry):
        rank, most = carry
        is_mine = owner == o
        flags = jnp.where(is_mine, 1.0, 0.0).astype(BF16)
        row_totals = dot(flags, ones).astype(BF16)
        bases = dot(above, row_totals)
        count = bases[rows : rows + 8].astype(I32)
        message[o] = count
        rank = jnp.where(is_mine, (dot(flags, before) + bases[0:rows]).astype(I32), rank)
        return rank, jnp.maximum(most, count)

    rank, most = jnp.zeros((rows, LANES), I32), jnp.zeros((8, LANES), I32)
    for part in range(4):
        rank, most = lax.fori_loop(part * n // 4, (part + 1) * n // 4, rank_step, (rank, most), unroll=4)
        settle_some(2)
    rank_ref[...] = rank
    most = jnp.max(most, axis=0, keepdims=True)
    pos_ref[...] = jnp.where(live, jnp.where(rank < cap, owner * cap + rank, n * cap + 1), n * cap)
    lists[...] = jnp.zeros_like(lists)
    device_row = iota((n, LANES), 0)
    rank_row = iota((LANES, LANES), 0)
    lane_value = (iota((n, LANES), 1)).astype(F32)

    def list_step(q, carry):
        for parity in range(2):
            picks, places = [], []
            for j in range(bag):
                r = (2 * q + parity) * bag + j
                owner_row = owner_ref[pl.ds(r, 1), :]
                local_row = local_ref[pl.ds(r, 1), :]
                hit = device_row == owner_row
                picks.append(
                    jnp.concatenate(
                        [
                            jnp.where(hit, ((local_row >> 7) + 1).astype(F32), 0.0),
                            jnp.where(hit, (local_row & 127).astype(F32), 0.0),
                            jnp.where(hit, (q + 1).astype(F32), 0.0),
                            jnp.where(hit, lane_value, 0.0),
                        ],
                        axis=0,
                    ).astype(BF16)
                )
                places.append(jnp.where(rank_row == rank_ref[pl.ds(r, 1), :], 1.0, 0.0).astype(BF16))
            lists[parity] += dot(jnp.concatenate(picks, axis=1), jnp.concatenate(places, axis=1), NT)
        return carry

    for part in range(2):
        lax.fori_loop(part * tables // 4, (part + 1) * tables // 4, list_step, 0)
        settle_some(1)
    sub = iota((8, LANES), 0)
    is_last = iota((1, LANES), 1) == LANES - 1

    def post(k):
        o = me ^ k
        tile = message[o]
        rows_list = []
        for parity in range(2):
            count = tile[2 + parity : 3 + parity]
            got = [lists[parity, pl.ds(part * n + o, 1), :].astype(I32) for part in range(4)]
            asked = jnp.where(got[0] > 0, (got[0] - 1) * LANES + got[1], rows_dev)
            slot = jnp.where(got[0] > 0, (got[2] - 1) * LANES + got[3], tables // 2 * LANES)
            rows_list.append(jnp.where(is_last, count, asked))
            mine_ref[o, parity : parity + 1, :] = jnp.where(is_last, count, slot)
        tile = jnp.where(sub == 0, rows_list[0], jnp.where(sub == 1, rows_list[1], tile))
        message[o] = jnp.where(sub == 4, most, jnp.where(sub == 5, weight_count, tile))

    def post_and_send(k):
        post(k)
        exchange(n, me, message, replies, send_b, recv_b, k).start()

    for_range(1, n, post_and_send)
    post(0)
    own_copy = pltpu.make_async_copy(message.at[me], replies.at[me], sems.at[0])
    own_copy.start()
    settle_some(2)
    width = table_ref.shape[0]
    table_copy.wait()
    rows_ref[rows_dev:, :] = jnp.zeros((rows_ref.shape[0] - rows_dev, LANES), F32)

    def turn(b):
        at = pl.ds(pl.multiple_of(b * LANES, LANES), LANES)
        rows_ref[at, :] = jnp.concatenate([table_ref[:, at]] * (LANES // width), axis=0).T

    for part in range(4):
        for_range(part * (rows_dev // LANES // 4), (part + 1) * (rows_dev // LANES // 4), turn)
        settle_some(2)
    for_range(1, n, lambda k: exchange(n, me, message, replies, send_b, recv_b, k).wait())
    own_copy.wait()

    def take(s, carry):
        most, total = carry
        tile = replies[s]
        asked = jnp.clip(tile[0:2], 0, rows_dev)
        theirs_ref[s] = asked
        table_rows = per_table * block_rows
        paired = lax.div(asked, 2 * table_rows) * table_rows + lax.rem(asked, table_rows)
        pairs_ref[s] = jnp.where(is_last, asked, paired)
        return jnp.maximum(most, tile), total + tile

    most, total = lax.fori_loop(0, n, take, (jnp.zeros((8, LANES), I32), jnp.zeros((8, LANES), I32)))
    stat_ref[...] = jnp.where(sub == 4, most, total)
    to_scalars = pltpu.make_async_copy(theirs_ref, asked_smem, sems.at[0])
    to_scalars.start()
    to_scalars.wait()
    lines_ref[n] = jnp.zeros((cap, LANES), F32)
    collect = collector(cap, asked_smem, rows_ref)

    def collect_and_send(i):
        k = n - i
        collect(me ^ k, rows_out, me ^ k)
        exchange(n, me, rows_out, lines_ref, send_c, recv_c, k).start()

    for part in range(8):
        for_range(part * n // 8 + (part == 0), (part + 1) * n // 8, collect_and_send)
        settle_some(3 * (part >= 4))
    collect(me, lines_ref, me)
    settle_some(len(events) - done[0])
    for_range(1, n, lambda k: exchange(n, me, rows_out, lines_ref, send_c, recv_c, k).wait())


def collector(cap, lists_ref, rows_ref):
    left = iota((1, LANES), 1) < LANES // 2

    def collect(peer, target, slot):
        def lines(g):
            for i in range(8):
                r = g * 8 + i
                even = rows_ref[pl.ds(lists_ref[peer, 0, r], 1), :]
                odd = rows_ref[pl.ds(lists_ref[peer, 1, r], 1), :]
                target[slot, pl.ds(r, 1), :] = jnp.where(left, even, odd)

        for_range(0, cap // 8, lines)

    return collect


def forward(
    n, cap, tail_rows, row_ids, lengths, counts, mask, labels, row_home, table, mat_home,
    experts_m, experts_v, towers_m, towers_v, gates_m, gates_v, small_m, small_v,
):
    samples, tables, bag = row_ids.shape
    rows_dev, width = table.shape
    tasks = labels.shape[1]
    experts, features, hidden = experts_m.shape
    per_table = row_home.shape[1] // n
    block_rows = rows_dev // (tables * per_table)
    levels = early_levels(n)
    sizes = (n, cap, tables, bag, tasks, experts, per_table, block_rows, rows_dev)
    ids = row_ids.transpose(1, 2, 0).reshape(tables * bag, samples)
    vmem = pl.BlockSpec(memory_space=pltpu.VMEM)
    smem = pl.BlockSpec(memory_space=pltpu.SMEM)
    hbm = pl.BlockSpec(memory_space=pl.ANY)
    slots = jax.ShapeDtypeStruct((tables * bag, LANES), I32)
    lists = jax.ShapeDtypeStruct((n, 2, LANES), I32)
    count = len(plan(n, experts, features, tail_rows))
    small = pltpu.VMEM((n, 8, LANES), F32)
    numbers = pltpu.VMEM((n, 8, LANES), I32)
    slot_scratch = pltpu.VMEM((tables * bag, LANES), I32)
    dma = pltpu.SemaphoreType.DMA((n,))
    hops = pltpu.SemaphoreType.DMA((count, n.bit_length()))
    return pl.pallas_call(
        functools.partial(forward_kernel, sizes),
        out_shape=(
            jax.ShapeDtypeStruct((8, LANES), F32), slots, lists, lists, lists,
            jax.ShapeDtypeStruct((8, LANES), I32), jax.ShapeDtypeStruct((n + 1, cap, LANES), F32),
            jax.ShapeDtypeStruct((count, 2, 8 * n >> levels, hidden), F32),
        ),
        in_specs=[vmem, vmem, smem, vmem, vmem, vmem, hbm, smem, hbm, hbm] + [vmem] * 6,
        out_specs=(vmem,) * 8,
        scratch_shapes=[
            small, small, numbers, numbers,
            pltpu.VMEM((2, 4 * n, LANES), F32), pltpu.VMEM((LANES, LANES), F32),
            slot_scratch, slot_scratch, slot_scratch,
            pltpu.SMEM((n, 2, LANES), I32), pltpu.VMEM((rows_dev + 8, LANES), F32), pltpu.VMEM((n, cap, LANES), F32),
            pltpu.VMEM((2, tail_rows, hidden), F32), pltpu.VMEM((count, 2, 4 * n, hidden), F32),
            pltpu.VMEM((width, rows_dev), F32),
        ]
        + [pltpu.VMEM((count, 2, 4 * n >> i, hidden), F32) for i in range(levels - 1)]
        + [dma] * 6 + [hops] * 2 + [pltpu.SemaphoreType.DMA((count, 2)), pltpu.SemaphoreType.DMA((2,))],
        compiler_params=pltpu.CompilerParams(collective_id=0, has_side_effects=True, vmem_limit_bytes=56 * 2**20),
        name="forward",
    )(
        ids, lengths.T, counts, mask.reshape(1, samples), labels.T, row_home, table.T, mat_home, experts_m, experts_v,
        towers_m.transpose(0, 2, 1), towers_v.transpose(0, 2, 1), gates_m.transpose(0, 2, 1), gates_v.transpose(0, 2, 1),
        small_m, small_v,
    )


def backward_kernel(
    sizes, lists_ref, stat_ref, items_ref, fields_ref, pooled_ref, moments_ref, experts_hbm, gates_ref, towers_ref, small_ref,
    lines_ref, experts_out, tail_out, *rest,
):
    n, cap, tail_rows = sizes
    levels, early = n.bit_length() - 1, early_levels(n)
    stages, rest = list(rest[:levels]), rest[levels:]
    late_stages, rest = [moments_ref] + list(rest[: levels - early]), rest[levels - early :]
    grads, tail, tail_w, news, rows_ref, side, rows_out, experts_ref = rest[:8]
    send_c, recv_c, sends, receives, send_m, recv_m, send_w, recv_w, local = rest[8:]
    experts, features, hidden = experts_ref.shape
    tasks, tower, _ = towers_ref.shape
    chains = plan(n, experts, features, tail_rows)
    unit = 8 * n
    me = lax.axis_index("dev")
    greet_all(n, me)
    weights_copy = pltpu.make_async_copy(experts_hbm, experts_ref, local.at[0])
    weights_copy.start()
    await_all(n)

    def late_hop(c, i):
        order = chains[c][2]
        bit = order[early + i]
        half = late_stages[i + 1].shape[2]
        at = rows_at((1 - bit_of(me, bit)) * half, half)
        return pltpu.make_async_remote_copy(
            src_ref=late_stages[i].at[c, :, at],
            dst_ref=late_stages[i + 1].at[c],
            send_sem=send_m.at[c, i],
            recv_sem=recv_m.at[c, i],
            device_id=(me ^ bit,),
            device_id_type=MESH,
        )

    chosen = owner_side(me, n, items_ref, experts, tasks, tower)

    def late_settle(i):
        for c, chain in enumerate(chains):
            late_hop(c, i).wait()
            half = late_stages[i + 1].shape[2]
            mine = rows_at(bit_of(me, chain[2][early + i]) * half, half)
            flag = chosen(chain, early + i, half)
            for w in range(2):
                late_stages[i + 1][c, w] = jnp.where(flag, late_stages[i][c, w, mine, :], late_stages[i + 1][c, w])
            if i + 1 < levels - early:
                late_hop(c, i + 1).start()

    for c in range(len(chains)):
        late_hop(c, 0).start()
    lines_ref[n] = jnp.zeros((cap, LANES), F32)
    fill_tail(tail_w, towers_ref, gates_ref, small_ref)

    def hop(c, i):
        array, first, order, _ = chains[c]
        source = tail if array == experts else grads.at[array]
        return halving(me, source.at[first : first + unit], stages, sends, receives, c, order, i)

    def settle(c, i):
        array, first, order, _ = chains[c]
        hop(c, i).wait()
        half = stages[i].shape[1]
        at = bit_of(me, order[i]) * half
        if i > 0:
            kept = stages[i - 1][c, rows_at(at, half), :]
        elif array == experts:
            kept = tail[rows_at(first + at, half), :]
        else:
            kept = grads[array, rows_at(first + at, half), :]
        stages[i][c] += kept
        if i + 1 < levels:
            hop(c, i + 1).start()

    def region(c, i):
        array, first, order, _ = chains[c]
        at = rows_at(first + start_of(me, order[: i + 1], unit), unit >> (i + 1))
        return tail_out.at[:, at] if array == experts else experts_out.at[array, :, at]

    def doubling(c, i):
        return pltpu.make_async_remote_copy(
            src_ref=news.at[c] if i == levels - 1 else region(c, i),
            dst_ref=region(c, i),
            send_sem=send_w.at[c, i],
            recv_sem=recv_w.at[c, i],
            device_id=(me ^ chains[c][2][i],),
            device_id_type=MESH,
        )

    def place(c):
        return pltpu.make_async_copy(news.at[c], region(c, levels - 1), local.at[c])

    def renew(c):
        array, first, order, _ = chains[c]
        at = rows_at(first + start_of(me, order, unit), 8)
        weight = tail_w[at, :] if array == experts else experts_ref[array, at, :]
        moment = late_stages[-1]
        grad = stages[-1][c]
        news[c, 0] = stepped(weight, *moments(moment[c, 0], moment[c, 1], grad))
        news[c, 1] = grad
        place(c).start()

    steps = len(set(chain[3] for chain in chains)) + 2 * levels

    def step(s):
        for c, chain in enumerate(chains):
            j = s - chain[3] // 2
            if 0 <= j < levels:
                settle(c, j)
            if j == levels - 1:
                renew(c)
                doubling(c, levels - 1).start()
            i = 2 * levels - 2 - j
            if i == levels - 2:
                place(c).wait()
            if 0 <= i < levels - 1:
                doubling(c, i + 1).wait()
                doubling(c, i).start()
            if j == 2 * levels - 1:
                doubling(c, 0).wait()

    def ready(array):
        for c, chain in enumerate(chains):
            if chain[0] == array:
                hop(c, 0).start()
        if array == experts:
            late_settle(0)

    weights_copy.wait()
    dense_pass(
        ready, stat_ref, fields_ref, pooled_ref, experts_ref, tail_w, towers_ref, small_ref, grads, tail, rows_ref, side
    )
    collect = collector(cap, lists_ref, rows_ref)

    def collect_and_send(i):
        k = n - i
        collect(me ^ k, rows_out, me ^ k)
        exchange(n, me, rows_out, lines_ref, send_c, recv_c, k).start()

    sent = 0
    for s in range(steps):
        goal = min(n - 1, sent + (16 if s == 0 else 4))
        if goal > sent:
            for_range(sent + 1, goal + 1, collect_and_send)
            sent = goal
        if 2 <= s < 2 + levels - early - 1:
            late_settle(s - 2 + 1)
        step(s)
    collect(me, lines_ref, me)
    for_range(1, n, lambda k: exchange(n, me, rows_out, lines_ref, send_c, recv_c, k).wait())


def backward(n, cap, tail_rows, lists, stat, items, fields, pooled, moment_slices, experts_w, gates_w, towers_w, small):
    experts, features, hidden = experts_w.shape
    samples = fields.shape[1]
    levels, early = n.bit_length() - 1, early_levels(n)
    count = len(plan(n, experts, features, tail_rows))
    vmem = pl.BlockSpec(memory_space=pltpu.VMEM)
    smem = pl.BlockSpec(memory_space=pltpu.SMEM)
    dma = pltpu.SemaphoreType.DMA((n,))
    hops = pltpu.SemaphoreType.DMA((count, levels))
    return pl.pallas_call(
        functools.partial(backward_kernel, (n, cap, tail_rows)),
        out_shape=(
            jax.ShapeDtypeStruct((n + 1, cap, LANES), F32),
            jax.ShapeDtypeStruct((experts, 2, features, hidden), F32),
            jax.ShapeDtypeStruct((2, tail_rows, hidden), F32),
        ),
        in_specs=[smem, smem, smem] + [vmem] * 3 + [pl.BlockSpec(memory_space=pl.ANY)] + [vmem] * 3,
        out_specs=(vmem, pl.BlockSpec(memory_space=pl.ANY), vmem),
        scratch_shapes=[pltpu.VMEM((count, 4 * n >> i, hidden), F32) for i in range(levels)]
        + [pltpu.VMEM((count, 2, 8 * n >> (early + i + 1), hidden), F32) for i in range(levels - early)]
        + [
            pltpu.VMEM((experts, features, hidden), F32), pltpu.VMEM((tail_rows, hidden), F32),
            pltpu.VMEM((tail_rows, hidden), F32), pltpu.VMEM((count, 2, 8, hidden), F32),
            pltpu.VMEM((features // LANES * samples + 8, LANES), F32), pltpu.VMEM((samples, samples), F32),
            pltpu.VMEM((n, cap, LANES), F32), pltpu.VMEM((experts, features, hidden), F32),
        ]
        + [dma] * 2 + [hops] * 6 + [pltpu.SemaphoreType.DMA((count,))],
        compiler_params=pltpu.CompilerParams(collective_id=1, has_side_effects=True, vmem_limit_bytes=56 * 2**20),
        name="backward",
    )(lists, stat, items, fields, pooled, moment_slices, experts_w, gates_w, towers_w, small)


def close_kernel(
    sizes,
    owned_ref, pairs_ref, lines_ref, table_ref, row_first_ref, row_second_ref,
    whole_ref, first_ref, second_ref, tail_ref, towers_m_ref, towers_v_ref, gates_m_ref, gates_v_ref, small_m_ref, small_v_ref,
    table_new_ref, row_first_new_ref, row_second_new_ref, new_ref, low_ref, first_new_ref, second_new_ref,
    towers_ref, towers_low_ref, towers_m_new_ref, towers_v_new_ref, gates_ref, gates_m_new_ref, gates_v_new_ref,
    small_ref, small_m_new_ref, small_v_new_ref, loss_ref,
    sums_even, sums_odd,
):
    n, cap, experts, first_steps, steps_each = sizes
    step = pl.program_id(0)
    width, block = table_ref.shape
    half = block // 2
    rows = sums_even.shape[0] - 8

    @pl.when(step == 0)
    def _():
        def clear(i):
            at = pl.ds(pl.multiple_of(i * half, half), half)
            sums_even[at, :] = jnp.zeros((half, LANES), F32)
            sums_odd[at, :] = jnp.zeros((half, LANES), F32)

        for_range(0, rows // half, clear)
        finish_tail(
            owned_ref, experts, tail_ref, towers_m_ref, towers_v_ref, gates_m_ref, gates_v_ref, small_m_ref, small_v_ref,
            towers_ref, towers_low_ref, towers_m_new_ref, towers_v_new_ref, gates_ref, gates_m_new_ref, gates_v_new_ref,
            small_ref, small_m_new_ref, small_v_new_ref, loss_ref,
        )

    @pl.when(step < first_steps)
    def _():
        e = lax.div(step, steps_each)
        new = whole_ref[0, 0]
        new_ref[0] = new
        low_ref[0] = new.astype(BF16)

        @pl.when(owned_ref[e] == 1)
        def _():
            first_new_ref[0], second_new_ref[0] = moments(first_ref[0], second_ref[0], whole_ref[0, 1])

        @pl.when(owned_ref[e] != 1)
        def _():
            first_new_ref[...] = jnp.zeros_like(first_new_ref)
            second_new_ref[...] = jnp.zeros_like(second_new_ref)

        def source(s):
            count = jnp.minimum(jnp.maximum(pairs_ref[s, 0, LANES - 1], pairs_ref[s, 1, LANES - 1]), cap)

            def add(g):
                for i in range(8):
                    r = g * 8 + i
                    line = lines_ref[pl.ds(s * cap + r, 1), :]
                    sums_even[pl.ds(pairs_ref[s, 0, r], 1), :] += line
                    sums_odd[pl.ds(pairs_ref[s, 1, r], 1), :] += line

            for_range(0, (count + 7) // 8, add)

        for_range(step * n // first_steps, (step + 1) * n // first_steps, source)

    @pl.when(step >= first_steps)
    def _():
        left = iota((LANES, LANES), 1) < width
        for b in range(half // LANES):
            at = pl.ds(pl.multiple_of((step - first_steps) * half + b * LANES, LANES), LANES)
            both = jnp.where(left, sums_even[at, :], sums_odd[at, :]).T
            for parity in range(2):
                here = slice(parity * half + b * LANES, parity * half + (b + 1) * LANES)
                grad = both[parity * width : (parity + 1) * width]
                first = BETA_ONE * row_first_ref[:, here] + (1.0 - BETA_ONE) * grad
                mean = jnp.sum(grad * grad, axis=0, keepdims=True) * (1.0 / width)
                second = BETA_TWO * row_second_ref[:, here] + (1.0 - BETA_TWO) * mean
                rate = (RATE_ROWS / (1.0 - BETA_ONE**STEP)) / (
                    jnp.sqrt(second * (1.0 / (1.0 - BETA_TWO**STEP))) + EPSILON
                )
                old = table_ref[:, here]
                table_new_ref[:, here] = old - (first * rate + (RATE_ROWS * DECAY) * old)
                row_first_new_ref[:, here] = first
                row_second_new_ref[:, here] = second


def finish_tail(
    owned_ref, experts, tail_ref, towers_m_ref, towers_v_ref, gates_m_ref, gates_v_ref, small_m_ref, small_v_ref,
    towers_ref, towers_low_ref, towers_m_new_ref, towers_v_new_ref, gates_ref, gates_m_new_ref, gates_v_new_ref,
    small_ref, small_m_new_ref, small_v_new_ref, loss_ref,
):
    tasks, tower, hidden = towers_ref.shape
    count = gates_ref.shape[1]

    def mine(item, pair):
        own = jnp.full((1, 1), owned_ref[item], I32) == 1
        return [jnp.where(own, x, 0.0) for x in pair]

    for k in range(tasks):
        at = slice(k * tower, (k + 1) * tower)
        towers_ref[k] = tail_ref[0, at]
        towers_low_ref[k] = tail_ref[0, at].astype(BF16)
        towers_m_new_ref[k], towers_v_new_ref[k] = mine(
            experts + tasks + k, moments(towers_m_ref[k], towers_v_ref[k], tail_ref[1, at])
        )
        for part in range(2):
            row = tasks * tower + part * GAP + k * count
            at = slice(row, row + count)
            to = slice(part * hidden, (part + 1) * hidden)
            gates_ref[k, :, to] = tail_ref[0, at]
            gates_m_new_ref[k, :, to], gates_v_new_ref[k, :, to] = mine(
                experts + k, moments(gates_m_ref[k, :, to], gates_v_ref[k, :, to], tail_ref[1, at])
            )
    base = tasks * tower + 2 * GAP
    size = small_ref.shape[1]
    for i in range(-(-size // hidden)):
        last = min(size, (i + 1) * hidden)
        to = slice(i * hidden, last)
        line = slice(0, last - i * hidden)
        small_ref[0:1, to] = tail_ref[0, base + i : base + i + 1, line]
        small_m_new_ref[0:1, to], small_v_new_ref[0:1, to] = mine(
            experts + 2 * tasks,
            moments(small_m_ref[0:1, to], small_v_ref[0:1, to], tail_ref[1, base + i : base + i + 1, line]),
        )
    loss_ref[...] = tail_ref[1, base + 8 : base + 9, 0:LANES]


def close(
    n, cap, table_rows, pairs, lines, table, table_m, table_v,
    owned, whole, tail, experts_m, experts_v, towers_m, towers_v, gates_m, gates_v, small_m, small_v,
):
    rows_dev, width = table.shape
    experts, features, hidden = experts_m.shape
    block = 2 * table_rows
    rows = 256
    steps_each = features // rows
    first_steps = experts * steps_each
    update_steps = rows_dev // block

    def late(i, *_):
        return (0, jnp.maximum(i - first_steps, 0))

    def place(i):
        i = jnp.minimum(i, first_steps - 1)
        return lax.div(i, steps_each), lax.rem(i, steps_each)

    def here(i, owned):
        e, b = place(i)
        return e, b, 0

    def only_owner(i, owned):
        e, b = place(i)
        return e, jnp.where(owned[e] == 1, b, 0), 0

    def both(i, owned):
        e, b = place(i)
        return e, 0, b, 0

    wide, thin = pl.BlockSpec((width, block), late), pl.BlockSpec((1, block), late)
    out_block, owners = pl.BlockSpec((1, rows, hidden), here), pl.BlockSpec((1, rows, hidden), only_owner)

    def full(x):
        return pl.BlockSpec(x.shape, lambda i, owned: (0,) * len(x.shape))

    sums = pltpu.VMEM((rows_dev // 2 + 8, LANES), F32)
    lines = lines.reshape((n + 1) * cap, LANES)
    towers = jax.ShapeDtypeStruct(towers_m.shape, F32)
    gates = jax.ShapeDtypeStruct(gates_m.shape, F32)
    small = jax.ShapeDtypeStruct(small_m.shape, F32)
    tail_shapes = (
        towers, jax.ShapeDtypeStruct(towers_m.shape, BF16), towers, towers, gates, gates, gates, small, small, small,
        jax.ShapeDtypeStruct((1, LANES), F32),
    )
    dense_shape = jax.ShapeDtypeStruct(experts_m.shape, F32)
    rows_shape = jax.ShapeDtypeStruct((width, rows_dev), F32)
    out_shape = (
        rows_shape, rows_shape, jax.ShapeDtypeStruct((1, rows_dev), F32),
        dense_shape, jax.ShapeDtypeStruct(experts_m.shape, BF16), dense_shape, dense_shape,
    ) + tail_shapes
    table_new, first_new, second_new, *others = pl.pallas_call(
        functools.partial(close_kernel, (n, cap, experts, first_steps, steps_each)),
        grid_spec=pltpu.PrefetchScalarGridSpec(
            num_scalar_prefetch=1,
            grid=(first_steps + update_steps,),
            in_specs=[
                pl.BlockSpec(memory_space=pltpu.SMEM), full(lines), wide, wide, thin,
                pl.BlockSpec((1, 2, rows, hidden), both), owners, owners,
                full(tail), full(towers_m), full(towers_v), full(gates_m), full(gates_v), full(small_m), full(small_v),
            ],
            out_specs=[wide, wide, thin] + [out_block] * 4 + [full(x) for x in tail_shapes],
            scratch_shapes=[sums, sums],
        ),
        out_shape=out_shape,
        compiler_params=pltpu.CompilerParams(vmem_limit_bytes=58 * 2**20),
        name="close",
    )(
        owned, pairs, lines, table.T, table_m.T, table_v.reshape(1, rows_dev),
        whole, experts_m, experts_v, tail, towers_m, towers_v, gates_m, gates_v, small_m, small_v,
    )
    return (table_new.T, first_new.T, second_new.reshape(rows_dev)), others


def pool_kernel(nothing, tables, bag, pos_ref, lines_ref, pooled_ref):
    samples = pos_ref.shape[1]
    pooled_ref[...] = jnp.zeros_like(pooled_ref)
    left = iota((1, LANES), 1) < LANES // 2

    def sample(s):
        @pl.when(pos_ref[0, s] != nothing)
        def _():
            for q in range(tables // 2):
                sums = []
                for parity in range(2):
                    base = (2 * q + parity) * bag
                    total = lines_ref[pl.ds(pos_ref[base, s], 1), :]
                    for j in range(1, bag):
                        total = total + lines_ref[pl.ds(pos_ref[base + j, s], 1), :]
                    sums.append(total)
                pooled_ref[pl.ds(q * samples + s, 1), :] = jnp.where(left, sums[0], sums[1])

    for_range(0, samples, sample)


def pool(n, cap, tables, bag, pos, lines):
    samples = pos.shape[1]
    return pl.pallas_call(
        functools.partial(pool_kernel, n * cap, tables, bag),
        out_shape=jax.ShapeDtypeStruct((tables // 2 * samples, LANES), F32),
        in_specs=[pl.BlockSpec(memory_space=pltpu.SMEM), pl.BlockSpec(memory_space=pltpu.VMEM)],
        out_specs=pl.BlockSpec(memory_space=pltpu.VMEM),
        compiler_params=pltpu.CompilerParams(vmem_limit_bytes=24 * 2**20),
        name="pool",
    )(pos, lines.reshape((n + 1) * cap, LANES))


def split2(x):
    high = x.astype(BF16)
    return high, (x - high.astype(F32)).astype(BF16)


def dot3(a, b, dims=NN):
    count = a[0].shape[0]
    if count > LANES:
        return dot(a[0], b[0], dims) + dot(a[0], b[1], dims) + dot(a[1], b[0], dims)
    both = dot(jnp.concatenate(a, axis=0), b[0], dims)
    return both[:count] + both[count:] + dot(a[0], b[1], dims)


def sigmoid(x):
    return 1.0 / (1.0 + jnp.exp(-x))


def dense_pass(
    ready, stat_ref, fields_ref, pooled_ref, experts_ref, tail_w, towers_ref, small_ref, grads, tail, rows_ref, side
):
    samples = fields_ref.shape[1]
    experts, features, hidden = experts_ref.shape
    tasks, tower, _ = towers_ref.shape
    tail[...] = jnp.zeros_like(tail)

    def put_tail(row, value):
        tail[row : row + value.shape[0], :] = value

    start = experts * hidden
    tower_at = start
    weight_at = start + tasks * tower
    bias_at = weight_at + tasks * tower
    side[0:8, :] = fields_ref[...]
    side[8:, :] = jnp.zeros((samples - 8, samples), F32)
    by_sample = side[...].T
    weight = by_sample[:, tasks : tasks + 1]
    scale = weight / stat_ref[0].astype(F32)
    x = jnp.concatenate([pooled_ref[q * samples : (q + 1) * samples] for q in range(features // LANES)], axis=1)
    x2 = split2(x)
    at = tasks * tower
    gate_w = jnp.concatenate([tail_w[at + k * GAP : at + k * GAP + tasks * experts, :] for k in range(2)], axis=1)
    gate_w2 = split2(gate_w)
    gate_logits = dot3(x2, gate_w2, NT)
    pres, sigs, hids = [], [], []
    for e in range(experts):
        pre = dot3(x2, split2(experts_ref[e])) + small_ref[0:1, e * hidden : (e + 1) * hidden]
        sig = sigmoid(pre)
        pres.append(pre)
        sigs.append(sig)
        hids.append(pre * sig)
    dhids = [jnp.zeros((samples, hidden), F32) for _ in range(experts)]
    dgate_logits = []
    loss = jnp.zeros((samples, 1), F32)
    tower_bias_grads, out_weight_grads, task_bias_grads = [], [], []
    for k in range(tasks):
        logits = [gate_logits[:, k * experts + e : k * experts + e + 1] for e in range(experts)]
        top = functools.reduce(jnp.maximum, logits)
        powers = [jnp.exp(v - top) for v in logits]
        whole = functools.reduce(jnp.add, powers)
        gates = [v / whole for v in powers]
        mix = functools.reduce(jnp.add, [gates[e] * hids[e] for e in range(experts)])
        mix2 = split2(mix)
        tower2 = split2(towers_ref[k])
        at = tower_at + k * tower
        pre = dot3(mix2, tower2, NT) + small_ref[0:1, at : at + tower]
        sig = sigmoid(pre)
        zed = pre * sig
        at = weight_at + k * tower
        out_weight = small_ref[0:1, at : at + tower]
        logit = jnp.sum(zed * out_weight, axis=1, keepdims=True) + small_ref[0:1, bias_at + k : bias_at + k + 1]
        label = by_sample[:, k : k + 1]
        softplus = jnp.maximum(logit, 0.0) + jnp.log1p(jnp.exp(-jnp.abs(logit)))
        loss = loss + weight * (softplus - label * logit)
        dlogit = scale * (sigmoid(logit) - label)
        task_bias_grads.append(jnp.sum(dlogit, axis=0, keepdims=True))
        out_weight_grads.append(jnp.sum(dlogit * zed, axis=0, keepdims=True))
        dpre = dlogit * out_weight * (sig * (1.0 + pre * (1.0 - sig)))
        tower_bias_grads.append(jnp.sum(dpre, axis=0, keepdims=True))
        dpre2 = split2(dpre)
        put_tail(k * tower, dot3(split2(dpre.T), mix2))
        dmix = dot3(dpre2, tower2)
        dgates = [jnp.sum(dmix * hids[e], axis=1, keepdims=True) for e in range(experts)]
        mean = functools.reduce(jnp.add, [gates[e] * dgates[e] for e in range(experts)])
        for e in range(experts):
            dgate_logits.append(gates[e] * (dgates[e] - mean))
            dhids[e] = dhids[e] + gates[e] * dmix
    lane = iota((samples, LANES), 1)
    dgl = jnp.zeros((samples, LANES), F32)
    for i, v in enumerate(dgate_logits):
        dgl = jnp.where(lane == i, v, dgl)
    count = tasks * experts
    dgl_t2 = split2(dgl.T[0:16])
    dgates_w = dot3(dgl_t2, x2)
    tail_at = tasks * tower
    put_tail(tail_at, dgates_w[:, :hidden])
    put_tail(tail_at + GAP, dgates_w[:, hidden:])
    expert_bias_grads, dpres = [], []
    for e in range(experts):
        dpre = dhids[e] * (sigs[e] * (1.0 + pres[e] * (1.0 - sigs[e])))
        expert_bias_grads.append(jnp.sum(dpre, axis=0, keepdims=True))
        dpres.append(split2(dpre))
    small_at = tail_at + 2 * GAP
    pad = jnp.zeros((1, 2 * hidden - 2 * tasks * tower - tasks), F32)
    line = jnp.concatenate(tower_bias_grads + out_weight_grads + task_bias_grads + [pad], axis=1)
    loss_row = jnp.where(iota((1, hidden), 1) == 0, jnp.sum(loss, axis=0, keepdims=True), 0.0)
    for e in range(experts):
        put_tail(small_at + e, expert_bias_grads[e])
    for i in range(line.shape[1] // hidden):
        put_tail(small_at + experts + i, line[:, i * hidden : (i + 1) * hidden])
    put_tail(small_at + 8, loss_row)
    ready(experts)
    x_t2 = split2(x.T)
    for e in range(experts):
        grads[e] = dot3(x_t2, dpres[e])
        ready(e)
    dx = dot3(split2(dgl[:, :count]), gate_w2)
    for e in range(experts):
        dx = dx + dot3(dpres[e], split2(experts_ref[e]), NT)
    for q in range(features // LANES):
        rows_ref[q * samples : (q + 1) * samples, :] = dx[:, q * LANES : (q + 1) * LANES]
    rows_ref[features // LANES * samples :, :] = jnp.zeros((8, LANES), F32)


def moments(first, second, grad):
    return (
        BETA_ONE * first + (1.0 - BETA_ONE) * grad,
        BETA_TWO * second + (1.0 - BETA_TWO) * grad * grad,
    )


def stepped(weight, first_new, second_new):
    first_hat = first_new / (1.0 - BETA_ONE**STEP)
    second_hat = second_new / (1.0 - BETA_TWO**STEP)
    return weight - RATE_DENSE * (first_hat / (jnp.sqrt(second_hat) + EPSILON) + DECAY * weight)


def all_sum(tree, axis):
    n = lax.axis_size(axis)
    bit = 1
    while bit < n:
        pairs = [(i, i ^ bit) for i in range(n)]
        tree = jax.tree.map(lambda x: x + lax.ppermute(x, axis, pairs), tree)
        bit *= 2
    return tree


def from_root(block, axis, source):
    block = jnp.where(lax.axis_index(axis) == source, block, jnp.zeros_like(block))
    return all_sum(block, axis)


def dense_forward(params, pooled, labels, weights):
    experts_w, gates_w, towers_w, small = params
    n_experts, _, hidden = experts_w.shape
    tasks, _, tower = towers_w.shape
    start = n_experts * hidden
    expert_bias = small[:start].reshape(n_experts, hidden)
    tower_bias = small[start : start + tasks * tower].reshape(tasks, tower)
    start = start + tasks * tower
    out_weight = small[start : start + tasks * tower].reshape(tasks, tower)
    task_bias = small[start + tasks * tower :]
    hidden_act = jax.nn.silu(
        jnp.einsum("si,eih->seh", pooled, experts_w, precision=lax.Precision.HIGHEST) + expert_bias
    )
    gate = jax.nn.softmax(jnp.einsum("si,kie->ske", pooled, gates_w, precision=lax.Precision.HIGHEST), axis=-1)
    mixed = jnp.einsum("ske,seh->skh", gate, hidden_act, precision=lax.Precision.HIGHEST)
    zed = jax.nn.silu(jnp.einsum("skh,khc->skc", mixed, towers_w, precision=lax.Precision.HIGHEST) + tower_bias)
    logit = jnp.sum(zed * out_weight, axis=-1) + task_bias
    losses = jax.nn.softplus(logit) - labels * logit
    return jnp.sum(weights[:, None] * losses)


def adam_step(weight, first, second, grad, rate):
    first_new = BETA_ONE * first + (1.0 - BETA_ONE) * grad
    second_new = BETA_TWO * second + (1.0 - BETA_TWO) * grad * grad
    first_hat = first_new / (1.0 - BETA_ONE**STEP)
    second_hat = second_new / (1.0 - BETA_TWO**STEP)
    weight_new = weight - rate * (first_hat / (jnp.sqrt(second_hat) + EPSILON) + DECAY * weight)
    return (weight_new, first_new, second_new)


def plain_step(
    row_ids,
    lengths,
    counts,
    mask,
    labels,
    row_home,
    mat_home,
    table,
    table_m,
    table_v,
    experts_w,
    gates_w,
    towers_w,
    small_params,
    experts_m,
    experts_v,
    gates_m,
    gates_v,
    towers_m,
    towers_v,
    small_m,
    small_v,
):
    devices = lax.axis_size("dev")
    myself = lax.axis_index("dev")
    samples, tables, bag_slots = row_ids.shape
    rows_dev, width = table.shape
    per_table = row_home.shape[1] // devices
    block_rows = rows_dev // (tables * per_table)
    slots = samples * tables * bag_slots
    average = slots // devices
    capacity = average + average // 2
    present = jnp.arange(samples) < counts[0]
    weights = jnp.where(present & (mask == 1), 1.0, 0.0).astype(jnp.float32)
    live = present[:, None, None] & (jnp.arange(bag_slots)[None, None, :] < lengths[:, :, None])
    table_of = jnp.broadcast_to(jnp.arange(tables)[None, :, None], row_ids.shape)
    homes = row_home[table_of, row_ids // block_rows]
    owners = (homes // per_table).reshape(-1)
    local_rows = (
        (table_of * per_table + homes % per_table) * block_rows + row_ids % block_rows
    ).reshape(-1)
    live_flat = live.reshape(-1)
    live_float = live_flat.astype(jnp.float32)
    targets = jnp.where(live_flat, owners, devices)
    order = jnp.argsort(targets, stable=True)
    sorted_targets = targets[order]
    starts = jnp.searchsorted(sorted_targets, jnp.arange(devices + 1), side="left")
    sorted_rank = jnp.arange(slots, dtype=jnp.int32) - starts[sorted_targets]
    slot_rank = jnp.zeros(slots, jnp.int32).at[order].set(sorted_rank)
    slot_rank = jnp.where(live_flat, slot_rank, 0)
    requests = (
        jnp.zeros((devices, capacity), jnp.int32)
        .at[targets, slot_rank]
        .set(local_rows, mode="drop")
    )
    asked_rows = lax.all_to_all(requests, "dev", split_axis=0, concat_axis=0, tiled=True)
    found = table[asked_rows]
    arrived = lax.all_to_all(found, "dev", split_axis=0, concat_axis=0, tiled=True)
    safe_owner = jnp.minimum(owners, devices - 1)
    slot_rows = arrived[safe_owner, slot_rank] * live_float[:, None]
    pooled = jnp.sum(slot_rows.reshape(samples, tables, bag_slots, width), axis=2).reshape(
        samples, tables * width
    )
    params = (experts_w, gates_w, towers_w, small_params)
    local_loss, pull = jax.vjp(
        lambda dense, features: dense_forward(dense, features, labels, weights), params, pooled
    )
    loss_sum, weight_sum = all_sum((local_loss, jnp.sum(weights)), "dev")
    local_grads, pooled_grad = pull(1.0 / weight_sum)
    slot_grads = (
        jnp.broadcast_to(
            pooled_grad.reshape(samples, tables, 1, width), (samples, tables, bag_slots, width)
        ).reshape(slots, width)
        * live_float[:, None]
    )
    outgoing = (
        jnp.zeros((devices, capacity, width), jnp.float32)
        .at[targets, slot_rank]
        .set(slot_grads, mode="drop")
    )
    incoming = lax.all_to_all(outgoing, "dev", split_axis=0, concat_axis=0, tiled=True)
    grad_table = (
        jnp.zeros((rows_dev, width), jnp.float32)
        .at[asked_rows.reshape(-1)]
        .add(incoming.reshape(-1, width))
    )
    table_m_new = BETA_ONE * table_m + (1.0 - BETA_ONE) * grad_table
    table_v_new = BETA_TWO * table_v + (1.0 - BETA_TWO) * jnp.mean(grad_table * grad_table, axis=1)
    first_hat = table_m_new / (1.0 - BETA_ONE**STEP)
    second_hat = table_v_new / (1.0 - BETA_TWO**STEP)
    table_new = table - RATE_ROWS * (
        first_hat / (jnp.sqrt(second_hat)[:, None] + EPSILON) + DECAY * table
    )
    grad_experts, grad_gates, grad_towers, grad_small = local_grads
    grad_experts, grad_gates, grad_towers, grad_small = all_sum(
        (grad_experts, grad_gates, grad_towers, grad_small), "dev"
    )
    kinds = (
        (experts_w, experts_m[0], experts_v[0], grad_experts),
        (gates_w, gates_m[0], gates_v[0], grad_gates),
        (towers_w, towers_m[0], towers_v[0], grad_towers),
        (small_params[None], small_m, small_v, grad_small[None]),
    )
    finals = []
    first_outs = []
    second_outs = []
    base = 0
    for stack, firsts, seconds, grad in kinds:
        kind_weights = []
        kind_firsts = []
        kind_seconds = []
        for position in range(stack.shape[0]):
            owner_id = mat_home[base + position]
            is_owner = owner_id == myself
            weight_new, first_new, second_new = adam_step(
                stack[position], firsts[position], seconds[position], grad[position], RATE_DENSE
            )
            kind_firsts.append(jnp.where(is_owner, first_new, 0.0))
            kind_seconds.append(jnp.where(is_owner, second_new, 0.0))
            kept = jnp.where(is_owner, weight_new, stack[position])
            kind_weights.append(from_root(kept, "dev", owner_id))
        base = base + stack.shape[0]
        finals.append(jnp.stack(kind_weights))
        first_outs.append(jnp.stack(kind_firsts)[None])
        second_outs.append(jnp.stack(kind_seconds)[None])
    experts_new, gates_new, towers_new, small_stack = finals
    small_new = small_stack[0]
    return (
        loss_sum,
        weight_sum,
        table_new,
        table_m_new,
        table_v_new,
        experts_new,
        gates_new,
        towers_new,
        small_new,
        first_outs[0],
        second_outs[0],
        first_outs[1],
        second_outs[1],
        first_outs[2],
        second_outs[2],
        first_outs[3][0],
        second_outs[3][0],
        experts_new.astype(jnp.bfloat16)[None],
        gates_new.astype(jnp.bfloat16)[None],
        towers_new.astype(jnp.bfloat16)[None],
        small_new.astype(jnp.bfloat16)[None],
    )


def per_device(*args):
    (
        row_ids, lengths, counts, mask, labels, row_home, mat_home, table, table_m, table_v,
        experts_w, gates_w, towers_w, small_params,
        experts_m, experts_v, gates_m, gates_v, towers_m, towers_v, small_m, small_v,
    ) = args
    n = lax.axis_size("dev")
    me = lax.axis_index("dev")
    samples, tables, bag = row_ids.shape
    rows_dev, width = table.shape
    cap = max(8, (samples * tables * bag // n * 5 // 16 + 7) // 8 * 8)
    experts, features, hidden = experts_w.shape
    tasks, _, tower = towers_w.shape
    tail_rows = -(-(tasks * tower + 2 * GAP + 16) // (8 * n)) * 8 * n
    fields, pos, mine, theirs, pairs, stat, lines, moment_slices = forward(
        n, cap, tail_rows, row_ids, lengths, counts, mask, labels, row_home, table, mat_home,
        experts_m[0], experts_v[0], towers_m[0], towers_v[0], gates_m[0], gates_v[0], small_m, small_v,
    )
    most, weight_count = stat[4, 0], stat[5, 0]

    def usual(fields, pos, mine, pairs, lines, moment_slices, weight_count, *args):
        (
            _, _, _, _, _, _, mat_home, table, table_m, table_v, experts_w, gates_w, towers_w, small_params,
            experts_m, experts_v, gates_m, gates_v, towers_m, towers_v, small_m, small_v,
        ) = args

        def turned(x):
            return x.transpose(0, 2, 1)

        gates_t, towers_t, small = turned(gates_w), turned(towers_w), small_params.reshape(1, -1)
        pooled = pool(n, cap, tables, bag, pos, lines)
        back, whole, tail = backward(
            n, cap, tail_rows, mine, weight_count[None], mat_home, fields, pooled, moment_slices,
            experts_w, gates_t, towers_t, small,
        )
        rows_new, (
            experts_new, experts_low, experts_m_new, experts_v_new,
            towers_new, towers_low, towers_m_new, towers_v_new, gates_new, gates_m_new, gates_v_new,
            small_new, small_m_new, small_v_new, loss,
        ) = close(
            n, cap, rows_dev // tables, pairs, back, table, table_m, table_v,
            (mat_home == me).astype(I32), whole, tail, experts_m[0], experts_v[0], turned(towers_m[0]), turned(towers_v[0]),
            turned(gates_m[0]), turned(gates_v[0]), small_m, small_v,
        )
        gates_new = turned(gates_new)
        small_new = small_new.reshape(-1)
        return (
            loss[0, 0], weight_count.astype(F32), *rows_new, experts_new, gates_new, turned(towers_new), small_new,
            experts_m_new[None], experts_v_new[None], turned(gates_m_new)[None], turned(gates_v_new)[None],
            turned(towers_m_new)[None], turned(towers_v_new)[None], small_m_new, small_v_new,
            experts_low[None], gates_new.astype(BF16)[None], turned(towers_low)[None], small_new.astype(BF16)[None],
        )

    def crowded(fields, pos, mine, pairs, lines, moment_slices, weight_count, *args):
        return plain_step(*args)

    return lax.cond(
        most <= cap, usual, crowded, fields, pos, mine, pairs, lines, moment_slices, weight_count, *args
    )


def solution(mesh):
    def split(dims):
        return P("dev", *(None,) * (dims - 1))

    by_device = split(4)
    return jax.shard_map(
        per_device,
        mesh=mesh,
        in_specs=(
            split(3), split(2), split(1), split(1), split(2), P(), P(), split(2), split(2), split(1),
            P(), P(), P(), P(),
        ) + (by_device,) * 6 + (split(2),) * 2,
        out_specs=(P(), P(), split(2), split(2), split(1), P(), P(), P(), P())
        + (by_device,) * 6 + (split(2),) * 2 + (by_device,) * 3 + (split(2),),
        check_vma=False,
    )
```

```python
import functools
import jax
import jax.numpy as jnp
from jax import lax
from jax.experimental import pallas as pl
from jax.experimental.pallas import tpu as pltpu
from jax.sharding import PartitionSpec as P

MESH = pl.DeviceIdType.MESH
F32, BF16, I32 = jnp.float32, jnp.bfloat16, jnp.int32
NN, NT, TN = (((1,), (0,)), ((), ())), (((1,), (1,)), ((), ())), (((0,), (0,)), ((), ()))
LANES = 128


def iota(shape, dim):
    return lax.broadcasted_iota(I32, shape, dim)


def dot(a, b, dims=NN):
    return lax.dot_general(a, b, dims, preferred_element_type=F32)


def split3(x):
    high = x.astype(BF16)
    rest = x - high.astype(F32)
    middle = rest.astype(BF16)
    low = (rest - middle.astype(F32)).astype(BF16)
    return high, middle, low


def greet_all(n, me):
    barrier = pltpu.get_barrier_semaphore()

    def signal(k, carry):
        pl.semaphore_signal(barrier, inc=1, device_id=(me ^ k,), device_id_type=MESH)
        return carry

    lax.fori_loop(1, n, signal, 0)


def await_all(n):
    pl.semaphore_wait(pltpu.get_barrier_semaphore(), n - 1)


def exchange(n, me, source, target, sends, receives, k):
    peer = me ^ k
    return pltpu.make_async_remote_copy(
        src_ref=source.at[peer],
        dst_ref=target.at[me],
        send_sem=sends.at[k],
        recv_sem=receives.at[k],
        device_id=(peer,),
        device_id_type=MESH,
    )


def for_range(low, high, body):
    def step(k, carry):
        body(k)
        return carry

    lax.fori_loop(low, high, step, 0)

STEP = 5
BETA_ONE = 0.9
BETA_TWO = 0.999
EPSILON = 1e-08
DECAY = 0.01
RATE_DENSE = 0.02
RATE_ROWS = 0.3
GAP = 16

def axis_orders(n):
    bits = [1 << i for i in range(n.bit_length() - 1)]
    core, rest = bits[:1], bits[1:]
    a = len(rest) // 3
    b = (len(rest) - a) // 2
    x, y, z = rest[:a], rest[a : a + b], rest[a + b :]
    return core + x + y + z, core + y + x + z, core + z + x + y, core + z + y + x


def early_levels(n):
    rest = n.bit_length() - 2
    a = rest // 3
    return 1 + a + (rest - a) // 2


def bit_of(me, bit):
    return lax.rem(lax.div(me, bit), 2)


def start_of(me, order, rows):
    start = 0
    for bit in order:
        rows = rows // 2
        start = start + bit_of(me, bit) * rows
    return start


def rows_at(start, count):
    return pl.ds(pl.multiple_of(start, 8), count)


def plan(n, experts, features, tail_rows):
    unit = 8 * n
    along_x, along_y, along_z, along_w = axis_orders(n)
    chains = []
    for k in range(features // unit):
        for e in range(experts):
            chains.append((e, k * unit, along_y if e % 2 else along_x, k))
    for k in range(tail_rows // unit):
        chains.append((experts, k * unit, along_w if k % 2 else along_z, k // 2))
    return chains


def halving(me, source, stages, sends, receives, c, order, i, lane=0):
    bit = order[i]
    before = source if i == 0 else stages[i - 1].at[c]
    target = stages[i].at[c]
    half = stages[i].shape[-2]
    at = rows_at((1 - bit_of(me, bit)) * half, half)
    if i == 0 and len(stages[0].shape) == 4:
        target = target.at[lane]
        lane_sem = lane * len(order)
    else:
        lane_sem = i
    return pltpu.make_async_remote_copy(
        src_ref=before.at[at] if len(before.shape) == 2 else before.at[:, at],
        dst_ref=target,
        send_sem=sends.at[c, lane_sem],
        recv_sem=receives.at[c, lane_sem],
        device_id=(me ^ bit,),
        device_id_type=MESH,
    )


def fill_tail(tail, towers, gates, small):
    tasks, tower, hidden = towers.shape
    count = gates.shape[1]
    size = small.shape[1]
    tail[...] = jnp.zeros_like(tail)
    tail[0 : tasks * tower, :] = towers[...].reshape(tasks * tower, hidden)
    for part in range(2):
        for k in range(tasks):
            at = tasks * tower + part * GAP + k * count
            tail[at : at + count, :] = gates[k][:, part * hidden : (part + 1) * hidden]
    at = tasks * tower + 2 * GAP
    for i in range(-(-size // hidden)):
        last = min(size, (i + 1) * hidden)
        tail[at + i : at + i + 1, 0 : last - i * hidden] = small[0:1, i * hidden : last]


def owner_side(me, n, items_ref, experts, tasks, tower):
    def chosen(chain, i, count):
        array, first, order, _ = chain
        bit = order[i]
        if array < experts:
            return bit_of(items_ref[array], bit) == bit_of(me, bit)
        towers = tasks * tower
        row = first + start_of(me, order[: i + 1], 8 * n) + iota((count, LANES), 0)
        item = lax.div(row, tower) + experts + tasks
        for part in range(2):
            at = towers + part * GAP
            item = jnp.where((row >= at) & (row < at + tasks * experts), experts + lax.div(row - at, experts), item)
        item = jnp.where(row >= towers + 2 * GAP, experts + 2 * tasks, item)
        home = jnp.zeros((count, LANES), I32)
        for k in range(experts, experts + 2 * tasks + 1):
            home = jnp.where(item == k, items_ref[k], home)
        return (bit_of(home, bit) == bit_of(me, bit))[:, :1]

    return chosen


def forward_kernel(
    sizes,
    ids_ref, lengths_ref, counts_ref, mask_ref, labels_ref, homes_ref, table_hbm, items_ref,
    experts_m_ref, experts_v_ref, towers_m_ref, towers_v_ref, gates_m_ref, gates_v_ref, small_m_ref, small_v_ref,
    fields_ref, pos_ref, mine_ref, theirs_ref, pairs_ref, stat_ref, lines_ref, moments_ref,
    outbox, inbox, message, replies, lists, field_scratch, owner_ref, rank_ref, local_ref, asked_smem, rows_ref, rows_out,
    tails, kept_ref, table_ref, *rest,
):
    n, cap, tables, bag, tasks, experts, per_table, block_rows, rows_dev = sizes
    levels = early_levels(n)
    stages = list(rest[: levels - 1]) + [moments_ref]
    send_a, recv_a, send_b, recv_b, send_c, recv_c, send_m, recv_m, keep_sem, sems = rest[levels - 1 :]
    chains = plan(n, experts, experts_m_ref.shape[1], tails.shape[1])
    unit = 8 * n
    rows = tables * bag
    me = lax.axis_index("dev")
    shift = lax.rem(me * 13, n)
    per_pair = LANES // n
    greet_all(n, me)
    table_copy = pltpu.make_async_copy(table_hbm, table_ref, sems.at[1])
    table_copy.start()
    table_of = lax.div(iota((rows, LANES), 0), bag)
    slot_of = lax.rem(iota((rows, LANES), 0), bag)
    expand = jnp.where(lax.div(iota((rows, tables), 0), bag) == iota((rows, tables), 1), 1.0, 0.0).astype(BF16)
    used = dot(expand, lengths_ref[...].astype(F32).astype(BF16)).astype(I32)
    present = iota((1, LANES), 1) < counts_ref[0]
    live = present & (slot_of < used)
    field_scratch[0:rows, :] = jnp.where(live, ids_ref[...], -1).astype(F32)
    field_scratch[rows : rows + tasks, :] = labels_ref[...]
    field_scratch[rows + tasks : rows + tasks + 1, :] = jnp.where(present & (mask_ref[...] == 1), 1.0, 0.0)
    field_scratch[rows + tasks + 1 :, :] = jnp.zeros((LANES - rows - tasks - 1, LANES), F32)
    row = iota((n * 8, LANES), 0)
    peer_of, piece = lax.div(row, 8), lax.rem(row, 8)
    column = iota((n * 8, LANES), 1)
    pick = jnp.where((piece < per_pair) & (column == piece * n + lax.rem(peer_of - shift + n, n)), 1.0, 0.0).astype(BF16)
    high, middle, low = split3(field_scratch[...])
    spread = dot(pick, high, NT) + dot(pick, middle, NT) + dot(pick, low, NT)
    outbox[...] = spread.reshape(n, 8, LANES)
    await_all(n)
    own_copy = pltpu.make_async_copy(outbox.at[me], inbox.at[me], sems.at[0])
    own_copy.start()
    for_range(1, n, lambda k: exchange(n, me, outbox, inbox, send_a, recv_a, k).start())
    fill_tail(tails.at[0], towers_m_ref, gates_m_ref, small_m_ref)
    fill_tail(tails.at[1], towers_v_ref, gates_v_ref, small_v_ref)

    def whole(c, w):
        array, first, _, _ = chains[c]
        source = tails.at[w] if array == experts else (experts_m_ref, experts_v_ref)[w].at[array]
        return source.at[first : first + unit]

    def hop(c, i, lane=0):
        return halving(me, whole(c, lane) if i == 0 else None, stages, send_m, recv_m, c, chains[c][2], i, lane)

    def keep(c, w):
        at = rows_at(bit_of(me, 1) * (unit // 2), unit // 2)
        return pltpu.make_async_copy(whole(c, w).at[at], kept_ref.at[c, w], keep_sem.at[c, w])

    for c in range(len(chains)):
        for w in range(2):
            hop(c, 0, w).start()
            keep(c, w).start()

    chosen = owner_side(me, n, items_ref, experts, tasks, towers_m_ref.shape[1])

    def settle(c, i):
        order = chains[c][2]
        for w in range(2 if i == 0 else 1):
            hop(c, i, w).wait()
            if i == 0:
                keep(c, w).wait()
        half = stages[i].shape[2]
        mine = rows_at(bit_of(me, order[i]) * half, half)
        flag = chosen(chains[c], i, half)
        for w in range(2):
            kept = kept_ref[c, w] if i == 0 else stages[i - 1][c, w, mine, :]
            stages[i][c, w] = jnp.where(flag, kept, stages[i][c, w])
        if i + 1 < levels:
            hop(c, i + 1).start()

    events = [(c, j) for t in range(16) for c, chain in enumerate(chains) for j in (t - chain[3],) if 0 <= j < levels]
    done = [0]

    def settle_some(count):
        for c, j in events[done[0] : done[0] + count]:
            settle(c, j)
        done[0] += count

    homes = homes_ref[...]
    blocks = homes.shape[1]
    homes_rows = (
        dot(expand, (homes >> 5).astype(F32).astype(BF16)) * 32.0 + dot(expand, (homes & 31).astype(F32).astype(BF16))
    ).astype(I32)
    gather_back = jnp.where((piece < per_pair) & (column == peer_of * per_pair + piece), 1.0, 0.0).astype(BF16)
    before = jnp.where(iota((LANES, LANES), 0) < iota((LANES, LANES), 1), 1.0, 0.0).astype(BF16)
    ones = jnp.ones((LANES, LANES), BF16)
    r_out, r_in = iota((rows + 8, rows), 0), iota((rows + 8, rows), 1)
    parity_in = lax.rem(lax.div(r_in, bag), 2)
    earlier = (r_out < rows) & (r_in < r_out) & (parity_in == lax.rem(lax.div(r_out, bag), 2))
    totals = (r_out == rows + 2 + parity_in)
    above = jnp.where(earlier | totals, 1.0, 0.0).astype(BF16)
    for_range(1, n, lambda k: exchange(n, me, outbox, inbox, send_a, recv_a, k).wait())
    own_copy.wait()
    settle_some(4)
    arrived = inbox[...].reshape(n * 8, LANES).T
    high, middle, low = split3(arrived)
    fields = dot(high, gather_back) + dot(middle, gather_back) + dot(low, gather_back)
    fields_ref[...] = fields[rows : rows + 8]
    ids = fields[0:rows].astype(I32)
    weight_count = jnp.sum(fields[rows + tasks : rows + tasks + 1], axis=1, keepdims=True).astype(I32)
    live = ids >= 0
    ids = jnp.maximum(ids, 0)
    block = lax.div(ids, block_rows)
    lane = block & (LANES - 1)
    home = jnp.zeros((rows, LANES), I32)
    for part in range(blocks // LANES):
        found = jnp.take_along_axis(homes_rows[:, part * LANES : (part + 1) * LANES], lane, axis=1, mode="promise_in_bounds")
        home = jnp.where(lax.div(block, LANES) == part, found, home)
    owner = jnp.where(live, lax.div(home, per_table), n)
    local = (table_of * per_table + lax.rem(home, per_table)) * block_rows + lax.rem(ids, block_rows)
    owner_ref[...] = owner
    local_ref[...] = local

    def rank_step(o, carry):
        rank, most = carry
        is_mine = owner == o
        flags = jnp.where(is_mine, 1.0, 0.0).astype(BF16)
        row_totals = dot(flags, ones).astype(BF16)
        bases = dot(above, row_totals)
        count = bases[rows : rows + 8].astype(I32)
        message[o] = count
        rank = jnp.where(is_mine, (dot(flags, before) + bases[0:rows]).astype(I32), rank)
        return rank, jnp.maximum(most, count)

    rank, most = jnp.zeros((rows, LANES), I32), jnp.zeros((8, LANES), I32)
    for part in range(4):
        rank, most = lax.fori_loop(part * n // 4, (part + 1) * n // 4, rank_step, (rank, most), unroll=4)
        settle_some(2)
    rank_ref[...] = rank
    most = jnp.max(most, axis=0, keepdims=True)
    pos_ref[...] = jnp.where(live, jnp.where(rank < cap, owner * cap + rank, n * cap + 1), n * cap)
    lists[...] = jnp.zeros_like(lists)
    device_row = iota((n, LANES), 0)
    rank_row = iota((LANES, LANES), 0)
    lane_value = (iota((n, LANES), 1)).astype(F32)

    def list_step(q, carry):
        for parity in range(2):
            picks, places = [], []
            for j in range(bag):
                r = (2 * q + parity) * bag + j
                owner_row = owner_ref[pl.ds(r, 1), :]
                local_row = local_ref[pl.ds(r, 1), :]
                hit = device_row == owner_row
                picks.append(
                    jnp.concatenate(
                        [
                            jnp.where(hit, ((local_row >> 7) + 1).astype(F32), 0.0),
                            jnp.where(hit, (local_row & 127).astype(F32), 0.0),
                            jnp.where(hit, (q + 1).astype(F32), 0.0),
                            jnp.where(hit, lane_value, 0.0),
                        ],
                        axis=0,
                    ).astype(BF16)
                )
                places.append(jnp.where(rank_row == rank_ref[pl.ds(r, 1), :], 1.0, 0.0).astype(BF16))
            lists[parity] += dot(jnp.concatenate(picks, axis=1), jnp.concatenate(places, axis=1), NT)
        return carry

    for part in range(2):
        lax.fori_loop(part * tables // 4, (part + 1) * tables // 4, list_step, 0)
        settle_some(1)
    sub = iota((8, LANES), 0)
    is_last = iota((1, LANES), 1) == LANES - 1

    def post(k):
        o = me ^ k
        tile = message[o]
        rows_list = []
        for parity in range(2):
            count = tile[2 + parity : 3 + parity]
            got = [lists[parity, pl.ds(part * n + o, 1), :].astype(I32) for part in range(4)]
            asked = jnp.where(got[0] > 0, (got[0] - 1) * LANES + got[1], rows_dev)
            slot = jnp.where(got[0] > 0, (got[2] - 1) * LANES + got[3], tables // 2 * LANES)
            rows_list.append(jnp.where(is_last, count, asked))
            mine_ref[o, parity : parity + 1, :] = jnp.where(is_last, count, slot)
        tile = jnp.where(sub == 0, rows_list[0], jnp.where(sub == 1, rows_list[1], tile))
        message[o] = jnp.where(sub == 4, most, jnp.where(sub == 5, weight_count, tile))

    def post_and_send(k):
        post(k)
        exchange(n, me, message, replies, send_b, recv_b, k).start()

    for_range(1, n, post_and_send)
    post(0)
    own_copy = pltpu.make_async_copy(message.at[me], replies.at[me], sems.at[0])
    own_copy.start()
    settle_some(2)
    width = table_ref.shape[0]
    table_copy.wait()
    rows_ref[rows_dev:, :] = jnp.zeros((rows_ref.shape[0] - rows_dev, LANES), F32)

    def turn(b):
        at = pl.ds(pl.multiple_of(b * LANES, LANES), LANES)
        rows_ref[at, :] = jnp.concatenate([table_ref[:, at]] * (LANES // width), axis=0).T

    for part in range(4):
        for_range(part * (rows_dev // LANES // 4), (part + 1) * (rows_dev // LANES // 4), turn)
        settle_some(2)
    for_range(1, n, lambda k: exchange(n, me, message, replies, send_b, recv_b, k).wait())
    own_copy.wait()

    def take(s, carry):
        most, total = carry
        tile = replies[s]
        asked = jnp.clip(tile[0:2], 0, rows_dev)
        theirs_ref[s] = asked
        table_rows = per_table * block_rows
        paired = lax.div(asked, 2 * table_rows) * table_rows + lax.rem(asked, table_rows)
        pairs_ref[s] = jnp.where(is_last, asked, paired)
        return jnp.maximum(most, tile), total + tile

    most, total = lax.fori_loop(0, n, take, (jnp.zeros((8, LANES), I32), jnp.zeros((8, LANES), I32)))
    stat_ref[...] = jnp.where(sub == 4, most, total)
    to_scalars = pltpu.make_async_copy(theirs_ref, asked_smem, sems.at[0])
    to_scalars.start()
    to_scalars.wait()
    lines_ref[n] = jnp.zeros((cap, LANES), F32)
    collect = collector(cap, asked_smem, rows_ref)

    def collect_and_send(i):
        k = n - i
        collect(me ^ k, rows_out, me ^ k)
        exchange(n, me, rows_out, lines_ref, send_c, recv_c, k).start()

    for part in range(8):
        for_range(part * n // 8 + (part == 0), (part + 1) * n // 8, collect_and_send)
        settle_some(3 * (part >= 4))
    collect(me, lines_ref, me)
    settle_some(len(events) - done[0])
    for_range(1, n, lambda k: exchange(n, me, rows_out, lines_ref, send_c, recv_c, k).wait())


def collector(cap, lists_ref, rows_ref):
    left = iota((1, LANES), 1) < LANES // 2

    def collect(peer, target, slot):
        def lines(g):
            for i in range(8):
                r = g * 8 + i
                even = rows_ref[pl.ds(lists_ref[peer, 0, r], 1), :]
                odd = rows_ref[pl.ds(lists_ref[peer, 1, r], 1), :]
                target[slot, pl.ds(r, 1), :] = jnp.where(left, even, odd)

        for_range(0, cap // 8, lines)

    return collect


def forward(
    n, cap, tail_rows, row_ids, lengths, counts, mask, labels, row_home, table, mat_home,
    experts_m, experts_v, towers_m, towers_v, gates_m, gates_v, small_m, small_v,
):
    samples, tables, bag = row_ids.shape
    rows_dev, width = table.shape
    tasks = labels.shape[1]
    experts, features, hidden = experts_m.shape
    per_table = row_home.shape[1] // n
    block_rows = rows_dev // (tables * per_table)
    levels = early_levels(n)
    sizes = (n, cap, tables, bag, tasks, experts, per_table, block_rows, rows_dev)
    ids = row_ids.transpose(1, 2, 0).reshape(tables * bag, samples)
    vmem = pl.BlockSpec(memory_space=pltpu.VMEM)
    smem = pl.BlockSpec(memory_space=pltpu.SMEM)
    hbm = pl.BlockSpec(memory_space=pl.ANY)
    slots = jax.ShapeDtypeStruct((tables * bag, LANES), I32)
    lists = jax.ShapeDtypeStruct((n, 2, LANES), I32)
    count = len(plan(n, experts, features, tail_rows))
    small = pltpu.VMEM((n, 8, LANES), F32)
    numbers = pltpu.VMEM((n, 8, LANES), I32)
    slot_scratch = pltpu.VMEM((tables * bag, LANES), I32)
    dma = pltpu.SemaphoreType.DMA((n,))
    hops = pltpu.SemaphoreType.DMA((count, n.bit_length()))
    return pl.pallas_call(
        functools.partial(forward_kernel, sizes),
        out_shape=(
            jax.ShapeDtypeStruct((8, LANES), F32), slots, lists, lists, lists,
            jax.ShapeDtypeStruct((8, LANES), I32), jax.ShapeDtypeStruct((n + 1, cap, LANES), F32),
            jax.ShapeDtypeStruct((count, 2, 8 * n >> levels, hidden), F32),
        ),
        in_specs=[vmem, vmem, smem, vmem, vmem, vmem, hbm, smem, hbm, hbm] + [vmem] * 6,
        out_specs=(vmem,) * 8,
        scratch_shapes=[
            small, small, numbers, numbers,
            pltpu.VMEM((2, 4 * n, LANES), F32), pltpu.VMEM((LANES, LANES), F32),
            slot_scratch, slot_scratch, slot_scratch,
            pltpu.SMEM((n, 2, LANES), I32), pltpu.VMEM((rows_dev + 8, LANES), F32), pltpu.VMEM((n, cap, LANES), F32),
            pltpu.VMEM((2, tail_rows, hidden), F32), pltpu.VMEM((count, 2, 4 * n, hidden), F32),
            pltpu.VMEM((width, rows_dev), F32),
        ]
        + [pltpu.VMEM((count, 2, 4 * n >> i, hidden), F32) for i in range(levels - 1)]
        + [dma] * 6 + [hops] * 2 + [pltpu.SemaphoreType.DMA((count, 2)), pltpu.SemaphoreType.DMA((2,))],
        compiler_params=pltpu.CompilerParams(collective_id=0, has_side_effects=True, vmem_limit_bytes=56 * 2**20),
        name="forward",
    )(
        ids, lengths.T, counts, mask.reshape(1, samples), labels.T, row_home, table.T, mat_home, experts_m, experts_v,
        towers_m.transpose(0, 2, 1), towers_v.transpose(0, 2, 1), gates_m.transpose(0, 2, 1), gates_v.transpose(0, 2, 1),
        small_m, small_v,
    )


def backward_kernel(
    sizes, lists_ref, stat_ref, items_ref, fields_ref, pooled_ref, moments_ref, experts_hbm, gates_ref, towers_ref, small_ref,
    lines_ref, experts_out, tail_out, *rest,
):
    n, cap, tail_rows = sizes
    levels, early = n.bit_length() - 1, early_levels(n)
    stages, rest = list(rest[:levels]), rest[levels:]
    late_stages, rest = [moments_ref] + list(rest[: levels - early]), rest[levels - early :]
    grads, tail, tail_w, news, rows_ref, side, rows_out, experts_ref = rest[:8]
    send_c, recv_c, sends, receives, send_m, recv_m, send_w, recv_w, local = rest[8:]
    experts, features, hidden = experts_ref.shape
    tasks, tower, _ = towers_ref.shape
    chains = plan(n, experts, features, tail_rows)
    unit = 8 * n
    me = lax.axis_index("dev")
    greet_all(n, me)
    weights_copy = pltpu.make_async_copy(experts_hbm, experts_ref, local.at[0])
    weights_copy.start()
    await_all(n)

    def late_hop(c, i):
        order = chains[c][2]
        bit = order[early + i]
        half = late_stages[i + 1].shape[2]
        at = rows_at((1 - bit_of(me, bit)) * half, half)
        return pltpu.make_async_remote_copy(
            src_ref=late_stages[i].at[c, :, at],
            dst_ref=late_stages[i + 1].at[c],
            send_sem=send_m.at[c, i],
            recv_sem=recv_m.at[c, i],
            device_id=(me ^ bit,),
            device_id_type=MESH,
        )

    chosen = owner_side(me, n, items_ref, experts, tasks, tower)

    def late_settle(i):
        for c, chain in enumerate(chains):
            late_hop(c, i).wait()
            half = late_stages[i + 1].shape[2]
            mine = rows_at(bit_of(me, chain[2][early + i]) * half, half)
            flag = chosen(chain, early + i, half)
            for w in range(2):
                late_stages[i + 1][c, w] = jnp.where(flag, late_stages[i][c, w, mine, :], late_stages[i + 1][c, w])
            if i + 1 < levels - early:
                late_hop(c, i + 1).start()

    for c in range(len(chains)):
        late_hop(c, 0).start()
    lines_ref[n] = jnp.zeros((cap, LANES), F32)
    fill_tail(tail_w, towers_ref, gates_ref, small_ref)

    def hop(c, i):
        array, first, order, _ = chains[c]
        source = tail if array == experts else grads.at[array]
        return halving(me, source.at[first : first + unit], stages, sends, receives, c, order, i)

    def settle(c, i):
        array, first, order, _ = chains[c]
        hop(c, i).wait()
        half = stages[i].shape[1]
        at = bit_of(me, order[i]) * half
        if i > 0:
            kept = stages[i - 1][c, rows_at(at, half), :]
        elif array == experts:
            kept = tail[rows_at(first + at, half), :]
        else:
            kept = grads[array, rows_at(first + at, half), :]
        stages[i][c] += kept
        if i + 1 < levels:
            hop(c, i + 1).start()

    def region(c, i):
        array, first, order, _ = chains[c]
        at = rows_at(first + start_of(me, order[: i + 1], unit), unit >> (i + 1))
        return tail_out.at[:, at] if array == experts else experts_out.at[array, :, at]

    def doubling(c, i):
        return pltpu.make_async_remote_copy(
            src_ref=news.at[c] if i == levels - 1 else region(c, i),
            dst_ref=region(c, i),
            send_sem=send_w.at[c, i],
            recv_sem=recv_w.at[c, i],
            device_id=(me ^ chains[c][2][i],),
            device_id_type=MESH,
        )

    def place(c):
        return pltpu.make_async_copy(news.at[c], region(c, levels - 1), local.at[c])

    def renew(c):
        array, first, order, _ = chains[c]
        at = rows_at(first + start_of(me, order, unit), 8)
        weight = tail_w[at, :] if array == experts else experts_ref[array, at, :]
        moment = late_stages[-1]
        grad = stages[-1][c]
        news[c, 0] = stepped(weight, *moments(moment[c, 0], moment[c, 1], grad))
        news[c, 1] = grad
        place(c).start()

    steps = len(set(chain[3] for chain in chains)) + 2 * levels

    def step(s):
        for c, chain in enumerate(chains):
            j = s - chain[3] // 2
            if 0 <= j < levels:
                settle(c, j)
            if j == levels - 1:
                renew(c)
                doubling(c, levels - 1).start()
            i = 2 * levels - 2 - j
            if i == levels - 2:
                place(c).wait()
            if 0 <= i < levels - 1:
                doubling(c, i + 1).wait()
                doubling(c, i).start()
            if j == 2 * levels - 1:
                doubling(c, 0).wait()

    def ready(array):
        for c, chain in enumerate(chains):
            if chain[0] == array:
                hop(c, 0).start()
        if array == experts:
            late_settle(0)

    weights_copy.wait()
    dense_pass(
        ready, stat_ref, fields_ref, pooled_ref, experts_ref, tail_w, towers_ref, small_ref, grads, tail, rows_ref, side
    )
    collect = collector(cap, lists_ref, rows_ref)

    def collect_and_send(i):
        k = n - i
        collect(me ^ k, rows_out, me ^ k)
        exchange(n, me, rows_out, lines_ref, send_c, recv_c, k).start()

    sent = 0
    for s in range(steps):
        goal = min(n - 1, sent + (16 if s == 0 else 4))
        if goal > sent:
            for_range(sent + 1, goal + 1, collect_and_send)
            sent = goal
        if 2 <= s < 2 + levels - early - 1:
            late_settle(s - 2 + 1)
        step(s)
    collect(me, lines_ref, me)
    for_range(1, n, lambda k: exchange(n, me, rows_out, lines_ref, send_c, recv_c, k).wait())


def backward(n, cap, tail_rows, lists, stat, items, fields, pooled, moment_slices, experts_w, gates_w, towers_w, small):
    experts, features, hidden = experts_w.shape
    samples = fields.shape[1]
    levels, early = n.bit_length() - 1, early_levels(n)
    count = len(plan(n, experts, features, tail_rows))
    vmem = pl.BlockSpec(memory_space=pltpu.VMEM)
    smem = pl.BlockSpec(memory_space=pltpu.SMEM)
    dma = pltpu.SemaphoreType.DMA((n,))
    hops = pltpu.SemaphoreType.DMA((count, levels))
    return pl.pallas_call(
        functools.partial(backward_kernel, (n, cap, tail_rows)),
        out_shape=(
            jax.ShapeDtypeStruct((n + 1, cap, LANES), F32),
            jax.ShapeDtypeStruct((experts, 2, features, hidden), F32),
            jax.ShapeDtypeStruct((2, tail_rows, hidden), F32),
        ),
        in_specs=[smem, smem, smem] + [vmem] * 3 + [pl.BlockSpec(memory_space=pl.ANY)] + [vmem] * 3,
        out_specs=(vmem, pl.BlockSpec(memory_space=pl.ANY), vmem),
        scratch_shapes=[pltpu.VMEM((count, 4 * n >> i, hidden), F32) for i in range(levels)]
        + [pltpu.VMEM((count, 2, 8 * n >> (early + i + 1), hidden), F32) for i in range(levels - early)]
        + [
            pltpu.VMEM((experts, features, hidden), F32), pltpu.VMEM((tail_rows, hidden), F32),
            pltpu.VMEM((tail_rows, hidden), F32), pltpu.VMEM((count, 2, 8, hidden), F32),
            pltpu.VMEM((features // LANES * samples + 8, LANES), F32), pltpu.VMEM((samples, samples), F32),
            pltpu.VMEM((n, cap, LANES), F32), pltpu.VMEM((experts, features, hidden), F32),
        ]
        + [dma] * 2 + [hops] * 6 + [pltpu.SemaphoreType.DMA((count,))],
        compiler_params=pltpu.CompilerParams(collective_id=1, has_side_effects=True, vmem_limit_bytes=56 * 2**20),
        name="backward",
    )(lists, stat, items, fields, pooled, moment_slices, experts_w, gates_w, towers_w, small)


def close_kernel(
    sizes,
    owned_ref, pairs_ref, lines_ref, table_ref, row_first_ref, row_second_ref,
    whole_ref, first_ref, second_ref, tail_ref, towers_m_ref, towers_v_ref, gates_m_ref, gates_v_ref, small_m_ref, small_v_ref,
    table_new_ref, row_first_new_ref, row_second_new_ref, new_ref, low_ref, first_new_ref, second_new_ref,
    towers_ref, towers_low_ref, towers_m_new_ref, towers_v_new_ref, gates_ref, gates_m_new_ref, gates_v_new_ref,
    small_ref, small_m_new_ref, small_v_new_ref, loss_ref,
    sums_even, sums_odd,
):
    n, cap, experts, first_steps, steps_each = sizes
    step = pl.program_id(0)
    width, block = table_ref.shape
    half = block // 2
    rows = sums_even.shape[0] - 8

    @pl.when(step == 0)
    def _():
        def clear(i):
            at = pl.ds(pl.multiple_of(i * half, half), half)
            sums_even[at, :] = jnp.zeros((half, LANES), F32)
            sums_odd[at, :] = jnp.zeros((half, LANES), F32)

        for_range(0, rows // half, clear)
        finish_tail(
            owned_ref, experts, tail_ref, towers_m_ref, towers_v_ref, gates_m_ref, gates_v_ref, small_m_ref, small_v_ref,
            towers_ref, towers_low_ref, towers_m_new_ref, towers_v_new_ref, gates_ref, gates_m_new_ref, gates_v_new_ref,
            small_ref, small_m_new_ref, small_v_new_ref, loss_ref,
        )

    @pl.when(step < first_steps)
    def _():
        e = lax.div(step, steps_each)
        new = whole_ref[0, 0]
        new_ref[0] = new
        low_ref[0] = new.astype(BF16)

        @pl.when(owned_ref[e] == 1)
        def _():
            first_new_ref[0], second_new_ref[0] = moments(first_ref[0], second_ref[0], whole_ref[0, 1])

        @pl.when(owned_ref[e] != 1)
        def _():
            first_new_ref[...] = jnp.zeros_like(first_new_ref)
            second_new_ref[...] = jnp.zeros_like(second_new_ref)

        def source(s):
            count = jnp.minimum(jnp.maximum(pairs_ref[s, 0, LANES - 1], pairs_ref[s, 1, LANES - 1]), cap)

            def add(g):
                for i in range(8):
                    r = g * 8 + i
                    line = lines_ref[pl.ds(s * cap + r, 1), :]
                    sums_even[pl.ds(pairs_ref[s, 0, r], 1), :] += line
                    sums_odd[pl.ds(pairs_ref[s, 1, r], 1), :] += line

            for_range(0, (count + 7) // 8, add)

        for_range(step * n // first_steps, (step + 1) * n // first_steps, source)

    @pl.when(step >= first_steps)
    def _():
        left = iota((LANES, LANES), 1) < width
        for b in range(half // LANES):
            at = pl.ds(pl.multiple_of((step - first_steps) * half + b * LANES, LANES), LANES)
            both = jnp.where(left, sums_even[at, :], sums_odd[at, :]).T
            for parity in range(2):
                here = slice(parity * half + b * LANES, parity * half + (b + 1) * LANES)
                grad = both[parity * width : (parity + 1) * width]
                first = BETA_ONE * row_first_ref[:, here] + (1.0 - BETA_ONE) * grad
                mean = jnp.sum(grad * grad, axis=0, keepdims=True) * (1.0 / width)
                second = BETA_TWO * row_second_ref[:, here] + (1.0 - BETA_TWO) * mean
                rate = (RATE_ROWS / (1.0 - BETA_ONE**STEP)) / (
                    jnp.sqrt(second * (1.0 / (1.0 - BETA_TWO**STEP))) + EPSILON
                )
                old = table_ref[:, here]
                table_new_ref[:, here] = old - (first * rate + (RATE_ROWS * DECAY) * old)
                row_first_new_ref[:, here] = first
                row_second_new_ref[:, here] = second


def finish_tail(
    owned_ref, experts, tail_ref, towers_m_ref, towers_v_ref, gates_m_ref, gates_v_ref, small_m_ref, small_v_ref,
    towers_ref, towers_low_ref, towers_m_new_ref, towers_v_new_ref, gates_ref, gates_m_new_ref, gates_v_new_ref,
    small_ref, small_m_new_ref, small_v_new_ref, loss_ref,
):
    tasks, tower, hidden = towers_ref.shape
    count = gates_ref.shape[1]

    def mine(item, pair):
        own = jnp.full((1, 1), owned_ref[item], I32) == 1
        return [jnp.where(own, x, 0.0) for x in pair]

    for k in range(tasks):
        at = slice(k * tower, (k + 1) * tower)
        towers_ref[k] = tail_ref[0, at]
        towers_low_ref[k] = tail_ref[0, at].astype(BF16)
        towers_m_new_ref[k], towers_v_new_ref[k] = mine(
            experts + tasks + k, moments(towers_m_ref[k], towers_v_ref[k], tail_ref[1, at])
        )
        for part in range(2):
            row = tasks * tower + part * GAP + k * count
            at = slice(row, row + count)
            to = slice(part * hidden, (part + 1) * hidden)
            gates_ref[k, :, to] = tail_ref[0, at]
            gates_m_new_ref[k, :, to], gates_v_new_ref[k, :, to] = mine(
                experts + k, moments(gates_m_ref[k, :, to], gates_v_ref[k, :, to], tail_ref[1, at])
            )
    base = tasks * tower + 2 * GAP
    size = small_ref.shape[1]
    for i in range(-(-size // hidden)):
        last = min(size, (i + 1) * hidden)
        to = slice(i * hidden, last)
        line = slice(0, last - i * hidden)
        small_ref[0:1, to] = tail_ref[0, base + i : base + i + 1, line]
        small_m_new_ref[0:1, to], small_v_new_ref[0:1, to] = mine(
            experts + 2 * tasks,
            moments(small_m_ref[0:1, to], small_v_ref[0:1, to], tail_ref[1, base + i : base + i + 1, line]),
        )
    loss_ref[...] = tail_ref[1, base + 8 : base + 9, 0:LANES]


def close(
    n, cap, table_rows, pairs, lines, table, table_m, table_v,
    owned, whole, tail, experts_m, experts_v, towers_m, towers_v, gates_m, gates_v, small_m, small_v,
):
    rows_dev, width = table.shape
    experts, features, hidden = experts_m.shape
    block = 2 * table_rows
    rows = 256
    steps_each = features // rows
    first_steps = experts * steps_each
    update_steps = rows_dev // block

    def late(i, *_):
        return (0, jnp.maximum(i - first_steps, 0))

    def place(i):
        i = jnp.minimum(i, first_steps - 1)
        return lax.div(i, steps_each), lax.rem(i, steps_each)

    def here(i, owned):
        e, b = place(i)
        return e, b, 0

    def only_owner(i, owned):
        e, b = place(i)
        return e, jnp.where(owned[e] == 1, b, 0), 0

    def both(i, owned):
        e, b = place(i)
        return e, 0, b, 0

    wide, thin = pl.BlockSpec((width, block), late), pl.BlockSpec((1, block), late)
    out_block, owners = pl.BlockSpec((1, rows, hidden), here), pl.BlockSpec((1, rows, hidden), only_owner)

    def full(x):
        return pl.BlockSpec(x.shape, lambda i, owned: (0,) * len(x.shape))

    sums = pltpu.VMEM((rows_dev // 2 + 8, LANES), F32)
    lines = lines.reshape((n + 1) * cap, LANES)
    towers = jax.ShapeDtypeStruct(towers_m.shape, F32)
    gates = jax.ShapeDtypeStruct(gates_m.shape, F32)
    small = jax.ShapeDtypeStruct(small_m.shape, F32)
    tail_shapes = (
        towers, jax.ShapeDtypeStruct(towers_m.shape, BF16), towers, towers, gates, gates, gates, small, small, small,
        jax.ShapeDtypeStruct((1, LANES), F32),
    )
    dense_shape = jax.ShapeDtypeStruct(experts_m.shape, F32)
    rows_shape = jax.ShapeDtypeStruct((width, rows_dev), F32)
    out_shape = (
        rows_shape, rows_shape, jax.ShapeDtypeStruct((1, rows_dev), F32),
        dense_shape, jax.ShapeDtypeStruct(experts_m.shape, BF16), dense_shape, dense_shape,
    ) + tail_shapes
    table_new, first_new, second_new, *others = pl.pallas_call(
        functools.partial(close_kernel, (n, cap, experts, first_steps, steps_each)),
        grid_spec=pltpu.PrefetchScalarGridSpec(
            num_scalar_prefetch=1,
            grid=(first_steps + update_steps,),
            in_specs=[
                pl.BlockSpec(memory_space=pltpu.SMEM), full(lines), wide, wide, thin,
                pl.BlockSpec((1, 2, rows, hidden), both), owners, owners,
                full(tail), full(towers_m), full(towers_v), full(gates_m), full(gates_v), full(small_m), full(small_v),
            ],
            out_specs=[wide, wide, thin] + [out_block] * 4 + [full(x) for x in tail_shapes],
            scratch_shapes=[sums, sums],
        ),
        out_shape=out_shape,
        compiler_params=pltpu.CompilerParams(vmem_limit_bytes=58 * 2**20),
        name="close",
    )(
        owned, pairs, lines, table.T, table_m.T, table_v.reshape(1, rows_dev),
        whole, experts_m, experts_v, tail, towers_m, towers_v, gates_m, gates_v, small_m, small_v,
    )
    return (table_new.T, first_new.T, second_new.reshape(rows_dev)), others


def pool_kernel(nothing, tables, bag, pos_ref, lines_ref, pooled_ref):
    samples = pos_ref.shape[1]
    pooled_ref[...] = jnp.zeros_like(pooled_ref)
    left = iota((1, LANES), 1) < LANES // 2

    def sample(s):
        @pl.when(pos_ref[0, s] != nothing)
        def _():
            for q in range(tables // 2):
                sums = []
                for parity in range(2):
                    base = (2 * q + parity) * bag
                    total = lines_ref[pl.ds(pos_ref[base, s], 1), :]
                    for j in range(1, bag):
                        total = total + lines_ref[pl.ds(pos_ref[base + j, s], 1), :]
                    sums.append(total)
                pooled_ref[pl.ds(q * samples + s, 1), :] = jnp.where(left, sums[0], sums[1])

    for_range(0, samples, sample)


def pool(n, cap, tables, bag, pos, lines):
    samples = pos.shape[1]
    return pl.pallas_call(
        functools.partial(pool_kernel, n * cap, tables, bag),
        out_shape=jax.ShapeDtypeStruct((tables // 2 * samples, LANES), F32),
        in_specs=[pl.BlockSpec(memory_space=pltpu.SMEM), pl.BlockSpec(memory_space=pltpu.VMEM)],
        out_specs=pl.BlockSpec(memory_space=pltpu.VMEM),
        compiler_params=pltpu.CompilerParams(vmem_limit_bytes=24 * 2**20),
        name="pool",
    )(pos, lines.reshape((n + 1) * cap, LANES))


def split2(x):
    high = x.astype(BF16)
    return high, (x - high.astype(F32)).astype(BF16)


def dot3(a, b, dims=NN):
    count = a[0].shape[0]
    if count > LANES:
        return dot(a[0], b[0], dims) + dot(a[0], b[1], dims) + dot(a[1], b[0], dims)
    both = dot(jnp.concatenate(a, axis=0), b[0], dims)
    return both[:count] + both[count:] + dot(a[0], b[1], dims)


def sigmoid(x):
    return 1.0 / (1.0 + jnp.exp(-x))


def dense_pass(
    ready, stat_ref, fields_ref, pooled_ref, experts_ref, tail_w, towers_ref, small_ref, grads, tail, rows_ref, side
):
    samples = fields_ref.shape[1]
    experts, features, hidden = experts_ref.shape
    tasks, tower, _ = towers_ref.shape
    tail[...] = jnp.zeros_like(tail)

    def put_tail(row, value):
        tail[row : row + value.shape[0], :] = value

    start = experts * hidden
    tower_at = start
    weight_at = start + tasks * tower
    bias_at = weight_at + tasks * tower
    side[0:8, :] = fields_ref[...]
    side[8:, :] = jnp.zeros((samples - 8, samples), F32)
    by_sample = side[...].T
    weight = by_sample[:, tasks : tasks + 1]
    scale = weight / stat_ref[0].astype(F32)
    x = jnp.concatenate([pooled_ref[q * samples : (q + 1) * samples] for q in range(features // LANES)], axis=1)
    x2 = split2(x)
    at = tasks * tower
    gate_w = jnp.concatenate([tail_w[at + k * GAP : at + k * GAP + tasks * experts, :] for k in range(2)], axis=1)
    gate_w2 = split2(gate_w)
    gate_logits = dot3(x2, gate_w2, NT)
    pres, sigs, hids = [], [], []
    for e in range(experts):
        pre = dot3(x2, split2(experts_ref[e])) + small_ref[0:1, e * hidden : (e + 1) * hidden]
        sig = sigmoid(pre)
        pres.append(pre)
        sigs.append(sig)
        hids.append(pre * sig)
    dhids = [jnp.zeros((samples, hidden), F32) for _ in range(experts)]
    dgate_logits = []
    loss = jnp.zeros((samples, 1), F32)
    tower_bias_grads, out_weight_grads, task_bias_grads = [], [], []
    for k in range(tasks):
        logits = [gate_logits[:, k * experts + e : k * experts + e + 1] for e in range(experts)]
        top = functools.reduce(jnp.maximum, logits)
        powers = [jnp.exp(v - top) for v in logits]
        whole = functools.reduce(jnp.add, powers)
        gates = [v / whole for v in powers]
        mix = functools.reduce(jnp.add, [gates[e] * hids[e] for e in range(experts)])
        mix2 = split2(mix)
        tower2 = split2(towers_ref[k])
        at = tower_at + k * tower
        pre = dot3(mix2, tower2, NT) + small_ref[0:1, at : at + tower]
        sig = sigmoid(pre)
        zed = pre * sig
        at = weight_at + k * tower
        out_weight = small_ref[0:1, at : at + tower]
        logit = jnp.sum(zed * out_weight, axis=1, keepdims=True) + small_ref[0:1, bias_at + k : bias_at + k + 1]
        label = by_sample[:, k : k + 1]
        softplus = jnp.maximum(logit, 0.0) + jnp.log1p(jnp.exp(-jnp.abs(logit)))
        loss = loss + weight * (softplus - label * logit)
        dlogit = scale * (sigmoid(logit) - label)
        task_bias_grads.append(jnp.sum(dlogit, axis=0, keepdims=True))
        out_weight_grads.append(jnp.sum(dlogit * zed, axis=0, keepdims=True))
        dpre = dlogit * out_weight * (sig * (1.0 + pre * (1.0 - sig)))
        tower_bias_grads.append(jnp.sum(dpre, axis=0, keepdims=True))
        dpre2 = split2(dpre)
        put_tail(k * tower, dot3(split2(dpre.T), mix2))
        dmix = dot3(dpre2, tower2)
        dgates = [jnp.sum(dmix * hids[e], axis=1, keepdims=True) for e in range(experts)]
        mean = functools.reduce(jnp.add, [gates[e] * dgates[e] for e in range(experts)])
        for e in range(experts):
            dgate_logits.append(gates[e] * (dgates[e] - mean))
            dhids[e] = dhids[e] + gates[e] * dmix
    lane = iota((samples, LANES), 1)
    dgl = jnp.zeros((samples, LANES), F32)
    for i, v in enumerate(dgate_logits):
        dgl = jnp.where(lane == i, v, dgl)
    count = tasks * experts
    dgl_t2 = split2(dgl.T[0:16])
    dgates_w = dot3(dgl_t2, x2)
    tail_at = tasks * tower
    put_tail(tail_at, dgates_w[:, :hidden])
    put_tail(tail_at + GAP, dgates_w[:, hidden:])
    expert_bias_grads, dpres = [], []
    for e in range(experts):
        dpre = dhids[e] * (sigs[e] * (1.0 + pres[e] * (1.0 - sigs[e])))
        expert_bias_grads.append(jnp.sum(dpre, axis=0, keepdims=True))
        dpres.append(split2(dpre))
    small_at = tail_at + 2 * GAP
    pad = jnp.zeros((1, 2 * hidden - 2 * tasks * tower - tasks), F32)
    line = jnp.concatenate(tower_bias_grads + out_weight_grads + task_bias_grads + [pad], axis=1)
    loss_row = jnp.where(iota((1, hidden), 1) == 0, jnp.sum(loss, axis=0, keepdims=True), 0.0)
    for e in range(experts):
        put_tail(small_at + e, expert_bias_grads[e])
    for i in range(line.shape[1] // hidden):
        put_tail(small_at + experts + i, line[:, i * hidden : (i + 1) * hidden])
    put_tail(small_at + 8, loss_row)
    ready(experts)
    x_t2 = split2(x.T)
    for e in range(experts):
        grads[e] = dot3(x_t2, dpres[e])
        ready(e)
    dx = dot3(split2(dgl[:, :count]), gate_w2)
    for e in range(experts):
        dx = dx + dot3(dpres[e], split2(experts_ref[e]), NT)
    for q in range(features // LANES):
        rows_ref[q * samples : (q + 1) * samples, :] = dx[:, q * LANES : (q + 1) * LANES]
    rows_ref[features // LANES * samples :, :] = jnp.zeros((8, LANES), F32)


def moments(first, second, grad):
    return (
        BETA_ONE * first + (1.0 - BETA_ONE) * grad,
        BETA_TWO * second + (1.0 - BETA_TWO) * grad * grad,
    )


def stepped(weight, first_new, second_new):
    first_hat = first_new / (1.0 - BETA_ONE**STEP)
    second_hat = second_new / (1.0 - BETA_TWO**STEP)
    return weight - RATE_DENSE * (first_hat / (jnp.sqrt(second_hat) + EPSILON) + DECAY * weight)


def all_sum(tree, axis):
    n = lax.axis_size(axis)
    bit = 1
    while bit < n:
        pairs = [(i, i ^ bit) for i in range(n)]
        tree = jax.tree.map(lambda x: x + lax.ppermute(x, axis, pairs), tree)
        bit *= 2
    return tree


def from_root(block, axis, source):
    block = jnp.where(lax.axis_index(axis) == source, block, jnp.zeros_like(block))
    return all_sum(block, axis)


def dense_forward(params, pooled, labels, weights):
    experts_w, gates_w, towers_w, small = params
    n_experts, _, hidden = experts_w.shape
    tasks, _, tower = towers_w.shape
    start = n_experts * hidden
    expert_bias = small[:start].reshape(n_experts, hidden)
    tower_bias = small[start : start + tasks * tower].reshape(tasks, tower)
    start = start + tasks * tower
    out_weight = small[start : start + tasks * tower].reshape(tasks, tower)
    task_bias = small[start + tasks * tower :]
    hidden_act = jax.nn.silu(
        jnp.einsum("si,eih->seh", pooled, experts_w, precision=lax.Precision.HIGHEST) + expert_bias
    )
    gate = jax.nn.softmax(jnp.einsum("si,kie->ske", pooled, gates_w, precision=lax.Precision.HIGHEST), axis=-1)
    mixed = jnp.einsum("ske,seh->skh", gate, hidden_act, precision=lax.Precision.HIGHEST)
    zed = jax.nn.silu(jnp.einsum("skh,khc->skc", mixed, towers_w, precision=lax.Precision.HIGHEST) + tower_bias)
    logit = jnp.sum(zed * out_weight, axis=-1) + task_bias
    losses = jax.nn.softplus(logit) - labels * logit
    return jnp.sum(weights[:, None] * losses)


def adam_step(weight, first, second, grad, rate):
    first_new = BETA_ONE * first + (1.0 - BETA_ONE) * grad
    second_new = BETA_TWO * second + (1.0 - BETA_TWO) * grad * grad
    first_hat = first_new / (1.0 - BETA_ONE**STEP)
    second_hat = second_new / (1.0 - BETA_TWO**STEP)
    weight_new = weight - rate * (first_hat / (jnp.sqrt(second_hat) + EPSILON) + DECAY * weight)
    return (weight_new, first_new, second_new)


def plain_step(
    row_ids,
    lengths,
    counts,
    mask,
    labels,
    row_home,
    mat_home,
    table,
    table_m,
    table_v,
    experts_w,
    gates_w,
    towers_w,
    small_params,
    experts_m,
    experts_v,
    gates_m,
    gates_v,
    towers_m,
    towers_v,
    small_m,
    small_v,
):
    devices = lax.axis_size("dev")
    myself = lax.axis_index("dev")
    samples, tables, bag_slots = row_ids.shape
    rows_dev, width = table.shape
    per_table = row_home.shape[1] // devices
    block_rows = rows_dev // (tables * per_table)
    slots = samples * tables * bag_slots
    average = slots // devices
    capacity = average + average // 2
    present = jnp.arange(samples) < counts[0]
    weights = jnp.where(present & (mask == 1), 1.0, 0.0).astype(jnp.float32)
    live = present[:, None, None] & (jnp.arange(bag_slots)[None, None, :] < lengths[:, :, None])
    table_of = jnp.broadcast_to(jnp.arange(tables)[None, :, None], row_ids.shape)
    homes = row_home[table_of, row_ids // block_rows]
    owners = (homes // per_table).reshape(-1)
    local_rows = (
        (table_of * per_table + homes % per_table) * block_rows + row_ids % block_rows
    ).reshape(-1)
    live_flat = live.reshape(-1)
    live_float = live_flat.astype(jnp.float32)
    targets = jnp.where(live_flat, owners, devices)
    order = jnp.argsort(targets, stable=True)
    sorted_targets = targets[order]
    starts = jnp.searchsorted(sorted_targets, jnp.arange(devices + 1), side="left")
    sorted_rank = jnp.arange(slots, dtype=jnp.int32) - starts[sorted_targets]
    slot_rank = jnp.zeros(slots, jnp.int32).at[order].set(sorted_rank)
    slot_rank = jnp.where(live_flat, slot_rank, 0)
    requests = (
        jnp.zeros((devices, capacity), jnp.int32)
        .at[targets, slot_rank]
        .set(local_rows, mode="drop")
    )
    asked_rows = lax.all_to_all(requests, "dev", split_axis=0, concat_axis=0, tiled=True)
    found = table[asked_rows]
    arrived = lax.all_to_all(found, "dev", split_axis=0, concat_axis=0, tiled=True)
    safe_owner = jnp.minimum(owners, devices - 1)
    slot_rows = arrived[safe_owner, slot_rank] * live_float[:, None]
    pooled = jnp.sum(slot_rows.reshape(samples, tables, bag_slots, width), axis=2).reshape(
        samples, tables * width
    )
    params = (experts_w, gates_w, towers_w, small_params)
    local_loss, pull = jax.vjp(
        lambda dense, features: dense_forward(dense, features, labels, weights), params, pooled
    )
    loss_sum, weight_sum = all_sum((local_loss, jnp.sum(weights)), "dev")
    local_grads, pooled_grad = pull(1.0 / weight_sum)
    slot_grads = (
        jnp.broadcast_to(
            pooled_grad.reshape(samples, tables, 1, width), (samples, tables, bag_slots, width)
        ).reshape(slots, width)
        * live_float[:, None]
    )
    outgoing = (
        jnp.zeros((devices, capacity, width), jnp.float32)
        .at[targets, slot_rank]
        .set(slot_grads, mode="drop")
    )
    incoming = lax.all_to_all(outgoing, "dev", split_axis=0, concat_axis=0, tiled=True)
    grad_table = (
        jnp.zeros((rows_dev, width), jnp.float32)
        .at[asked_rows.reshape(-1)]
        .add(incoming.reshape(-1, width))
    )
    table_m_new = BETA_ONE * table_m + (1.0 - BETA_ONE) * grad_table
    table_v_new = BETA_TWO * table_v + (1.0 - BETA_TWO) * jnp.mean(grad_table * grad_table, axis=1)
    first_hat = table_m_new / (1.0 - BETA_ONE**STEP)
    second_hat = table_v_new / (1.0 - BETA_TWO**STEP)
    table_new = table - RATE_ROWS * (
        first_hat / (jnp.sqrt(second_hat)[:, None] + EPSILON) + DECAY * table
    )
    grad_experts, grad_gates, grad_towers, grad_small = local_grads
    grad_experts, grad_gates, grad_towers, grad_small = all_sum(
        (grad_experts, grad_gates, grad_towers, grad_small), "dev"
    )
    kinds = (
        (experts_w, experts_m[0], experts_v[0], grad_experts),
        (gates_w, gates_m[0], gates_v[0], grad_gates),
        (towers_w, towers_m[0], towers_v[0], grad_towers),
        (small_params[None], small_m, small_v, grad_small[None]),
    )
    finals = []
    first_outs = []
    second_outs = []
    base = 0
    for stack, firsts, seconds, grad in kinds:
        kind_weights = []
        kind_firsts = []
        kind_seconds = []
        for position in range(stack.shape[0]):
            owner_id = mat_home[base + position]
            is_owner = owner_id == myself
            weight_new, first_new, second_new = adam_step(
                stack[position], firsts[position], seconds[position], grad[position], RATE_DENSE
            )
            kind_firsts.append(jnp.where(is_owner, first_new, 0.0))
            kind_seconds.append(jnp.where(is_owner, second_new, 0.0))
            kept = jnp.where(is_owner, weight_new, stack[position])
            kind_weights.append(from_root(kept, "dev", owner_id))
        base = base + stack.shape[0]
        finals.append(jnp.stack(kind_weights))
        first_outs.append(jnp.stack(kind_firsts)[None])
        second_outs.append(jnp.stack(kind_seconds)[None])
    experts_new, gates_new, towers_new, small_stack = finals
    small_new = small_stack[0]
    return (
        loss_sum,
        weight_sum,
        table_new,
        table_m_new,
        table_v_new,
        experts_new,
        gates_new,
        towers_new,
        small_new,
        first_outs[0],
        second_outs[0],
        first_outs[1],
        second_outs[1],
        first_outs[2],
        second_outs[2],
        first_outs[3][0],
        second_outs[3][0],
        experts_new.astype(jnp.bfloat16)[None],
        gates_new.astype(jnp.bfloat16)[None],
        towers_new.astype(jnp.bfloat16)[None],
        small_new.astype(jnp.bfloat16)[None],
    )


def per_device(*args):
    (
        row_ids, lengths, counts, mask, labels, row_home, mat_home, table, table_m, table_v,
        experts_w, gates_w, towers_w, small_params,
        experts_m, experts_v, gates_m, gates_v, towers_m, towers_v, small_m, small_v,
    ) = args
    n = lax.axis_size("dev")
    me = lax.axis_index("dev")
    samples, tables, bag = row_ids.shape
    rows_dev, width = table.shape
    cap = max(8, (samples * tables * bag // n * 11 // 32 + 7) // 8 * 8)
    experts, features, hidden = experts_w.shape
    tasks, _, tower = towers_w.shape
    tail_rows = -(-(tasks * tower + 2 * GAP + 16) // (8 * n)) * 8 * n
    fields, pos, mine, theirs, pairs, stat, lines, moment_slices = forward(
        n, cap, tail_rows, row_ids, lengths, counts, mask, labels, row_home, table, mat_home,
        experts_m[0], experts_v[0], towers_m[0], towers_v[0], gates_m[0], gates_v[0], small_m, small_v,
    )
    most, weight_count = stat[4, 0], stat[5, 0]

    def usual(fields, pos, mine, pairs, lines, moment_slices, weight_count, *args):
        (
            _, _, _, _, _, _, mat_home, table, table_m, table_v, experts_w, gates_w, towers_w, small_params,
            experts_m, experts_v, gates_m, gates_v, towers_m, towers_v, small_m, small_v,
        ) = args

        def turned(x):
            return x.transpose(0, 2, 1)

        gates_t, towers_t, small = turned(gates_w), turned(towers_w), small_params.reshape(1, -1)
        pooled = pool(n, cap, tables, bag, pos, lines)
        back, whole, tail = backward(
            n, cap, tail_rows, mine, weight_count[None], mat_home, fields, pooled, moment_slices,
            experts_w, gates_t, towers_t, small,
        )
        rows_new, (
            experts_new, experts_low, experts_m_new, experts_v_new,
            towers_new, towers_low, towers_m_new, towers_v_new, gates_new, gates_m_new, gates_v_new,
            small_new, small_m_new, small_v_new, loss,
        ) = close(
            n, cap, rows_dev // tables, pairs, back, table, table_m, table_v,
            (mat_home == me).astype(I32), whole, tail, experts_m[0], experts_v[0], turned(towers_m[0]), turned(towers_v[0]),
            turned(gates_m[0]), turned(gates_v[0]), small_m, small_v,
        )
        gates_new = turned(gates_new)
        small_new = small_new.reshape(-1)
        return (
            loss[0, 0], weight_count.astype(F32), *rows_new, experts_new, gates_new, turned(towers_new), small_new,
            experts_m_new[None], experts_v_new[None], turned(gates_m_new)[None], turned(gates_v_new)[None],
            turned(towers_m_new)[None], turned(towers_v_new)[None], small_m_new, small_v_new,
            experts_low[None], gates_new.astype(BF16)[None], turned(towers_low)[None], small_new.astype(BF16)[None],
        )

    def crowded(fields, pos, mine, pairs, lines, moment_slices, weight_count, *args):
        return plain_step(*args)

    return lax.cond(
        most <= cap, usual, crowded, fields, pos, mine, pairs, lines, moment_slices, weight_count, *args
    )


def solution(mesh):
    def split(dims):
        return P("dev", *(None,) * (dims - 1))

    by_device = split(4)
    return jax.shard_map(
        per_device,
        mesh=mesh,
        in_specs=(
            split(3), split(2), split(1), split(1), split(2), P(), P(), split(2), split(2), split(1),
            P(), P(), P(), P(),
        ) + (by_device,) * 6 + (split(2),) * 2,
        out_specs=(P(), P(), split(2), split(2), split(1), P(), P(), P(), P())
        + (by_device,) * 6 + (split(2),) * 2 + (by_device,) * 3 + (split(2),),
        check_vma=False,
    )
```

```python
import functools
import jax
import jax.numpy as jnp
from jax import lax
from jax.experimental import pallas as pl
from jax.experimental.pallas import tpu as pltpu
from jax.sharding import PartitionSpec as P

MESH = pl.DeviceIdType.MESH
F32, BF16, I32 = jnp.float32, jnp.bfloat16, jnp.int32
NN, NT, TN = (((1,), (0,)), ((), ())), (((1,), (1,)), ((), ())), (((0,), (0,)), ((), ()))
LANES = 128


def iota(shape, dim):
    return lax.broadcasted_iota(I32, shape, dim)


def dot(a, b, dims=NN):
    return lax.dot_general(a, b, dims, preferred_element_type=F32)


def split3(x):
    high = x.astype(BF16)
    rest = x - high.astype(F32)
    middle = rest.astype(BF16)
    low = (rest - middle.astype(F32)).astype(BF16)
    return high, middle, low


def greet_all(n, me):
    barrier = pltpu.get_barrier_semaphore()

    def signal(k, carry):
        pl.semaphore_signal(barrier, inc=1, device_id=(me ^ k,), device_id_type=MESH)
        return carry

    lax.fori_loop(1, n, signal, 0)


def await_all(n):
    pl.semaphore_wait(pltpu.get_barrier_semaphore(), n - 1)


def exchange(n, me, source, target, sends, receives, k):
    peer = me ^ k
    return pltpu.make_async_remote_copy(
        src_ref=source.at[peer],
        dst_ref=target.at[me],
        send_sem=sends.at[k],
        recv_sem=receives.at[k],
        device_id=(peer,),
        device_id_type=MESH,
    )


def for_range(low, high, body):
    def step(k, carry):
        body(k)
        return carry

    lax.fori_loop(low, high, step, 0)

STEP = 5
BETA_ONE = 0.9
BETA_TWO = 0.999
EPSILON = 1e-08
DECAY = 0.01
RATE_DENSE = 0.02
RATE_ROWS = 0.3
GAP = 16

def axis_orders(n):
    bits = [1 << i for i in range(n.bit_length() - 1)]
    core, rest = bits[:1], bits[1:]
    a = len(rest) // 3
    b = (len(rest) - a) // 2
    x, y, z = rest[:a], rest[a : a + b], rest[a + b :]
    return core + x + y + z, core + y + x + z, core + z + x + y, core + z + y + x


def early_levels(n):
    rest = n.bit_length() - 2
    a = rest // 3
    return 1 + a + (rest - a) // 2


def bit_of(me, bit):
    return lax.rem(lax.div(me, bit), 2)


def start_of(me, order, rows):
    start = 0
    for bit in order:
        rows = rows // 2
        start = start + bit_of(me, bit) * rows
    return start


def rows_at(start, count):
    return pl.ds(pl.multiple_of(start, 8), count)


def plan(n, experts, features, tail_rows):
    unit = 8 * n
    along_x, along_y, along_z, along_w = axis_orders(n)
    chains = []
    for k in range(features // unit):
        for e in range(experts):
            chains.append((e, k * unit, along_y if e % 2 else along_x, k))
    for k in range(tail_rows // unit):
        chains.append((experts, k * unit, along_w if k % 2 else along_z, k // 2))
    return chains


def halving(me, source, stages, sends, receives, c, order, i, lane=0):
    bit = order[i]
    before = source if i == 0 else stages[i - 1].at[c]
    target = stages[i].at[c]
    half = stages[i].shape[-2]
    at = rows_at((1 - bit_of(me, bit)) * half, half)
    if i == 0 and len(stages[0].shape) == 4:
        target = target.at[lane]
        lane_sem = lane * len(order)
    else:
        lane_sem = i
    return pltpu.make_async_remote_copy(
        src_ref=before.at[at] if len(before.shape) == 2 else before.at[:, at],
        dst_ref=target,
        send_sem=sends.at[c, lane_sem],
        recv_sem=receives.at[c, lane_sem],
        device_id=(me ^ bit,),
        device_id_type=MESH,
    )


def fill_tail(tail, towers, gates, small):
    tasks, tower, hidden = towers.shape
    count = gates.shape[1]
    size = small.shape[1]
    tail[...] = jnp.zeros_like(tail)
    tail[0 : tasks * tower, :] = towers[...].reshape(tasks * tower, hidden)
    for part in range(2):
        for k in range(tasks):
            at = tasks * tower + part * GAP + k * count
            tail[at : at + count, :] = gates[k][:, part * hidden : (part + 1) * hidden]
    at = tasks * tower + 2 * GAP
    for i in range(-(-size // hidden)):
        last = min(size, (i + 1) * hidden)
        tail[at + i : at + i + 1, 0 : last - i * hidden] = small[0:1, i * hidden : last]


def owner_side(me, n, items_ref, experts, tasks, tower):
    def chosen(chain, i, count):
        array, first, order, _ = chain
        bit = order[i]
        if array < experts:
            return bit_of(items_ref[array], bit) == bit_of(me, bit)
        towers = tasks * tower
        row = first + start_of(me, order[: i + 1], 8 * n) + iota((count, LANES), 0)
        item = lax.div(row, tower) + experts + tasks
        for part in range(2):
            at = towers + part * GAP
            item = jnp.where((row >= at) & (row < at + tasks * experts), experts + lax.div(row - at, experts), item)
        item = jnp.where(row >= towers + 2 * GAP, experts + 2 * tasks, item)
        home = jnp.zeros((count, LANES), I32)
        for k in range(experts, experts + 2 * tasks + 1):
            home = jnp.where(item == k, items_ref[k], home)
        return (bit_of(home, bit) == bit_of(me, bit))[:, :1]

    return chosen


def forward_kernel(
    sizes,
    ids_ref, lengths_ref, counts_ref, mask_ref, labels_ref, homes_ref, table_hbm, items_ref,
    experts_m_ref, experts_v_ref, towers_m_ref, towers_v_ref, gates_m_ref, gates_v_ref, small_m_ref, small_v_ref,
    fields_ref, pos_ref, mine_ref, theirs_ref, pairs_ref, stat_ref, lines_ref, moments_ref,
    outbox, inbox, message, replies, lists, field_scratch, owner_ref, rank_ref, local_ref, asked_smem, rows_ref, rows_out,
    tails, kept_ref, table_ref, *rest,
):
    n, cap, tables, bag, tasks, experts, per_table, block_rows, rows_dev = sizes
    levels = early_levels(n)
    stages = list(rest[: levels - 1]) + [moments_ref]
    send_a, recv_a, send_b, recv_b, send_c, recv_c, send_m, recv_m, keep_sem, sems = rest[levels - 1 :]
    chains = plan(n, experts, experts_m_ref.shape[1], tails.shape[1])
    unit = 8 * n
    rows = tables * bag
    me = lax.axis_index("dev")
    shift = lax.rem(me * 13, n)
    per_pair = LANES // n
    greet_all(n, me)
    table_copy = pltpu.make_async_copy(table_hbm, table_ref, sems.at[1])
    table_copy.start()
    table_of = lax.div(iota((rows, LANES), 0), bag)
    slot_of = lax.rem(iota((rows, LANES), 0), bag)
    expand = jnp.where(lax.div(iota((rows, tables), 0), bag) == iota((rows, tables), 1), 1.0, 0.0).astype(BF16)
    used = dot(expand, lengths_ref[...].astype(F32).astype(BF16)).astype(I32)
    present = iota((1, LANES), 1) < counts_ref[0]
    live = present & (slot_of < used)
    field_scratch[0:rows, :] = jnp.where(live, ids_ref[...], -1).astype(F32)
    field_scratch[rows : rows + tasks, :] = labels_ref[...]
    field_scratch[rows + tasks : rows + tasks + 1, :] = jnp.where(present & (mask_ref[...] == 1), 1.0, 0.0)
    field_scratch[rows + tasks + 1 :, :] = jnp.zeros((LANES - rows - tasks - 1, LANES), F32)
    row = iota((n * 8, LANES), 0)
    peer_of, piece = lax.div(row, 8), lax.rem(row, 8)
    column = iota((n * 8, LANES), 1)
    pick = jnp.where((piece < per_pair) & (column == piece * n + lax.rem(peer_of - shift + n, n)), 1.0, 0.0).astype(BF16)
    high, middle, low = split3(field_scratch[...])
    spread = dot(pick, high, NT) + dot(pick, middle, NT) + dot(pick, low, NT)
    outbox[...] = spread.reshape(n, 8, LANES)
    await_all(n)
    own_copy = pltpu.make_async_copy(outbox.at[me], inbox.at[me], sems.at[0])
    own_copy.start()
    for_range(1, n, lambda k: exchange(n, me, outbox, inbox, send_a, recv_a, k).start())
    fill_tail(tails.at[0], towers_m_ref, gates_m_ref, small_m_ref)
    fill_tail(tails.at[1], towers_v_ref, gates_v_ref, small_v_ref)

    def whole(c, w):
        array, first, _, _ = chains[c]
        source = tails.at[w] if array == experts else (experts_m_ref, experts_v_ref)[w].at[array]
        return source.at[first : first + unit]

    def hop(c, i, lane=0):
        return halving(me, whole(c, lane) if i == 0 else None, stages, send_m, recv_m, c, chains[c][2], i, lane)

    def keep(c, w):
        at = rows_at(bit_of(me, 1) * (unit // 2), unit // 2)
        return pltpu.make_async_copy(whole(c, w).at[at], kept_ref.at[c, w], keep_sem.at[c, w])

    for c in range(len(chains)):
        for w in range(2):
            hop(c, 0, w).start()
            keep(c, w).start()

    chosen = owner_side(me, n, items_ref, experts, tasks, towers_m_ref.shape[1])

    def settle(c, i):
        order = chains[c][2]
        for w in range(2 if i == 0 else 1):
            hop(c, i, w).wait()
            if i == 0:
                keep(c, w).wait()
        half = stages[i].shape[2]
        mine = rows_at(bit_of(me, order[i]) * half, half)
        flag = chosen(chains[c], i, half)
        for w in range(2):
            kept = kept_ref[c, w] if i == 0 else stages[i - 1][c, w, mine, :]
            stages[i][c, w] = jnp.where(flag, kept, stages[i][c, w])
        if i + 1 < levels:
            hop(c, i + 1).start()

    events = [(c, j) for t in range(16) for c, chain in enumerate(chains) for j in (t - chain[3],) if 0 <= j < levels]
    done = [0]

    def settle_some(count):
        for c, j in events[done[0] : done[0] + count]:
            settle(c, j)
        done[0] += count

    homes = homes_ref[...]
    blocks = homes.shape[1]
    homes_rows = (
        dot(expand, (homes >> 5).astype(F32).astype(BF16)) * 32.0 + dot(expand, (homes & 31).astype(F32).astype(BF16))
    ).astype(I32)
    gather_back = jnp.where((piece < per_pair) & (column == peer_of * per_pair + piece), 1.0, 0.0).astype(BF16)
    before = jnp.where(iota((LANES, LANES), 0) < iota((LANES, LANES), 1), 1.0, 0.0).astype(BF16)
    ones = jnp.ones((LANES, LANES), BF16)
    r_out, r_in = iota((rows + 8, rows), 0), iota((rows + 8, rows), 1)
    parity_in = lax.rem(lax.div(r_in, bag), 2)
    earlier = (r_out < rows) & (r_in < r_out) & (parity_in == lax.rem(lax.div(r_out, bag), 2))
    totals = (r_out == rows + 2 + parity_in)
    above = jnp.where(earlier | totals, 1.0, 0.0).astype(BF16)
    for_range(1, n, lambda k: exchange(n, me, outbox, inbox, send_a, recv_a, k).wait())
    own_copy.wait()
    settle_some(4)
    arrived = inbox[...].reshape(n * 8, LANES).T
    high, middle, low = split3(arrived)
    fields = dot(high, gather_back) + dot(middle, gather_back) + dot(low, gather_back)
    fields_ref[...] = fields[rows : rows + 8]
    ids = fields[0:rows].astype(I32)
    weight_count = jnp.sum(fields[rows + tasks : rows + tasks + 1], axis=1, keepdims=True).astype(I32)
    live = ids >= 0
    ids = jnp.maximum(ids, 0)
    block = lax.div(ids, block_rows)
    lane = block & (LANES - 1)
    home = jnp.zeros((rows, LANES), I32)
    for part in range(blocks // LANES):
        found = jnp.take_along_axis(homes_rows[:, part * LANES : (part + 1) * LANES], lane, axis=1, mode="promise_in_bounds")
        home = jnp.where(lax.div(block, LANES) == part, found, home)
    owner = jnp.where(live, lax.div(home, per_table), n)
    local = (table_of * per_table + lax.rem(home, per_table)) * block_rows + lax.rem(ids, block_rows)
    owner_ref[...] = owner
    local_ref[...] = local

    def rank_step(o, carry):
        rank, most = carry
        is_mine = owner == o
        flags = jnp.where(is_mine, 1.0, 0.0).astype(BF16)
        row_totals = dot(flags, ones).astype(BF16)
        bases = dot(above, row_totals)
        count = bases[rows : rows + 8].astype(I32)
        message[o] = count
        rank = jnp.where(is_mine, (dot(flags, before) + bases[0:rows]).astype(I32), rank)
        return rank, jnp.maximum(most, count)

    rank, most = jnp.zeros((rows, LANES), I32), jnp.zeros((8, LANES), I32)
    for part in range(4):
        rank, most = lax.fori_loop(part * n // 4, (part + 1) * n // 4, rank_step, (rank, most), unroll=4)
        settle_some(2)
    rank_ref[...] = rank
    most = jnp.max(most, axis=0, keepdims=True)
    pos_ref[...] = jnp.where(live, jnp.where(rank < cap, owner * cap + rank, n * cap + 1), n * cap)
    lists[...] = jnp.zeros_like(lists)
    device_row = iota((n, LANES), 0)
    rank_row = iota((LANES, LANES), 0)
    lane_value = (iota((n, LANES), 1)).astype(F32)

    def list_step(q, carry):
        for parity in range(2):
            picks, places = [], []
            for j in range(bag):
                r = (2 * q + parity) * bag + j
                owner_row = owner_ref[pl.ds(r, 1), :]
                local_row = local_ref[pl.ds(r, 1), :]
                hit = device_row == owner_row
                picks.append(
                    jnp.concatenate(
                        [
                            jnp.where(hit, ((local_row >> 7) + 1).astype(F32), 0.0),
                            jnp.where(hit, (local_row & 127).astype(F32), 0.0),
                            jnp.where(hit, (q + 1).astype(F32), 0.0),
                            jnp.where(hit, lane_value, 0.0),
                        ],
                        axis=0,
                    ).astype(BF16)
                )
                places.append(jnp.where(rank_row == rank_ref[pl.ds(r, 1), :], 1.0, 0.0).astype(BF16))
            lists[parity] += dot(jnp.concatenate(picks, axis=1), jnp.concatenate(places, axis=1), NT)
        return carry

    for part in range(2):
        lax.fori_loop(part * tables // 4, (part + 1) * tables // 4, list_step, 0)
        settle_some(1)
    sub = iota((8, LANES), 0)
    is_last = iota((1, LANES), 1) == LANES - 1

    def post(k):
        o = me ^ k
        tile = message[o]
        rows_list = []
        for parity in range(2):
            count = tile[2 + parity : 3 + parity]
            got = [lists[parity, pl.ds(part * n + o, 1), :].astype(I32) for part in range(4)]
            asked = jnp.where(got[0] > 0, (got[0] - 1) * LANES + got[1], rows_dev)
            slot = jnp.where(got[0] > 0, (got[2] - 1) * LANES + got[3], tables // 2 * LANES)
            rows_list.append(jnp.where(is_last, count, asked))
            mine_ref[o, parity : parity + 1, :] = jnp.where(is_last, count, slot)
        tile = jnp.where(sub == 0, rows_list[0], jnp.where(sub == 1, rows_list[1], tile))
        message[o] = jnp.where(sub == 4, most, jnp.where(sub == 5, weight_count, tile))

    def post_and_send(k):
        post(k)
        exchange(n, me, message, replies, send_b, recv_b, k).start()

    for_range(1, n, post_and_send)
    post(0)
    own_copy = pltpu.make_async_copy(message.at[me], replies.at[me], sems.at[0])
    own_copy.start()
    settle_some(2)
    width = table_ref.shape[0]
    table_copy.wait()
    rows_ref[rows_dev:, :] = jnp.zeros((rows_ref.shape[0] - rows_dev, LANES), F32)

    def turn(b):
        at = pl.ds(pl.multiple_of(b * LANES, LANES), LANES)
        rows_ref[at, :] = jnp.concatenate([table_ref[:, at]] * (LANES // width), axis=0).T

    for part in range(4):
        for_range(part * (rows_dev // LANES // 4), (part + 1) * (rows_dev // LANES // 4), turn)
        settle_some(2)
    for_range(1, n, lambda k: exchange(n, me, message, replies, send_b, recv_b, k).wait())
    own_copy.wait()

    def take(s, carry):
        most, total = carry
        tile = replies[s]
        asked = jnp.clip(tile[0:2], 0, rows_dev)
        theirs_ref[s] = asked
        table_rows = per_table * block_rows
        paired = lax.div(asked, 2 * table_rows) * table_rows + lax.rem(asked, table_rows)
        pairs_ref[s] = jnp.where(is_last, asked, paired)
        return jnp.maximum(most, tile), total + tile

    most, total = lax.fori_loop(0, n, take, (jnp.zeros((8, LANES), I32), jnp.zeros((8, LANES), I32)))
    stat_ref[...] = jnp.where(sub == 4, most, total)
    to_scalars = pltpu.make_async_copy(theirs_ref, asked_smem, sems.at[0])
    to_scalars.start()
    to_scalars.wait()
    lines_ref[n] = jnp.zeros((cap, LANES), F32)
    collect = collector(cap, asked_smem, rows_ref)

    def collect_and_send(i):
        k = n - i
        collect(me ^ k, rows_out, me ^ k)
        exchange(n, me, rows_out, lines_ref, send_c, recv_c, k).start()

    for part in range(8):
        for_range(part * n // 8 + (part == 0), (part + 1) * n // 8, collect_and_send)
        settle_some(3 * (part >= 4))
    collect(me, lines_ref, me)
    settle_some(len(events) - done[0])
    for_range(1, n, lambda k: exchange(n, me, rows_out, lines_ref, send_c, recv_c, k).wait())


def collector(cap, lists_ref, rows_ref):
    left = iota((1, LANES), 1) < LANES // 2

    def collect(peer, target, slot):
        def lines(g):
            for i in range(8):
                r = g * 8 + i
                even = rows_ref[pl.ds(lists_ref[peer, 0, r], 1), :]
                odd = rows_ref[pl.ds(lists_ref[peer, 1, r], 1), :]
                target[slot, pl.ds(r, 1), :] = jnp.where(left, even, odd)

        for_range(0, cap // 8, lines)

    return collect


def forward(
    n, cap, tail_rows, row_ids, lengths, counts, mask, labels, row_home, table, mat_home,
    experts_m, experts_v, towers_m, towers_v, gates_m, gates_v, small_m, small_v,
):
    samples, tables, bag = row_ids.shape
    rows_dev, width = table.shape
    tasks = labels.shape[1]
    experts, features, hidden = experts_m.shape
    per_table = row_home.shape[1] // n
    block_rows = rows_dev // (tables * per_table)
    levels = early_levels(n)
    sizes = (n, cap, tables, bag, tasks, experts, per_table, block_rows, rows_dev)
    ids = row_ids.transpose(1, 2, 0).reshape(tables * bag, samples)
    vmem = pl.BlockSpec(memory_space=pltpu.VMEM)
    smem = pl.BlockSpec(memory_space=pltpu.SMEM)
    hbm = pl.BlockSpec(memory_space=pl.ANY)
    slots = jax.ShapeDtypeStruct((tables * bag, LANES), I32)
    lists = jax.ShapeDtypeStruct((n, 2, LANES), I32)
    count = len(plan(n, experts, features, tail_rows))
    small = pltpu.VMEM((n, 8, LANES), F32)
    numbers = pltpu.VMEM((n, 8, LANES), I32)
    slot_scratch = pltpu.VMEM((tables * bag, LANES), I32)
    dma = pltpu.SemaphoreType.DMA((n,))
    hops = pltpu.SemaphoreType.DMA((count, n.bit_length()))
    return pl.pallas_call(
        functools.partial(forward_kernel, sizes),
        out_shape=(
            jax.ShapeDtypeStruct((8, LANES), F32), slots, lists, lists, lists,
            jax.ShapeDtypeStruct((8, LANES), I32), jax.ShapeDtypeStruct((n + 1, cap, LANES), F32),
            jax.ShapeDtypeStruct((count, 2, 8 * n >> levels, hidden), F32),
        ),
        in_specs=[vmem, vmem, smem, vmem, vmem, vmem, hbm, smem, hbm, hbm] + [vmem] * 6,
        out_specs=(vmem,) * 8,
        scratch_shapes=[
            small, small, numbers, numbers,
            pltpu.VMEM((2, 4 * n, LANES), F32), pltpu.VMEM((LANES, LANES), F32),
            slot_scratch, slot_scratch, slot_scratch,
            pltpu.SMEM((n, 2, LANES), I32), pltpu.VMEM((rows_dev + 8, LANES), F32), pltpu.VMEM((n, cap, LANES), F32),
            pltpu.VMEM((2, tail_rows, hidden), F32), pltpu.VMEM((count, 2, 4 * n, hidden), F32),
            pltpu.VMEM((width, rows_dev), F32),
        ]
        + [pltpu.VMEM((count, 2, 4 * n >> i, hidden), F32) for i in range(levels - 1)]
        + [dma] * 6 + [hops] * 2 + [pltpu.SemaphoreType.DMA((count, 2)), pltpu.SemaphoreType.DMA((2,))],
        compiler_params=pltpu.CompilerParams(collective_id=0, has_side_effects=True, vmem_limit_bytes=56 * 2**20),
        name="forward",
    )(
        ids, lengths.T, counts, mask.reshape(1, samples), labels.T, row_home, table.T, mat_home, experts_m, experts_v,
        towers_m.transpose(0, 2, 1), towers_v.transpose(0, 2, 1), gates_m.transpose(0, 2, 1), gates_v.transpose(0, 2, 1),
        small_m, small_v,
    )


def backward_kernel(
    sizes, lists_ref, stat_ref, items_ref, fields_ref, pooled_ref, moments_ref, experts_hbm, gates_ref, towers_ref, small_ref,
    lines_ref, experts_out, tail_out, *rest,
):
    n, cap, tail_rows = sizes
    levels, early = n.bit_length() - 1, early_levels(n)
    stages, rest = list(rest[:levels]), rest[levels:]
    late_stages, rest = [moments_ref] + list(rest[: levels - early]), rest[levels - early :]
    grads, tail, tail_w, news, rows_ref, side, rows_out, experts_ref = rest[:8]
    send_c, recv_c, sends, receives, send_m, recv_m, send_w, recv_w, local = rest[8:]
    experts, features, hidden = experts_ref.shape
    tasks, tower, _ = towers_ref.shape
    chains = plan(n, experts, features, tail_rows)
    unit = 8 * n
    me = lax.axis_index("dev")
    greet_all(n, me)
    weights_copy = pltpu.make_async_copy(experts_hbm, experts_ref, local.at[0])
    weights_copy.start()
    await_all(n)

    def late_hop(c, i):
        order = chains[c][2]
        bit = order[early + i]
        half = late_stages[i + 1].shape[2]
        at = rows_at((1 - bit_of(me, bit)) * half, half)
        return pltpu.make_async_remote_copy(
            src_ref=late_stages[i].at[c, :, at],
            dst_ref=late_stages[i + 1].at[c],
            send_sem=send_m.at[c, i],
            recv_sem=recv_m.at[c, i],
            device_id=(me ^ bit,),
            device_id_type=MESH,
        )

    chosen = owner_side(me, n, items_ref, experts, tasks, tower)

    def late_settle(i):
        for c, chain in enumerate(chains):
            late_hop(c, i).wait()
            half = late_stages[i + 1].shape[2]
            mine = rows_at(bit_of(me, chain[2][early + i]) * half, half)
            flag = chosen(chain, early + i, half)
            for w in range(2):
                late_stages[i + 1][c, w] = jnp.where(flag, late_stages[i][c, w, mine, :], late_stages[i + 1][c, w])
            if i + 1 < levels - early:
                late_hop(c, i + 1).start()

    for c in range(len(chains)):
        late_hop(c, 0).start()
    lines_ref[n] = jnp.zeros((cap, LANES), F32)
    fill_tail(tail_w, towers_ref, gates_ref, small_ref)

    def hop(c, i):
        array, first, order, _ = chains[c]
        source = tail if array == experts else grads.at[array]
        return halving(me, source.at[first : first + unit], stages, sends, receives, c, order, i)

    def settle(c, i):
        array, first, order, _ = chains[c]
        hop(c, i).wait()
        half = stages[i].shape[1]
        at = bit_of(me, order[i]) * half
        if i > 0:
            kept = stages[i - 1][c, rows_at(at, half), :]
        elif array == experts:
            kept = tail[rows_at(first + at, half), :]
        else:
            kept = grads[array, rows_at(first + at, half), :]
        stages[i][c] += kept
        if i + 1 < levels:
            hop(c, i + 1).start()

    def region(c, i):
        array, first, order, _ = chains[c]
        at = rows_at(first + start_of(me, order[: i + 1], unit), unit >> (i + 1))
        return tail_out.at[:, at] if array == experts else experts_out.at[array, :, at]

    def doubling(c, i):
        return pltpu.make_async_remote_copy(
            src_ref=news.at[c] if i == levels - 1 else region(c, i),
            dst_ref=region(c, i),
            send_sem=send_w.at[c, i],
            recv_sem=recv_w.at[c, i],
            device_id=(me ^ chains[c][2][i],),
            device_id_type=MESH,
        )

    def place(c):
        return pltpu.make_async_copy(news.at[c], region(c, levels - 1), local.at[c])

    def renew(c):
        array, first, order, _ = chains[c]
        at = rows_at(first + start_of(me, order, unit), 8)
        weight = tail_w[at, :] if array == experts else experts_ref[array, at, :]
        moment = late_stages[-1]
        grad = stages[-1][c]
        news[c, 0] = stepped(weight, *moments(moment[c, 0], moment[c, 1], grad))
        news[c, 1] = grad
        place(c).start()

    steps = len(set(chain[3] for chain in chains)) + 2 * levels

    def step(s):
        for c, chain in enumerate(chains):
            j = s - chain[3] // 2
            if 0 <= j < levels:
                settle(c, j)
            if j == levels - 1:
                renew(c)
                doubling(c, levels - 1).start()
            i = 2 * levels - 2 - j
            if i == levels - 2:
                place(c).wait()
            if 0 <= i < levels - 1:
                doubling(c, i + 1).wait()
                doubling(c, i).start()
            if j == 2 * levels - 1:
                doubling(c, 0).wait()

    def ready(array):
        for c, chain in enumerate(chains):
            if chain[0] == array:
                hop(c, 0).start()
        if array == experts:
            late_settle(0)

    weights_copy.wait()
    dense_pass(
        ready, stat_ref, fields_ref, pooled_ref, experts_ref, tail_w, towers_ref, small_ref, grads, tail, rows_ref, side
    )
    collect = collector(cap, lists_ref, rows_ref)

    def collect_and_send(i):
        k = n - i
        collect(me ^ k, rows_out, me ^ k)
        exchange(n, me, rows_out, lines_ref, send_c, recv_c, k).start()

    sent = 0
    for s in range(steps):
        goal = min(n - 1, sent + (16 if s == 0 else 4))
        if goal > sent:
            for_range(sent + 1, goal + 1, collect_and_send)
            sent = goal
        if 2 <= s < 2 + levels - early - 1:
            late_settle(s - 2 + 1)
        step(s)
    collect(me, lines_ref, me)
    for_range(1, n, lambda k: exchange(n, me, rows_out, lines_ref, send_c, recv_c, k).wait())


def backward(n, cap, tail_rows, lists, stat, items, fields, pooled, moment_slices, experts_w, gates_w, towers_w, small):
    experts, features, hidden = experts_w.shape
    samples = fields.shape[1]
    levels, early = n.bit_length() - 1, early_levels(n)
    count = len(plan(n, experts, features, tail_rows))
    vmem = pl.BlockSpec(memory_space=pltpu.VMEM)
    smem = pl.BlockSpec(memory_space=pltpu.SMEM)
    dma = pltpu.SemaphoreType.DMA((n,))
    hops = pltpu.SemaphoreType.DMA((count, levels))
    return pl.pallas_call(
        functools.partial(backward_kernel, (n, cap, tail_rows)),
        out_shape=(
            jax.ShapeDtypeStruct((n + 1, cap, LANES), F32),
            jax.ShapeDtypeStruct((experts, 2, features, hidden), F32),
            jax.ShapeDtypeStruct((2, tail_rows, hidden), F32),
        ),
        in_specs=[smem, smem, smem] + [vmem] * 3 + [pl.BlockSpec(memory_space=pl.ANY)] + [vmem] * 3,
        out_specs=(vmem, pl.BlockSpec(memory_space=pl.ANY), vmem),
        scratch_shapes=[pltpu.VMEM((count, 4 * n >> i, hidden), F32) for i in range(levels)]
        + [pltpu.VMEM((count, 2, 8 * n >> (early + i + 1), hidden), F32) for i in range(levels - early)]
        + [
            pltpu.VMEM((experts, features, hidden), F32), pltpu.VMEM((tail_rows, hidden), F32),
            pltpu.VMEM((tail_rows, hidden), F32), pltpu.VMEM((count, 2, 8, hidden), F32),
            pltpu.VMEM((features // LANES * samples + 8, LANES), F32), pltpu.VMEM((samples, samples), F32),
            pltpu.VMEM((n, cap, LANES), F32), pltpu.VMEM((experts, features, hidden), F32),
        ]
        + [dma] * 2 + [hops] * 6 + [pltpu.SemaphoreType.DMA((count,))],
        compiler_params=pltpu.CompilerParams(collective_id=1, has_side_effects=True, vmem_limit_bytes=56 * 2**20),
        name="backward",
    )(lists, stat, items, fields, pooled, moment_slices, experts_w, gates_w, towers_w, small)


def close_kernel(
    sizes,
    owned_ref, pairs_ref, lines_ref, table_ref, row_first_ref, row_second_ref,
    whole_ref, first_ref, second_ref, tail_ref, towers_m_ref, towers_v_ref, gates_m_ref, gates_v_ref, small_m_ref, small_v_ref,
    table_new_ref, row_first_new_ref, row_second_new_ref, new_ref, low_ref, first_new_ref, second_new_ref,
    towers_ref, towers_low_ref, towers_m_new_ref, towers_v_new_ref, gates_ref, gates_m_new_ref, gates_v_new_ref,
    small_ref, small_m_new_ref, small_v_new_ref, loss_ref,
    sums_even, sums_odd,
):
    n, cap, experts, first_steps, steps_each = sizes
    step = pl.program_id(0)
    width, block = table_ref.shape
    half = block // 2
    rows = sums_even.shape[0] - 8

    @pl.when(step == 0)
    def _():
        def clear(i):
            at = pl.ds(pl.multiple_of(i * half, half), half)
            sums_even[at, :] = jnp.zeros((half, LANES), F32)
            sums_odd[at, :] = jnp.zeros((half, LANES), F32)

        for_range(0, rows // half, clear)
        finish_tail(
            owned_ref, experts, tail_ref, towers_m_ref, towers_v_ref, gates_m_ref, gates_v_ref, small_m_ref, small_v_ref,
            towers_ref, towers_low_ref, towers_m_new_ref, towers_v_new_ref, gates_ref, gates_m_new_ref, gates_v_new_ref,
            small_ref, small_m_new_ref, small_v_new_ref, loss_ref,
        )

    @pl.when(step < first_steps)
    def _():
        e = lax.div(step, steps_each)
        new = whole_ref[0, 0]
        new_ref[0] = new
        low_ref[0] = new.astype(BF16)

        @pl.when(owned_ref[e] == 1)
        def _():
            first_new_ref[0], second_new_ref[0] = moments(first_ref[0], second_ref[0], whole_ref[0, 1])

        @pl.when(owned_ref[e] != 1)
        def _():
            first_new_ref[...] = jnp.zeros_like(first_new_ref)
            second_new_ref[...] = jnp.zeros_like(second_new_ref)

        def source(s):
            count = jnp.minimum(jnp.maximum(pairs_ref[s, 0, LANES - 1], pairs_ref[s, 1, LANES - 1]), cap)

            def add(g):
                for i in range(8):
                    r = g * 8 + i
                    line = lines_ref[pl.ds(s * cap + r, 1), :]
                    sums_even[pl.ds(pairs_ref[s, 0, r], 1), :] += line
                    sums_odd[pl.ds(pairs_ref[s, 1, r], 1), :] += line

            for_range(0, (count + 7) // 8, add)

        for_range(step * n // first_steps, (step + 1) * n // first_steps, source)

    @pl.when(step >= first_steps)
    def _():
        left = iota((LANES, LANES), 1) < width
        for b in range(half // LANES):
            at = pl.ds(pl.multiple_of((step - first_steps) * half + b * LANES, LANES), LANES)
            both = jnp.where(left, sums_even[at, :], sums_odd[at, :]).T
            for parity in range(2):
                here = slice(parity * half + b * LANES, parity * half + (b + 1) * LANES)
                grad = both[parity * width : (parity + 1) * width]
                first = BETA_ONE * row_first_ref[:, here] + (1.0 - BETA_ONE) * grad
                mean = jnp.sum(grad * grad, axis=0, keepdims=True) * (1.0 / width)
                second = BETA_TWO * row_second_ref[:, here] + (1.0 - BETA_TWO) * mean
                rate = (RATE_ROWS / (1.0 - BETA_ONE**STEP)) / (
                    jnp.sqrt(second * (1.0 / (1.0 - BETA_TWO**STEP))) + EPSILON
                )
                old = table_ref[:, here]
                table_new_ref[:, here] = old - (first * rate + (RATE_ROWS * DECAY) * old)
                row_first_new_ref[:, here] = first
                row_second_new_ref[:, here] = second


def finish_tail(
    owned_ref, experts, tail_ref, towers_m_ref, towers_v_ref, gates_m_ref, gates_v_ref, small_m_ref, small_v_ref,
    towers_ref, towers_low_ref, towers_m_new_ref, towers_v_new_ref, gates_ref, gates_m_new_ref, gates_v_new_ref,
    small_ref, small_m_new_ref, small_v_new_ref, loss_ref,
):
    tasks, tower, hidden = towers_ref.shape
    count = gates_ref.shape[1]

    def mine(item, pair):
        own = jnp.full((1, 1), owned_ref[item], I32) == 1
        return [jnp.where(own, x, 0.0) for x in pair]

    for k in range(tasks):
        at = slice(k * tower, (k + 1) * tower)
        towers_ref[k] = tail_ref[0, at]
        towers_low_ref[k] = tail_ref[0, at].astype(BF16)
        towers_m_new_ref[k], towers_v_new_ref[k] = mine(
            experts + tasks + k, moments(towers_m_ref[k], towers_v_ref[k], tail_ref[1, at])
        )
        for part in range(2):
            row = tasks * tower + part * GAP + k * count
            at = slice(row, row + count)
            to = slice(part * hidden, (part + 1) * hidden)
            gates_ref[k, :, to] = tail_ref[0, at]
            gates_m_new_ref[k, :, to], gates_v_new_ref[k, :, to] = mine(
                experts + k, moments(gates_m_ref[k, :, to], gates_v_ref[k, :, to], tail_ref[1, at])
            )
    base = tasks * tower + 2 * GAP
    size = small_ref.shape[1]
    for i in range(-(-size // hidden)):
        last = min(size, (i + 1) * hidden)
        to = slice(i * hidden, last)
        line = slice(0, last - i * hidden)
        small_ref[0:1, to] = tail_ref[0, base + i : base + i + 1, line]
        small_m_new_ref[0:1, to], small_v_new_ref[0:1, to] = mine(
            experts + 2 * tasks,
            moments(small_m_ref[0:1, to], small_v_ref[0:1, to], tail_ref[1, base + i : base + i + 1, line]),
        )
    loss_ref[...] = tail_ref[1, base + 8 : base + 9, 0:LANES]


def close(
    n, cap, table_rows, pairs, lines, table, table_m, table_v,
    owned, whole, tail, experts_m, experts_v, towers_m, towers_v, gates_m, gates_v, small_m, small_v,
):
    rows_dev, width = table.shape
    experts, features, hidden = experts_m.shape
    block = 2 * table_rows
    rows = min(512, features)
    steps_each = features // rows
    first_steps = experts * steps_each
    update_steps = rows_dev // block

    def late(i, *_):
        return (0, jnp.maximum(i - first_steps, 0))

    def place(i):
        i = jnp.minimum(i, first_steps - 1)
        return lax.div(i, steps_each), lax.rem(i, steps_each)

    def here(i, owned):
        e, b = place(i)
        return e, b, 0

    def only_owner(i, owned):
        e, b = place(i)
        return e, jnp.where(owned[e] == 1, b, 0), 0

    def both(i, owned):
        e, b = place(i)
        return e, 0, b, 0

    wide, thin = pl.BlockSpec((width, block), late), pl.BlockSpec((1, block), late)
    out_block, owners = pl.BlockSpec((1, rows, hidden), here), pl.BlockSpec((1, rows, hidden), only_owner)

    def full(x):
        return pl.BlockSpec(x.shape, lambda i, owned: (0,) * len(x.shape))

    sums = pltpu.VMEM((rows_dev // 2 + 8, LANES), F32)
    lines = lines.reshape((n + 1) * cap, LANES)
    towers = jax.ShapeDtypeStruct(towers_m.shape, F32)
    gates = jax.ShapeDtypeStruct(gates_m.shape, F32)
    small = jax.ShapeDtypeStruct(small_m.shape, F32)
    tail_shapes = (
        towers, jax.ShapeDtypeStruct(towers_m.shape, BF16), towers, towers, gates, gates, gates, small, small, small,
        jax.ShapeDtypeStruct((1, LANES), F32),
    )
    dense_shape = jax.ShapeDtypeStruct(experts_m.shape, F32)
    rows_shape = jax.ShapeDtypeStruct((width, rows_dev), F32)
    out_shape = (
        rows_shape, rows_shape, jax.ShapeDtypeStruct((1, rows_dev), F32),
        dense_shape, jax.ShapeDtypeStruct(experts_m.shape, BF16), dense_shape, dense_shape,
    ) + tail_shapes
    table_new, first_new, second_new, *others = pl.pallas_call(
        functools.partial(close_kernel, (n, cap, experts, first_steps, steps_each)),
        grid_spec=pltpu.PrefetchScalarGridSpec(
            num_scalar_prefetch=1,
            grid=(first_steps + update_steps,),
            in_specs=[
                pl.BlockSpec(memory_space=pltpu.SMEM), full(lines), wide, wide, thin,
                pl.BlockSpec((1, 2, rows, hidden), both), owners, owners,
                full(tail), full(towers_m), full(towers_v), full(gates_m), full(gates_v), full(small_m), full(small_v),
            ],
            out_specs=[wide, wide, thin] + [out_block] * 4 + [full(x) for x in tail_shapes],
            scratch_shapes=[sums, sums],
        ),
        out_shape=out_shape,
        compiler_params=pltpu.CompilerParams(vmem_limit_bytes=58 * 2**20),
        name="close",
    )(
        owned, pairs, lines, table.T, table_m.T, table_v.reshape(1, rows_dev),
        whole, experts_m, experts_v, tail, towers_m, towers_v, gates_m, gates_v, small_m, small_v,
    )
    return (table_new.T, first_new.T, second_new.reshape(rows_dev)), others


def pool_kernel(nothing, tables, bag, pos_ref, lines_ref, pooled_ref):
    samples = pos_ref.shape[1]
    pooled_ref[...] = jnp.zeros_like(pooled_ref)
    left = iota((1, LANES), 1) < LANES // 2

    def sample(s):
        @pl.when(pos_ref[0, s] != nothing)
        def _():
            for q in range(tables // 2):
                sums = []
                for parity in range(2):
                    base = (2 * q + parity) * bag
                    total = lines_ref[pl.ds(pos_ref[base, s], 1), :]
                    for j in range(1, bag):
                        total = total + lines_ref[pl.ds(pos_ref[base + j, s], 1), :]
                    sums.append(total)
                pooled_ref[pl.ds(q * samples + s, 1), :] = jnp.where(left, sums[0], sums[1])

    for_range(0, samples, sample)


def pool(n, cap, tables, bag, pos, lines):
    samples = pos.shape[1]
    return pl.pallas_call(
        functools.partial(pool_kernel, n * cap, tables, bag),
        out_shape=jax.ShapeDtypeStruct((tables // 2 * samples, LANES), F32),
        in_specs=[pl.BlockSpec(memory_space=pltpu.SMEM), pl.BlockSpec(memory_space=pltpu.VMEM)],
        out_specs=pl.BlockSpec(memory_space=pltpu.VMEM),
        compiler_params=pltpu.CompilerParams(vmem_limit_bytes=24 * 2**20),
        name="pool",
    )(pos, lines.reshape((n + 1) * cap, LANES))


def split2(x):
    high = x.astype(BF16)
    return high, (x - high.astype(F32)).astype(BF16)


def dot3(a, b, dims=NN):
    count = a[0].shape[0]
    if count > LANES:
        return dot(a[0], b[0], dims) + dot(a[0], b[1], dims) + dot(a[1], b[0], dims)
    both = dot(jnp.concatenate(a, axis=0), b[0], dims)
    return both[:count] + both[count:] + dot(a[0], b[1], dims)


def sigmoid(x):
    return 1.0 / (1.0 + jnp.exp(-x))


def dense_pass(
    ready, stat_ref, fields_ref, pooled_ref, experts_ref, tail_w, towers_ref, small_ref, grads, tail, rows_ref, side
):
    samples = fields_ref.shape[1]
    experts, features, hidden = experts_ref.shape
    tasks, tower, _ = towers_ref.shape
    tail[...] = jnp.zeros_like(tail)

    def put_tail(row, value):
        tail[row : row + value.shape[0], :] = value

    start = experts * hidden
    tower_at = start
    weight_at = start + tasks * tower
    bias_at = weight_at + tasks * tower
    side[0:8, :] = fields_ref[...]
    side[8:, :] = jnp.zeros((samples - 8, samples), F32)
    by_sample = side[...].T
    weight = by_sample[:, tasks : tasks + 1]
    scale = weight / stat_ref[0].astype(F32)
    x = jnp.concatenate([pooled_ref[q * samples : (q + 1) * samples] for q in range(features // LANES)], axis=1)
    x2 = split2(x)
    at = tasks * tower
    gate_w = jnp.concatenate([tail_w[at + k * GAP : at + k * GAP + tasks * experts, :] for k in range(2)], axis=1)
    gate_w2 = split2(gate_w)
    gate_logits = dot3(x2, gate_w2, NT)
    pres, sigs, hids = [], [], []
    for e in range(experts):
        pre = dot3(x2, split2(experts_ref[e])) + small_ref[0:1, e * hidden : (e + 1) * hidden]
        sig = sigmoid(pre)
        pres.append(pre)
        sigs.append(sig)
        hids.append(pre * sig)
    dhids = [jnp.zeros((samples, hidden), F32) for _ in range(experts)]
    dgate_logits = []
    loss = jnp.zeros((samples, 1), F32)
    tower_bias_grads, out_weight_grads, task_bias_grads = [], [], []
    for k in range(tasks):
        logits = [gate_logits[:, k * experts + e : k * experts + e + 1] for e in range(experts)]
        top = functools.reduce(jnp.maximum, logits)
        powers = [jnp.exp(v - top) for v in logits]
        whole = functools.reduce(jnp.add, powers)
        gates = [v / whole for v in powers]
        mix = functools.reduce(jnp.add, [gates[e] * hids[e] for e in range(experts)])
        mix2 = split2(mix)
        tower2 = split2(towers_ref[k])
        at = tower_at + k * tower
        pre = dot3(mix2, tower2, NT) + small_ref[0:1, at : at + tower]
        sig = sigmoid(pre)
        zed = pre * sig
        at = weight_at + k * tower
        out_weight = small_ref[0:1, at : at + tower]
        logit = jnp.sum(zed * out_weight, axis=1, keepdims=True) + small_ref[0:1, bias_at + k : bias_at + k + 1]
        label = by_sample[:, k : k + 1]
        softplus = jnp.maximum(logit, 0.0) + jnp.log1p(jnp.exp(-jnp.abs(logit)))
        loss = loss + weight * (softplus - label * logit)
        dlogit = scale * (sigmoid(logit) - label)
        task_bias_grads.append(jnp.sum(dlogit, axis=0, keepdims=True))
        out_weight_grads.append(jnp.sum(dlogit * zed, axis=0, keepdims=True))
        dpre = dlogit * out_weight * (sig * (1.0 + pre * (1.0 - sig)))
        tower_bias_grads.append(jnp.sum(dpre, axis=0, keepdims=True))
        dpre2 = split2(dpre)
        put_tail(k * tower, dot3(split2(dpre.T), mix2))
        dmix = dot3(dpre2, tower2)
        dgates = [jnp.sum(dmix * hids[e], axis=1, keepdims=True) for e in range(experts)]
        mean = functools.reduce(jnp.add, [gates[e] * dgates[e] for e in range(experts)])
        for e in range(experts):
            dgate_logits.append(gates[e] * (dgates[e] - mean))
            dhids[e] = dhids[e] + gates[e] * dmix
    lane = iota((samples, LANES), 1)
    dgl = jnp.zeros((samples, LANES), F32)
    for i, v in enumerate(dgate_logits):
        dgl = jnp.where(lane == i, v, dgl)
    count = tasks * experts
    dgl_t2 = split2(dgl.T[0:16])
    dgates_w = dot3(dgl_t2, x2)
    tail_at = tasks * tower
    put_tail(tail_at, dgates_w[:, :hidden])
    put_tail(tail_at + GAP, dgates_w[:, hidden:])
    expert_bias_grads, dpres = [], []
    for e in range(experts):
        dpre = dhids[e] * (sigs[e] * (1.0 + pres[e] * (1.0 - sigs[e])))
        expert_bias_grads.append(jnp.sum(dpre, axis=0, keepdims=True))
        dpres.append(split2(dpre))
    small_at = tail_at + 2 * GAP
    pad = jnp.zeros((1, 2 * hidden - 2 * tasks * tower - tasks), F32)
    line = jnp.concatenate(tower_bias_grads + out_weight_grads + task_bias_grads + [pad], axis=1)
    loss_row = jnp.where(iota((1, hidden), 1) == 0, jnp.sum(loss, axis=0, keepdims=True), 0.0)
    for e in range(experts):
        put_tail(small_at + e, expert_bias_grads[e])
    for i in range(line.shape[1] // hidden):
        put_tail(small_at + experts + i, line[:, i * hidden : (i + 1) * hidden])
    put_tail(small_at + 8, loss_row)
    ready(experts)
    x_t2 = split2(x.T)
    for e in range(experts):
        grads[e] = dot3(x_t2, dpres[e])
        ready(e)
    dx = dot3(split2(dgl[:, :count]), gate_w2)
    for e in range(experts):
        dx = dx + dot3(dpres[e], split2(experts_ref[e]), NT)
    for q in range(features // LANES):
        rows_ref[q * samples : (q + 1) * samples, :] = dx[:, q * LANES : (q + 1) * LANES]
    rows_ref[features // LANES * samples :, :] = jnp.zeros((8, LANES), F32)


def moments(first, second, grad):
    return (
        BETA_ONE * first + (1.0 - BETA_ONE) * grad,
        BETA_TWO * second + (1.0 - BETA_TWO) * grad * grad,
    )


def stepped(weight, first_new, second_new):
    first_hat = first_new / (1.0 - BETA_ONE**STEP)
    second_hat = second_new / (1.0 - BETA_TWO**STEP)
    return weight - RATE_DENSE * (first_hat / (jnp.sqrt(second_hat) + EPSILON) + DECAY * weight)


def all_sum(tree, axis):
    n = lax.axis_size(axis)
    bit = 1
    while bit < n:
        pairs = [(i, i ^ bit) for i in range(n)]
        tree = jax.tree.map(lambda x: x + lax.ppermute(x, axis, pairs), tree)
        bit *= 2
    return tree


def from_root(block, axis, source):
    block = jnp.where(lax.axis_index(axis) == source, block, jnp.zeros_like(block))
    return all_sum(block, axis)


def dense_forward(params, pooled, labels, weights):
    experts_w, gates_w, towers_w, small = params
    n_experts, _, hidden = experts_w.shape
    tasks, _, tower = towers_w.shape
    start = n_experts * hidden
    expert_bias = small[:start].reshape(n_experts, hidden)
    tower_bias = small[start : start + tasks * tower].reshape(tasks, tower)
    start = start + tasks * tower
    out_weight = small[start : start + tasks * tower].reshape(tasks, tower)
    task_bias = small[start + tasks * tower :]
    hidden_act = jax.nn.silu(
        jnp.einsum("si,eih->seh", pooled, experts_w, precision=lax.Precision.HIGHEST) + expert_bias
    )
    gate = jax.nn.softmax(jnp.einsum("si,kie->ske", pooled, gates_w, precision=lax.Precision.HIGHEST), axis=-1)
    mixed = jnp.einsum("ske,seh->skh", gate, hidden_act, precision=lax.Precision.HIGHEST)
    zed = jax.nn.silu(jnp.einsum("skh,khc->skc", mixed, towers_w, precision=lax.Precision.HIGHEST) + tower_bias)
    logit = jnp.sum(zed * out_weight, axis=-1) + task_bias
    losses = jax.nn.softplus(logit) - labels * logit
    return jnp.sum(weights[:, None] * losses)


def adam_step(weight, first, second, grad, rate):
    first_new = BETA_ONE * first + (1.0 - BETA_ONE) * grad
    second_new = BETA_TWO * second + (1.0 - BETA_TWO) * grad * grad
    first_hat = first_new / (1.0 - BETA_ONE**STEP)
    second_hat = second_new / (1.0 - BETA_TWO**STEP)
    weight_new = weight - rate * (first_hat / (jnp.sqrt(second_hat) + EPSILON) + DECAY * weight)
    return (weight_new, first_new, second_new)


def plain_step(
    row_ids,
    lengths,
    counts,
    mask,
    labels,
    row_home,
    mat_home,
    table,
    table_m,
    table_v,
    experts_w,
    gates_w,
    towers_w,
    small_params,
    experts_m,
    experts_v,
    gates_m,
    gates_v,
    towers_m,
    towers_v,
    small_m,
    small_v,
):
    devices = lax.axis_size("dev")
    myself = lax.axis_index("dev")
    samples, tables, bag_slots = row_ids.shape
    rows_dev, width = table.shape
    per_table = row_home.shape[1] // devices
    block_rows = rows_dev // (tables * per_table)
    slots = samples * tables * bag_slots
    average = slots // devices
    capacity = average + average // 2
    present = jnp.arange(samples) < counts[0]
    weights = jnp.where(present & (mask == 1), 1.0, 0.0).astype(jnp.float32)
    live = present[:, None, None] & (jnp.arange(bag_slots)[None, None, :] < lengths[:, :, None])
    table_of = jnp.broadcast_to(jnp.arange(tables)[None, :, None], row_ids.shape)
    homes = row_home[table_of, row_ids // block_rows]
    owners = (homes // per_table).reshape(-1)
    local_rows = (
        (table_of * per_table + homes % per_table) * block_rows + row_ids % block_rows
    ).reshape(-1)
    live_flat = live.reshape(-1)
    live_float = live_flat.astype(jnp.float32)
    targets = jnp.where(live_flat, owners, devices)
    order = jnp.argsort(targets, stable=True)
    sorted_targets = targets[order]
    starts = jnp.searchsorted(sorted_targets, jnp.arange(devices + 1), side="left")
    sorted_rank = jnp.arange(slots, dtype=jnp.int32) - starts[sorted_targets]
    slot_rank = jnp.zeros(slots, jnp.int32).at[order].set(sorted_rank)
    slot_rank = jnp.where(live_flat, slot_rank, 0)
    requests = (
        jnp.zeros((devices, capacity), jnp.int32)
        .at[targets, slot_rank]
        .set(local_rows, mode="drop")
    )
    asked_rows = lax.all_to_all(requests, "dev", split_axis=0, concat_axis=0, tiled=True)
    found = table[asked_rows]
    arrived = lax.all_to_all(found, "dev", split_axis=0, concat_axis=0, tiled=True)
    safe_owner = jnp.minimum(owners, devices - 1)
    slot_rows = arrived[safe_owner, slot_rank] * live_float[:, None]
    pooled = jnp.sum(slot_rows.reshape(samples, tables, bag_slots, width), axis=2).reshape(
        samples, tables * width
    )
    params = (experts_w, gates_w, towers_w, small_params)
    local_loss, pull = jax.vjp(
        lambda dense, features: dense_forward(dense, features, labels, weights), params, pooled
    )
    loss_sum, weight_sum = all_sum((local_loss, jnp.sum(weights)), "dev")
    local_grads, pooled_grad = pull(1.0 / weight_sum)
    slot_grads = (
        jnp.broadcast_to(
            pooled_grad.reshape(samples, tables, 1, width), (samples, tables, bag_slots, width)
        ).reshape(slots, width)
        * live_float[:, None]
    )
    outgoing = (
        jnp.zeros((devices, capacity, width), jnp.float32)
        .at[targets, slot_rank]
        .set(slot_grads, mode="drop")
    )
    incoming = lax.all_to_all(outgoing, "dev", split_axis=0, concat_axis=0, tiled=True)
    grad_table = (
        jnp.zeros((rows_dev, width), jnp.float32)
        .at[asked_rows.reshape(-1)]
        .add(incoming.reshape(-1, width))
    )
    table_m_new = BETA_ONE * table_m + (1.0 - BETA_ONE) * grad_table
    table_v_new = BETA_TWO * table_v + (1.0 - BETA_TWO) * jnp.mean(grad_table * grad_table, axis=1)
    first_hat = table_m_new / (1.0 - BETA_ONE**STEP)
    second_hat = table_v_new / (1.0 - BETA_TWO**STEP)
    table_new = table - RATE_ROWS * (
        first_hat / (jnp.sqrt(second_hat)[:, None] + EPSILON) + DECAY * table
    )
    grad_experts, grad_gates, grad_towers, grad_small = local_grads
    grad_experts, grad_gates, grad_towers, grad_small = all_sum(
        (grad_experts, grad_gates, grad_towers, grad_small), "dev"
    )
    kinds = (
        (experts_w, experts_m[0], experts_v[0], grad_experts),
        (gates_w, gates_m[0], gates_v[0], grad_gates),
        (towers_w, towers_m[0], towers_v[0], grad_towers),
        (small_params[None], small_m, small_v, grad_small[None]),
    )
    finals = []
    first_outs = []
    second_outs = []
    base = 0
    for stack, firsts, seconds, grad in kinds:
        kind_weights = []
        kind_firsts = []
        kind_seconds = []
        for position in range(stack.shape[0]):
            owner_id = mat_home[base + position]
            is_owner = owner_id == myself
            weight_new, first_new, second_new = adam_step(
                stack[position], firsts[position], seconds[position], grad[position], RATE_DENSE
            )
            kind_firsts.append(jnp.where(is_owner, first_new, 0.0))
            kind_seconds.append(jnp.where(is_owner, second_new, 0.0))
            kept = jnp.where(is_owner, weight_new, stack[position])
            kind_weights.append(from_root(kept, "dev", owner_id))
        base = base + stack.shape[0]
        finals.append(jnp.stack(kind_weights))
        first_outs.append(jnp.stack(kind_firsts)[None])
        second_outs.append(jnp.stack(kind_seconds)[None])
    experts_new, gates_new, towers_new, small_stack = finals
    small_new = small_stack[0]
    return (
        loss_sum,
        weight_sum,
        table_new,
        table_m_new,
        table_v_new,
        experts_new,
        gates_new,
        towers_new,
        small_new,
        first_outs[0],
        second_outs[0],
        first_outs[1],
        second_outs[1],
        first_outs[2],
        second_outs[2],
        first_outs[3][0],
        second_outs[3][0],
        experts_new.astype(jnp.bfloat16)[None],
        gates_new.astype(jnp.bfloat16)[None],
        towers_new.astype(jnp.bfloat16)[None],
        small_new.astype(jnp.bfloat16)[None],
    )


def per_device(*args):
    (
        row_ids, lengths, counts, mask, labels, row_home, mat_home, table, table_m, table_v,
        experts_w, gates_w, towers_w, small_params,
        experts_m, experts_v, gates_m, gates_v, towers_m, towers_v, small_m, small_v,
    ) = args
    n = lax.axis_size("dev")
    me = lax.axis_index("dev")
    samples, tables, bag = row_ids.shape
    rows_dev, width = table.shape
    cap = max(8, (samples * tables * bag // n * 11 // 32 + 7) // 8 * 8)
    experts, features, hidden = experts_w.shape
    tasks, _, tower = towers_w.shape
    tail_rows = -(-(tasks * tower + 2 * GAP + 16) // (8 * n)) * 8 * n
    fields, pos, mine, theirs, pairs, stat, lines, moment_slices = forward(
        n, cap, tail_rows, row_ids, lengths, counts, mask, labels, row_home, table, mat_home,
        experts_m[0], experts_v[0], towers_m[0], towers_v[0], gates_m[0], gates_v[0], small_m, small_v,
    )
    most, weight_count = stat[4, 0], stat[5, 0]

    def usual(fields, pos, mine, pairs, lines, moment_slices, weight_count, *args):
        (
            _, _, _, _, _, _, mat_home, table, table_m, table_v, experts_w, gates_w, towers_w, small_params,
            experts_m, experts_v, gates_m, gates_v, towers_m, towers_v, small_m, small_v,
        ) = args

        def turned(x):
            return x.transpose(0, 2, 1)

        gates_t, towers_t, small = turned(gates_w), turned(towers_w), small_params.reshape(1, -1)
        pooled = pool(n, cap, tables, bag, pos, lines)
        back, whole, tail = backward(
            n, cap, tail_rows, mine, weight_count[None], mat_home, fields, pooled, moment_slices,
            experts_w, gates_t, towers_t, small,
        )
        rows_new, (
            experts_new, experts_low, experts_m_new, experts_v_new,
            towers_new, towers_low, towers_m_new, towers_v_new, gates_new, gates_m_new, gates_v_new,
            small_new, small_m_new, small_v_new, loss,
        ) = close(
            n, cap, rows_dev // tables, pairs, back, table, table_m, table_v,
            (mat_home == me).astype(I32), whole, tail, experts_m[0], experts_v[0], turned(towers_m[0]), turned(towers_v[0]),
            turned(gates_m[0]), turned(gates_v[0]), small_m, small_v,
        )
        gates_new = turned(gates_new)
        small_new = small_new.reshape(-1)
        return (
            loss[0, 0], weight_count.astype(F32), *rows_new, experts_new, gates_new, turned(towers_new), small_new,
            experts_m_new[None], experts_v_new[None], turned(gates_m_new)[None], turned(gates_v_new)[None],
            turned(towers_m_new)[None], turned(towers_v_new)[None], small_m_new, small_v_new,
            experts_low[None], gates_new.astype(BF16)[None], turned(towers_low)[None], small_new.astype(BF16)[None],
        )

    def crowded(fields, pos, mine, pairs, lines, moment_slices, weight_count, *args):
        return plain_step(*args)

    return lax.cond(
        most <= cap, usual, crowded, fields, pos, mine, pairs, lines, moment_slices, weight_count, *args
    )


def solution(mesh):
    def split(dims):
        return P("dev", *(None,) * (dims - 1))

    by_device = split(4)
    return jax.shard_map(
        per_device,
        mesh=mesh,
        in_specs=(
            split(3), split(2), split(1), split(1), split(2), P(), P(), split(2), split(2), split(1),
            P(), P(), P(), P(),
        ) + (by_device,) * 6 + (split(2),) * 2,
        out_specs=(P(), P(), split(2), split(2), split(1), P(), P(), P(), P())
        + (by_device,) * 6 + (split(2),) * 2 + (by_device,) * 3 + (split(2),),
        check_vma=False,
    )
```
